32 devices in a mesh: seq: 8 (over z, y), fsdp: 4 (over x, core).
Axes of the slice: x: 2, y: 2, z: 4, core: 2. Of those that a mesh axis runs over, the one named last changes fastest.
Arguments:
- tokens: bfloat16 [4, 3072, 1024], P('fsdp', 'seq'), may hold values from -6 to 6
- cotangent: bfloat16 [4, 3072, 1024], P('fsdp', 'seq'), may hold values from -6 to 6
- lengths: int32 [4, 4], replicated, may hold values from 1 to 1152, as said below
- deal: int32 [4], replicated, may hold values from 0 to 3, each once
- ln1_gain: bfloat16 [1024], P('fsdp'), may hold values from 0.5 to 1.5
- ln1_shift: bfloat16 [1024], P('fsdp'), may hold values from -1.75 to 1.75
- w_qkv: bfloat16 [1024, 3072], P('fsdp'), may hold values from -0.1875 to 0.1875
- bias_qv: bfloat16 [2048], P('fsdp'), may hold values from -1.75 to 1.75
- w_out: bfloat16 [1024, 1024], P('fsdp'), may hold values from -3 to 3
- bias_out: bfloat16 [1024], P('fsdp'), may hold values from -1.75 to 1.75
- ln2_gain: bfloat16 [1024], P('fsdp'), may hold values from 0.5 to 1.5
- ln2_shift: bfloat16 [1024], P('fsdp'), may hold values from -1.75 to 1.75
- w_fc: bfloat16 [1024, 4096], P('fsdp'), may hold values from -0.1875 to 0.1875
- bias_fc: bfloat16 [4096], P('fsdp'), may hold values from -1.75 to 1.75
- w_proj: bfloat16 [4096, 1024], P('fsdp'), may hold values from -0.09375 to 0.09375
- bias_proj: bfloat16 [1024], P('fsdp'), may hold values from -1.75 to 1.75
Outputs:
- output: bfloat16 [4, 3072, 1024], P('fsdp', 'seq')
- input_grad: float32 [4, 3072, 1024], P('fsdp', 'seq')
- grad_ln1_gain: float32 [1024], P('fsdp')
- grad_ln1_shift: float32 [1024], P('fsdp')
- grad_w_qkv: float32 [1024, 3072], P('fsdp')
- grad_bias_qv: float32 [2048], P('fsdp')
- grad_w_out: float32 [1024, 1024], P('fsdp')
- grad_bias_out: float32 [1024], P('fsdp')
- grad_ln2_gain: float32 [1024], P('fsdp')
- grad_ln2_shift: float32 [1024], P('fsdp')
- grad_w_fc: float32 [1024, 4096], P('fsdp')
- grad_bias_fc: float32 [4096], P('fsdp')
- grad_w_proj: float32 [4096, 1024], P('fsdp')
- grad_bias_proj: float32 [1024], P('fsdp')
- stats: float32 [3], replicated
The draws below stay inside these ranges and needn't reach their ends.
Inputs may be any that keep to these rules, and one draw needn't show every extreme that they name: Each row lists 4 - 1 sequence lengths and then the padding count, which is 1 or more; every sequence has 384 tokens or more, one in each row exactly 1152; a row sums to 3072. `deal`: every group is named by exactly one home pack.
All inputs are finite; a program needn't handle non-finite values.
Results may differ from the reference program's by a relative error of at most 0.017.
Values may be sent and summed in bfloat16 or wider, within the bound.
No kernel may reach another device: no remote copies, remote signals or barrier semaphores. Data moves between devices by JAX's collectives and lax.ppermute only.
A program may use at most 192 MiB of HBM per device.

```python
import jax
import jax.numpy as jnp
from jax import lax

D = 1024
H = 16
HEAD = 64
FF = 4096
SEGS = 4
GROUPS = 4
GROUP_TOK = 3072
MOST = 1152
MINLEN = 384


def draw_lengths(key, part):
    key = jax.random.fold_in(key, 17)
    one_key, two_key, place_key = jax.random.split(key, 3)
    leftover = GROUP_TOK - MOST - 2 * MINLEN - 1
    reach = MOST - MINLEN
    extra_one = jax.random.randint(one_key, (GROUPS,), 0, min(leftover, reach) + 1)
    extra_two = jax.random.randint(two_key, (GROUPS,), 0, 1 << 20) % (jnp.minimum(leftover - extra_one, reach) + 1)
    longest = jax.random.randint(place_key, (GROUPS,), 0, 3)
    short_one = MINLEN + extra_one
    short_two = MINLEN + extra_two
    slot_zero = jnp.where(longest == 0, MOST, short_one)
    slot_one = jnp.where(longest == 1, MOST, jnp.where(longest == 0, short_one, short_two))
    slot_two = jnp.where(longest == 2, MOST, short_two)
    padding = GROUP_TOK - slot_zero - slot_one - slot_two
    return jnp.stack([slot_zero, slot_one, slot_two, padding], axis=1).astype(jnp.int32)


def block_levels(stream_key, extent, cuts, smallest, top_value):
    def one(dim, parts):
        draws = jax.random.uniform(jax.random.fold_in(jax.random.fold_in(stream_key, 6), dim), (parts,), jnp.float32, smallest / len(cuts), top_value / len(cuts))
        return jnp.repeat(jnp.exp(draws), extent[dim] // parts).reshape((-1,) + (1,) * (len(extent) - dim - 1))

    loudness = one(*cuts[0])
    for cut in cuts[1:]:
        loudness = loudness * one(*cut)
    return loudness


def noise(own_key, dims, width, most, pieces=(), kind=jnp.bfloat16):
    entries = width * jax.random.normal(own_key, dims, jnp.float32)
    if pieces:
        entries = entries * block_levels(own_key, dims, pieces, -0.22, 0.18)
    return jnp.clip(entries, -most, most).astype(kind)


def setup_inputs(seed: int = 0) -> dict:
    splits = jax.random.split(jax.random.key(seed), 17)
    return {
        "tokens": noise(splits[0], (GROUPS, GROUP_TOK, D), 1.0, 6.0, ((0, 4), (1, 8))),
        "cotangent": noise(splits[1], (GROUPS, GROUP_TOK, D), 1.0, 6.0, ((0, 4), (1, 8))),
        "lengths": draw_lengths(jax.random.fold_in(splits[16], 71), 0),
        "deal": jax.random.permutation(splits[3], GROUPS).astype(jnp.int32),
        "ln1_gain": jnp.clip(1.0 + 0.1 * jax.random.normal(splits[4], (D,), jnp.float32), 0.5, 1.5).astype(jnp.bfloat16),
        "ln1_shift": noise(splits[5], (D,), 0.3, 1.75, ((0, 4),)),
        "w_qkv": noise(splits[6], (D, 3 * D), D ** -0.5, 0.1875, ((0, 4),)),
        "bias_qv": noise(splits[7], (2 * D,), 0.3, 1.75, ((0, 4),)),
        "w_out": noise(splits[8], (D, D), (max(D // 256, 1)) ** -0.5, 3.0, ((0, 4),)),
        "bias_out": noise(splits[9], (D,), 0.3, 1.75, ((0, 4),)),
        "ln2_gain": jnp.clip(1.0 + 0.1 * jax.random.normal(splits[10], (D,), jnp.float32), 0.5, 1.5).astype(jnp.bfloat16),
        "ln2_shift": noise(splits[11], (D,), 0.3, 1.75, ((0, 4),)),
        "w_fc": noise(splits[12], (D, FF), D ** -0.5, 0.1875, ((0, 4),)),
        "bias_fc": noise(splits[13], (FF,), 0.3, 1.75, ((0, 4),)),
        "w_proj": noise(splits[14], (FF, D), FF ** -0.5, 0.09375, ((0, 4),)),
        "bias_proj": noise(splits[15], (D,), 0.3, 1.75, ((0, 4),)),
    }


@jax.custom_vjp
def low(v):
    return lax.optimization_barrier(v.astype(jnp.bfloat16)).astype(jnp.float32)

@jax.custom_vjp
def low_back(v):
    return v

def low_keep(v):
    return (low(v), None)

def low_pass(kept, grad):
    return (grad,)

def back_keep(v):
    return (v, None)

def back_low(kept, grad):
    return (low(grad),)
low.defvjp(low_keep, low_pass)
low_back.defvjp(back_keep, back_low)
highest = lax.Precision.HIGHEST

def layer_norm(value, gain, shift):
    mean = lax.optimization_barrier(jnp.mean(value, axis=-1, keepdims=True))
    centred = value - mean
    spread = lax.optimization_barrier(jnp.mean(centred * centred, axis=-1, keepdims=True))
    return centred * lax.rsqrt(spread + 1e-05) * gain + shift

def segment_ids(row, count):
    ends = jnp.cumsum(row).astype(jnp.int32)
    places = jnp.arange(count, dtype=jnp.int32)
    return lax.optimization_barrier(jnp.sum((places[:, None] >= ends[None, :]).astype(jnp.int32), axis=1))

def forward(xf, params, segments):
    gain_one, shift_one, wqkv, bqv, wout, bout, gain_two, shift_two, wfc, bfc, wproj, bproj = params
    count = xf.shape[0]
    normed_one = low(layer_norm(xf, gain_one, shift_one))
    mixed = jnp.dot(normed_one, wqkv, precision=highest).reshape(count, H, 3, HEAD)
    biases = bqv.reshape(H, 2, HEAD)
    queries = low_back(low(mixed[:, :, 0] + biases[:, 0]))
    keys = low_back(low(mixed[:, :, 1]))
    values = low_back(low(mixed[:, :, 2] + biases[:, 1]))
    block = min(512, count)
    scale = HEAD ** (-0.5)
    places = jnp.arange(count, dtype=jnp.int32)

    def attend(first):
        query_rows = lax.dynamic_slice_in_dim(queries, first, block, 0)
        seg_rows = lax.dynamic_slice_in_dim(segments, first, block, 0)
        query_pos = first + jnp.arange(block, dtype=jnp.int32)
        allowed = (seg_rows[:, None] == segments[None, :]) & (places[None, :] <= query_pos[:, None])
        raw = low_back(jnp.einsum('qhe,khe->hqk', query_rows, keys, precision=highest) * scale)
        scores = jnp.where(allowed[None], raw, -1e+30)
        top = lax.optimization_barrier(jnp.max(scores, axis=-1, keepdims=True))
        expd = jnp.exp(scores - top)
        probs = low(expd / lax.optimization_barrier(jnp.sum(expd, axis=-1, keepdims=True)))
        return jnp.einsum('hqk,khe->qhe', probs, values, precision=highest)
    starts = (jnp.arange(count // block, dtype=jnp.int32) * block).astype(jnp.int32)
    attended = lax.map(jax.checkpoint(attend), starts).reshape(count, H * HEAD)
    attended = low_back(low(attended))
    attn_branch = low_back(jnp.dot(attended, wout, precision=highest) + bout)
    middle = xf + attn_branch
    normed_two = low(layer_norm(middle, gain_two, shift_two))
    inner = low_back(jnp.dot(normed_two, wfc, precision=highest) + bfc)
    hidden = low(jax.nn.gelu(inner, approximate=True))
    mlp_branch = low_back(jnp.dot(hidden, wproj, precision=highest) + bproj)
    result = middle + mlp_branch
    valid = (segments < SEGS - 1)[:, None]
    output = jnp.where(valid, result, 0.0)
    squares = jnp.stack([jnp.sum(jnp.where(valid, part * part, 0.0)) for part in (result, attn_branch, mlp_branch)])
    return (output, squares)

def reference(tokens, cotangent, lengths, deal, ln1_gain, ln1_shift, w_qkv, bias_qv, w_out, bias_out, ln2_gain, ln2_shift, w_fc, bias_fc, w_proj, bias_proj):
    params = tuple((weight.astype(jnp.float32) for weight in (ln1_gain, ln1_shift, w_qkv, bias_qv, w_out, bias_out, ln2_gain, ln2_shift, w_fc, bias_fc, w_proj, bias_proj)))

    def one_group(totals, item):
        group_x, group_dy, target = item
        row = lengths[target]
        segments = segment_ids(row, group_x.shape[0])

        def run(xf, weights):
            return forward(xf, weights, segments)
        output, pullback, squares = jax.vjp(run, group_x.astype(jnp.float32), params, has_aux=True)
        input_grad, weight_grads = pullback(group_dy.astype(jnp.float32))
        counted = jnp.sum((segments < SEGS - 1).astype(jnp.float32))
        grads, square_sums, count_sum = totals
        updated = (jax.tree.map(jnp.add, grads, weight_grads), square_sums + squares, count_sum + counted)
        return (updated, (output.astype(jnp.bfloat16), input_grad))
    start = (tuple((jnp.zeros_like(weight) for weight in params)), jnp.zeros((3,), jnp.float32), jnp.zeros((), jnp.float32))
    (grads, square_sums, count_sum), (outputs, input_grads) = lax.scan(one_group, start, (tokens, cotangent, deal))
    stats = jnp.sqrt(square_sums / (count_sum * D))
    return (outputs, input_grads, grads[0], grads[1], grads[2], grads[3], grads[4], grads[5], grads[6], grads[7], grads[8], grads[9], grads[10], grads[11], stats)
```

```python
import functools

import jax
import jax.numpy as jnp
from jax import lax
from jax.experimental import pallas as pl
from jax.experimental.pallas import tpu as pltpu
from jax.sharding import PartitionSpec as P

H = 16
HEAD = 64
NT = (((1,), (1,)), ((), ()))
TN = (((0,), (0,)), ((), ()))
F32 = jnp.float32
BF16 = jnp.bfloat16


def seg_starts(len_ref, segs, place):
    start = jnp.zeros_like(place)
    end = jnp.int32(0)
    for k in range(segs - 1):
        end = end + len_ref[k]
        start = jnp.where(place >= end, end, start)
    return start


def head_part(block, h, heads):
    if heads == 1:
        return block
    lane = lax.broadcasted_iota(jnp.int32, block.shape, 1)
    return jnp.where((lane >= h * HEAD) & (lane < (h + 1) * HEAD), block, jnp.zeros_like(block))


def forward_kernel(heads, block, segs, len_ref, qkv_ref, o_ref, lse_ref, vt_ref):
    hd = heads * HEAD
    steps = qkv_ref.shape[0] // block

    def flip(i, _):
        at = pl.multiple_of(i * block, block)
        vt_ref[:, pl.ds(at, block)] = qkv_ref[pl.ds(at, block), 2 * hd : 3 * hd].T
        return 0

    lax.fori_loop(0, steps, flip, 0)
    key_rows = lax.broadcasted_iota(jnp.int32, (block, block), 0)

    def query_step(i, _):
        r0 = pl.multiple_of(i * block, block)
        q = qkv_ref[pl.ds(r0, block), 0:hd] * jnp.asarray(HEAD**-0.5, BF16)
        qs = [head_part(q, h, heads) for h in range(heads)]
        place = r0 + lax.broadcasted_iota(jnp.int32, (1, block), 1)
        start = seg_starts(len_ref, segs, place)
        first = seg_starts(len_ref, segs, r0) // block

        def key_step(j, carry):
            c0 = pl.multiple_of(j * block, block)
            kb = qkv_ref[pl.ds(c0, block), hd : 2 * hd]
            key_pos = key_rows + c0
            ok = (key_pos >= start) & (key_pos <= place)
            out = []
            for h in range(heads):
                top, total, acc = carry[3 * h : 3 * h + 3]
                s = lax.dot_general(kb, qs[h], NT, preferred_element_type=F32)
                s = jnp.where(ok, s, -1e30)
                new = jnp.maximum(top, jnp.max(s, axis=0, keepdims=True))
                p = jnp.exp(s - new)
                shrink = jnp.exp(top - new)
                total = total * shrink + jnp.sum(p, axis=0, keepdims=True)
                vt = vt_ref[h * HEAD : (h + 1) * HEAD, pl.ds(c0, block)]
                acc = acc * shrink + jnp.dot(vt, p.astype(BF16), preferred_element_type=F32)
                out += [new, total, acc]
            return tuple(out)

        init = (
            jnp.full((1, block), -1e30, F32),
            jnp.zeros((1, block), F32),
            jnp.zeros((HEAD, block), F32),
        ) * heads
        res = lax.fori_loop(first, i + 1, key_step, init)
        flat = jnp.concatenate([res[3 * h + 2] / res[3 * h + 1] for h in range(heads)], axis=0)
        o_ref[pl.ds(r0, block), :] = flat.T.astype(BF16)
        for h in range(heads):
            lse_ref[h : h + 1, pl.ds(r0, block)] = res[3 * h] + jnp.log(res[3 * h + 1])
        return 0

    lax.fori_loop(0, steps, query_step, 0)


def backward_kernel(
    heads, block, segs, len_ref, qkv_ref, o_ref, lse_ref, do_ref, d_ref, kt_ref, dk_ref, dv_ref
):
    hd = heads * HEAD
    steps = qkv_ref.shape[0] // block

    def flip(i, _):
        at = pl.multiple_of(i * block, block)
        kt_ref[:, pl.ds(at, block)] = qkv_ref[pl.ds(at, block), hd : 2 * hd].T
        dk_ref[pl.ds(at, block), :] = jnp.zeros((block, hd), F32)
        dv_ref[pl.ds(at, block), :] = jnp.zeros((block, hd), F32)
        return 0

    lax.fori_loop(0, steps, flip, 0)
    key_rows = lax.broadcasted_iota(jnp.int32, (block, block), 0)

    def query_step(i, _):
        r0 = pl.multiple_of(i * block, block)
        q = qkv_ref[pl.ds(r0, block), 0:hd] * jnp.asarray(HEAD**-0.5, BF16)
        do = do_ref[pl.ds(r0, block), :]
        both = (do.astype(F32) * o_ref[pl.ds(r0, block), :].astype(F32)).T
        qs = [head_part(q, h, heads) for h in range(heads)]
        dos = [head_part(do, h, heads) for h in range(heads)]
        q_all = jnp.concatenate(qs, axis=0)
        do_all = jnp.concatenate(dos, axis=0)
        delta = [
            jnp.sum(both[h * HEAD : (h + 1) * HEAD], axis=0, keepdims=True) for h in range(heads)
        ]
        lse = [lse_ref[h : h + 1, pl.ds(r0, block)] for h in range(heads)]
        place = r0 + lax.broadcasted_iota(jnp.int32, (1, block), 1)
        start = seg_starts(len_ref, segs, place)
        first = seg_starts(len_ref, segs, r0) // block

        def key_step(j, dqs):
            c0 = pl.multiple_of(j * block, block)
            kb = qkv_ref[pl.ds(c0, block), hd : 2 * hd]
            vb = qkv_ref[pl.ds(c0, block), 2 * hd : 3 * hd]
            key_pos = key_rows + c0
            ok = (key_pos >= start) & (key_pos <= place)
            ps = []
            dss = []
            out = []
            for h in range(heads):
                s = lax.dot_general(kb, qs[h], NT, preferred_element_type=F32)
                p = jnp.where(ok, jnp.exp(s - lse[h]), 0.0)
                dp = lax.dot_general(vb, dos[h], NT, preferred_element_type=F32)
                ds = (p * (dp - delta[h])).astype(BF16)
                ps.append(p.astype(BF16))
                dss.append(ds)
                kt = kt_ref[h * HEAD : (h + 1) * HEAD, pl.ds(c0, block)]
                out.append(dqs[h] + jnp.dot(kt, ds, preferred_element_type=F32))
            dv_ref[pl.ds(c0, block), :] += jnp.dot(
                jnp.concatenate(ps, axis=1), do_all, preferred_element_type=F32
            )
            dk_ref[pl.ds(c0, block), :] += jnp.dot(
                jnp.concatenate(dss, axis=1), q_all, preferred_element_type=F32
            )
            return tuple(out)

        res = lax.fori_loop(first, i + 1, key_step, (jnp.zeros((HEAD, block), F32),) * heads)
        dq = jnp.concatenate(res, axis=0) * HEAD**-0.5
        d_ref[pl.ds(r0, block), 0:hd] = dq.T.astype(BF16)
        return 0

    lax.fori_loop(0, steps, query_step, 0)

    def finish(i, _):
        at = pl.multiple_of(i * block, block)
        d_ref[pl.ds(at, block), hd : 2 * hd] = dk_ref[pl.ds(at, block), :].astype(BF16)
        d_ref[pl.ds(at, block), 2 * hd : 3 * hd] = dv_ref[pl.ds(at, block), :].astype(BF16)
        return 0

    lax.fori_loop(0, steps, finish, 0)


VM = pl.BlockSpec(memory_space=pltpu.VMEM)
SM = pl.BlockSpec(memory_space=pltpu.SMEM)
LIMIT = 40 << 20


def attention_forward(row, qkv, block):
    rows, wide = qkv.shape
    hd = wide // 3
    heads = hd // HEAD
    pairs = rows * rows // 3 * heads
    return pl.pallas_call(
        functools.partial(forward_kernel, heads, block, row.shape[0]),
        out_shape=(
            jax.ShapeDtypeStruct((rows, hd), BF16),
            jax.ShapeDtypeStruct((heads, rows), F32),
        ),
        in_specs=[SM, VM],
        out_specs=(VM, VM),
        scratch_shapes=[pltpu.VMEM((hd, rows), BF16)],
        compiler_params=pltpu.CompilerParams(vmem_limit_bytes=LIMIT),
        cost_estimate=pl.CostEstimate(
            flops=pairs * 4 * HEAD, bytes_accessed=rows * wide * 4, transcendentals=pairs
        ),
        name="attention_forward",
    )(row, qkv)


def attention_backward(row, qkv, o, lse, do, block):
    rows, wide = qkv.shape
    hd = wide // 3
    heads = hd // HEAD
    pairs = rows * rows // 3 * heads
    return pl.pallas_call(
        functools.partial(backward_kernel, heads, block, row.shape[0]),
        out_shape=jax.ShapeDtypeStruct((rows, wide), BF16),
        in_specs=[SM] + [VM] * 4,
        out_specs=VM,
        scratch_shapes=[
            pltpu.VMEM((hd, rows), BF16),
            pltpu.VMEM((rows, hd), F32),
            pltpu.VMEM((rows, hd), F32),
        ],
        compiler_params=pltpu.CompilerParams(vmem_limit_bytes=LIMIT),
        cost_estimate=pl.CostEstimate(
            flops=pairs * 10 * HEAD, bytes_accessed=rows * wide * 6, transcendentals=pairs
        ),
        name="attention_backward",
    )(row, qkv, o, lse, do)


class Ring:
    def __init__(self, axis):
        self.axis = axis
        self.n = n = lax.axis_size(axis)
        me = lax.axis_index(axis)
        self.pos = jnp.where(me % 2 == 0, me // 2, n - 1 - me // 2)
        order = list(range(0, n, 2)) + list(range(1, n, 2))[::-1]
        self.up = [(order[i], order[(i + 1) % n]) for i in range(n)]
        self.down = [(b, a) for a, b in self.up]

    def shard(self, distance):
        p = (self.pos + distance + self.n) % self.n
        return jnp.where(p < self.n // 2, 2 * p, 2 * (self.n - 1 - p) + 1)

    def send_up(self, value):
        return lax.ppermute(value, self.axis, self.up)

    def send_down(self, value):
        return lax.ppermute(value, self.axis, self.down)

    def gather(self, value):
        half = value.shape[0] // 2
        above = below = value
        out = [(0, value)]
        for step in range(1, self.n // 2):
            below = self.send_up(below)
            above = self.send_down(above)
            out += [(-step, below), (step, above)]
        far = jnp.concatenate([self.send_up(below[:half]), self.send_down(above[half:])], axis=0)
        out.append((self.n // 2, far))
        return out

    def reduce(self, term):
        mid = self.n // 2
        far = term(mid).astype(BF16)
        half = far.shape[0] // 2
        up = self.send_up(far[:half])
        down = self.send_down(far[half:])
        for step in range(mid - 1, 0, -1):
            mine = term(step)
            other = term(-step)
            if step == mid - 1:
                low_mine = jnp.concatenate([mine[:half] + up.astype(F32), mine[half:]], axis=0)
                low_other = jnp.concatenate([other[:half], other[half:] + down.astype(F32)], axis=0)
            else:
                low_mine = mine + up.astype(F32)
                low_other = other + down.astype(F32)
            up = self.send_up(low_mine.astype(BF16))
            down = self.send_down(low_other.astype(BF16))
        return term(0) + up.astype(F32) + down.astype(F32)


def bits(n):
    return [1 << b for b in range(n.bit_length() - 1)]


def swap(value, axis, bit):
    n = lax.axis_size(axis)
    return lax.ppermute(value, axis, [(i, i ^ bit) for i in range(n)])


def cube_gather(value, axis):
    me = lax.axis_index(axis)
    held = [(0, value)]
    for bit in reversed(bits(lax.axis_size(axis))):
        held = held + [(mask ^ bit, swap(block, axis, bit)) for mask, block in held]
    return [(me ^ mask, block) for mask, block in held]


def gather_rows(value, axis):
    count = value.shape[0]
    whole = jnp.zeros((count * lax.axis_size(axis),) + value.shape[1:], value.dtype)
    for index, block in cube_gather(value, axis):
        whole = lax.dynamic_update_slice_in_dim(whole, block, index * count, 0)
    return whole


def scatter_sum(left, right, axis):
    n = lax.axis_size(axis)
    me = lax.axis_index(axis)
    tokens, wide = left.shape
    if n == 1:
        return lax.dot_general(left, right, TN, preferred_element_type=F32)
    split = left.reshape(tokens, n // 2, 2, wide // n)

    def half(which):
        part = lax.dynamic_index_in_dim(split, which, 2, keepdims=False)
        part = part.reshape(tokens, wide // 2)
        return lax.dot_general(part, right, TN, preferred_element_type=F32)

    away = half(1 - me % 2).astype(BF16)
    held = half(me % 2) + swap(away, axis, 1).astype(F32)
    count = n // 2
    for bit in bits(n)[1:]:
        held = held.reshape(count // 2, 2, wide // n, -1)
        side = (me // bit) % 2
        away = lax.dynamic_index_in_dim(held, 1 - side, 1, keepdims=False).astype(BF16)
        mine = lax.dynamic_index_in_dim(held, side, 1, keepdims=False)
        held = mine + swap(away, axis, bit).astype(F32)
        count = count // 2
    return held.reshape(wide // n, right.shape[1])


def ring_total(ring, value):
    rows, columns = value.shape
    wide = columns // ring.n

    def term(distance):
        return lax.dynamic_slice_in_dim(value, ring.shard(distance) * wide, wide, 1)

    mine = ring.reduce(term).astype(BF16)
    whole = jnp.zeros((rows, columns), F32)
    for distance, block in ring.gather(mine):
        whole = lax.dynamic_update_slice_in_dim(
            whole, block.astype(F32), ring.shard(distance) * wide, 1
        )
    return whole


def cube_sum(value):
    for axis in ("fsdp", "seq"):
        for bit in bits(lax.axis_size(axis)):
            value = value + swap(value, axis, bit)
    return value


def layer_norm(value, gain, shift):
    mean = jnp.mean(value, axis=-1, keepdims=True)
    centred = value - mean
    spread = jnp.mean(centred * centred, axis=-1, keepdims=True)
    return centred * lax.rsqrt(spread + 1e-05) * gain + shift


def shards(
    tokens,
    cotangent,
    lengths,
    deal,
    ln1_gain,
    ln1_shift,
    w_qkv,
    bias_qv,
    w_out,
    bias_out,
    ln2_gain,
    ln2_shift,
    w_fc,
    bias_fc,
    w_proj,
    bias_proj,
):
    x = tokens[0]
    dy = cotangent[0]
    rows, width = x.shape
    ring = Ring("seq")
    n_seq = ring.n
    n_fsdp = lax.axis_size("fsdp")
    me_seq = lax.axis_index("seq")
    me_fsdp = lax.axis_index("fsdp")
    group_rows = rows * n_seq
    heads = H // n_seq
    hd = heads * HEAD
    block = rows
    row = lengths[deal[me_fsdp]]
    last = lengths.shape[1] - 1

    small = (ln1_gain, ln1_shift, bias_qv, bias_out, ln2_gain, ln2_shift, bias_fc, bias_proj)
    packed_small = gather_rows(jnp.concatenate(small)[None], "fsdp")
    vectors = []
    at = 0
    for vector in small:
        count = vector.shape[0]
        vectors.append(packed_small[:, at : at + count].reshape(-1).astype(F32))
        at += count
    gain_one, shift_one, bqv, bout, gain_two, shift_two, bfc, bproj = vectors

    own_cols = lax.dynamic_index_in_dim(
        w_qkv.reshape(-1, n_seq, heads, 3, HEAD), me_seq, 1, keepdims=False
    )
    own_cols = own_cols.transpose(0, 2, 1, 3).reshape(-1, 3 * hd)
    w_own = gather_rows(own_cols, "fsdp")
    b_own = lax.dynamic_index_in_dim(bqv.reshape(n_seq, heads, 2, HEAD), me_seq, 0, keepdims=False)
    b_own = jnp.concatenate(
        [b_own[:, 0].reshape(hd), jnp.zeros((hd,), F32), b_own[:, 1].reshape(hd)]
    )

    wout = gather_rows(w_out, "fsdp")
    wfc = gather_rows(w_fc, "fsdp")
    wproj = gather_rows(w_proj, "fsdp")

    low_all = jnp.zeros((group_rows, width), BF16)
    qkv = jnp.zeros((group_rows, 3 * hd), BF16)
    for distance, piece in ring.gather(x):
        low = layer_norm(piece.astype(F32), gain_one, shift_one).astype(BF16)
        part = (jnp.dot(low, w_own, preferred_element_type=F32) + b_own).astype(BF16)
        place = ring.shard(distance) * rows
        low_all = lax.dynamic_update_slice_in_dim(low_all, low, place, 0)
        qkv = lax.dynamic_update_slice_in_dim(qkv, part, place, 0)

    attended, lse = attention_forward(row, qkv, block)
    merged = lax.all_to_all(
        attended.reshape(n_seq, rows, hd), "seq", split_axis=0, concat_axis=0, tiled=True
    )
    merged = merged.transpose(1, 0, 2).reshape(rows, n_seq * hd)

    xf = x.astype(F32)
    ends = jnp.cumsum(row)
    places = me_seq * rows + jnp.arange(rows, dtype=jnp.int32)
    own = jnp.sum((places[:, None] >= ends[None, :]).astype(jnp.int32), axis=1)
    valid = (own < last)[:, None]

    attn_branch = jnp.dot(merged, wout, preferred_element_type=F32) + bout
    middle = xf + attn_branch
    normed_two, norm_two_back = jax.vjp(layer_norm, middle, gain_two, shift_two)
    low_two = normed_two.astype(BF16)
    inner = jnp.dot(low_two, wfc, preferred_element_type=F32) + bfc
    activated, gelu_back = jax.vjp(functools.partial(jax.nn.gelu, approximate=True), inner)
    hidden = activated.astype(BF16)
    mlp_branch = jnp.dot(hidden, wproj, preferred_element_type=F32) + bproj
    result = middle + mlp_branch
    output = jnp.where(valid, result, 0.0).astype(BF16)
    squares = jnp.stack(
        [jnp.sum(jnp.where(valid, part * part, 0.0)) for part in (result, attn_branch, mlp_branch)]
        + [jnp.sum(valid.astype(F32))]
    )

    d_result = jnp.where(valid, dy.astype(F32), 0.0)
    d_mlp = d_result.astype(BF16)
    grad_bproj = jnp.sum(d_result, axis=0)
    d_hidden = lax.dot_general(d_mlp, wproj, NT, preferred_element_type=F32)
    d_inner = gelu_back(d_hidden)[0].astype(BF16)
    grad_bfc = jnp.sum(d_inner.astype(F32), axis=0)
    d_two = lax.dot_general(d_inner, wfc, NT, preferred_element_type=F32)
    d_mid_norm, grad_gain_two, grad_shift_two = norm_two_back(d_two)
    d_middle = d_result + d_mid_norm
    d_attn = d_middle.astype(BF16)
    grad_bout = jnp.sum(d_attn.astype(F32), axis=0)
    d_merged = lax.dot_general(d_attn, wout, NT, preferred_element_type=F32).astype(BF16)
    d_heads = lax.all_to_all(
        d_merged.reshape(rows, n_seq, hd).transpose(1, 0, 2),
        "seq",
        split_axis=0,
        concat_axis=0,
        tiled=True,
    ).reshape(group_rows, hd)

    grad_wproj = ring_total(ring, scatter_sum(hidden, d_mlp, "fsdp"))
    share_wfc = scatter_sum(low_two, d_inner, "fsdp")
    share_wout = scatter_sum(merged, d_attn, "fsdp")
    total = ring_total(ring, jnp.concatenate([share_wfc, share_wout], axis=1))
    grad_wfc = total[:, : wfc.shape[1]]
    grad_wout = total[:, wfc.shape[1] :]

    d_own = attention_backward(row, qkv, attended, lse, d_heads, block)

    share_qkv = scatter_sum(low_all, d_own, "fsdp").astype(BF16)
    parts = jnp.zeros((n_seq,) + share_qkv.shape, BF16)
    for distance, piece in ring.gather(share_qkv):
        parts = lax.dynamic_update_slice_in_dim(parts, piece[None], ring.shard(distance), 0)
    grad_wqkv = (
        parts.reshape(n_seq, -1, 3, heads, HEAD)
        .transpose(1, 0, 3, 2, 4)
        .reshape(-1, 3 * H * HEAD)
        .astype(F32)
    )
    d_sums = jnp.sum(d_own.astype(F32), axis=0).reshape(3, heads, HEAD)
    d_sums = jnp.stack([d_sums[0], d_sums[2]], axis=1).reshape(1, 2 * hd)
    grad_bqv = lax.dynamic_update_slice_in_dim(
        jnp.zeros((n_seq, 2 * hd), F32), d_sums, me_seq, 0
    ).reshape(-1)

    def share_one(distance):
        part = lax.dynamic_slice_in_dim(d_own, ring.shard(distance) * rows, rows, 0)
        return lax.dot_general(part, w_own, NT, preferred_element_type=F32)

    d_one = ring.reduce(share_one)
    _, norm_one_back = jax.vjp(layer_norm, xf, gain_one, shift_one)
    d_in_norm, grad_gain_one, grad_shift_one = norm_one_back(d_one)
    input_grad = d_middle + d_in_norm

    def own_share(vector):
        count = vector.shape[0] // n_fsdp
        return lax.dynamic_slice_in_dim(vector, me_fsdp * count, count, 0)

    early = [grad_bout, grad_gain_two, grad_shift_two, grad_bfc, grad_bproj, squares]
    late = [grad_gain_one, grad_shift_one, grad_bqv]

    def summed(vectors):
        flat = cube_sum(jnp.concatenate(vectors))
        out = []
        at = 0
        for vector in vectors:
            out.append(flat[at : at + vector.shape[0]])
            at += vector.shape[0]
        return out

    sum_bout, sum_g2, sum_s2, sum_bfc, sum_bproj, sum_squares = summed(early)
    sum_g1, sum_s1, sum_bqv = summed(late)
    stats = jnp.sqrt(sum_squares[:3] / (sum_squares[3] * width))
    return (
        output[None],
        input_grad[None],
        own_share(sum_g1),
        own_share(sum_s1),
        grad_wqkv,
        own_share(sum_bqv),
        grad_wout,
        own_share(sum_bout),
        own_share(sum_g2),
        own_share(sum_s2),
        grad_wfc,
        own_share(sum_bfc),
        grad_wproj,
        own_share(sum_bproj),
        stats,
    )


def solution(mesh):
    rows_split = P("fsdp", "seq", None)
    matrix = P("fsdp", None)
    vector = P("fsdp")
    params = (
        vector,
        vector,
        matrix,
        vector,
        matrix,
        vector,
        vector,
        vector,
        matrix,
        vector,
        matrix,
        vector,
    )
    return jax.shard_map(
        shards,
        mesh=mesh,
        in_specs=(rows_split, rows_split, P(), P()) + params,
        out_specs=(rows_split, rows_split) + params + (P(),),
        check_vma=False,
    )
```

```python
import functools

import jax
import jax.numpy as jnp
from jax import lax
from jax.experimental import pallas as pl
from jax.experimental.pallas import tpu as pltpu
from jax.sharding import PartitionSpec as P

H = 16
HEAD = 64
NT = (((1,), (1,)), ((), ()))
TN = (((0,), (0,)), ((), ()))
F32 = jnp.float32
BF16 = jnp.bfloat16


def seg_starts(len_ref, segs, place):
    start = jnp.zeros_like(place)
    end = jnp.int32(0)
    for k in range(segs - 1):
        end = end + len_ref[k]
        start = jnp.where(place >= end, end, start)
    return start


def head_part(block, h, heads):
    if heads == 1:
        return block
    lane = lax.broadcasted_iota(jnp.int32, block.shape, 1)
    return jnp.where((lane >= h * HEAD) & (lane < (h + 1) * HEAD), block, jnp.zeros_like(block))


def forward_kernel(heads, block, segs, len_ref, qkv_ref, o_ref, lse_ref, vt_ref):
    hd = heads * HEAD
    steps = qkv_ref.shape[0] // block

    def flip(i, _):
        at = pl.multiple_of(i * block, block)
        vt_ref[:, pl.ds(at, block)] = qkv_ref[pl.ds(at, block), 2 * hd : 3 * hd].T
        return 0

    lax.fori_loop(0, steps, flip, 0)
    key_rows = lax.broadcasted_iota(jnp.int32, (block, block), 0)

    def query_step(i, _):
        r0 = pl.multiple_of(i * block, block)
        q = qkv_ref[pl.ds(r0, block), 0:hd] * jnp.asarray(HEAD**-0.5, BF16)
        qs = [head_part(q, h, heads) for h in range(heads)]
        place = r0 + lax.broadcasted_iota(jnp.int32, (1, block), 1)
        start = seg_starts(len_ref, segs, place)
        first = seg_starts(len_ref, segs, r0) // block

        def key_step(j, carry):
            c0 = pl.multiple_of(j * block, block)
            kb = qkv_ref[pl.ds(c0, block), hd : 2 * hd]
            key_pos = key_rows + c0
            ok = (key_pos >= start) & (key_pos <= place)
            out = []
            for h in range(heads):
                top, total, acc = carry[3 * h : 3 * h + 3]
                s = lax.dot_general(kb, qs[h], NT, preferred_element_type=F32)
                s = jnp.where(ok, s, -1e30)
                new = jnp.maximum(top, jnp.max(s, axis=0, keepdims=True))
                p = jnp.exp(s - new)
                shrink = jnp.exp(top - new)
                total = total * shrink + jnp.sum(p, axis=0, keepdims=True)
                vt = vt_ref[h * HEAD : (h + 1) * HEAD, pl.ds(c0, block)]
                acc = acc * shrink + jnp.dot(vt, p.astype(BF16), preferred_element_type=F32)
                out += [new, total, acc]
            return tuple(out)

        init = (
            jnp.full((1, block), -1e30, F32),
            jnp.zeros((1, block), F32),
            jnp.zeros((HEAD, block), F32),
        ) * heads
        res = lax.fori_loop(first, i + 1, key_step, init)
        flat = jnp.concatenate([res[3 * h + 2] / res[3 * h + 1] for h in range(heads)], axis=0)
        o_ref[pl.ds(r0, block), :] = flat.T.astype(BF16)
        for h in range(heads):
            lse_ref[h : h + 1, pl.ds(r0, block)] = res[3 * h] + jnp.log(res[3 * h + 1])
        return 0

    lax.fori_loop(0, steps, query_step, 0)


def backward_kernel(heads, h, block, segs, len_ref, qkv_ref, o_ref, lse_ref, do_ref, *rest):
    before_ref = rest[0] if h else None
    d_ref, kt_ref, dq_ref, dk_ref, dv_ref = rest[-5:]
    hd = heads * HEAD
    steps = qkv_ref.shape[0] // block
    mine = slice(h * HEAD, (h + 1) * HEAD)

    def flip(i, _):
        at = pl.multiple_of(i * block, block)
        kt_ref[:, pl.ds(at, block)] = qkv_ref[pl.ds(at, block), hd : 2 * hd].T[mine]
        dk_ref[pl.ds(at, block), :] = jnp.zeros((block, hd), F32)
        dv_ref[pl.ds(at, block), :] = jnp.zeros((block, hd), F32)
        return 0

    lax.fori_loop(0, steps, flip, 0)
    key_rows = lax.broadcasted_iota(jnp.int32, (block, block), 0)

    def query_step(i, _):
        r0 = pl.multiple_of(i * block, block)
        q = qkv_ref[pl.ds(r0, block), 0:hd] * jnp.asarray(HEAD**-0.5, BF16)
        q = head_part(q, h, heads)
        do = head_part(do_ref[pl.ds(r0, block), :], h, heads)
        both = (do.astype(F32) * o_ref[pl.ds(r0, block), :].astype(F32)).T
        delta = jnp.sum(both[mine], axis=0, keepdims=True)
        lse = lse_ref[h : h + 1, pl.ds(r0, block)]
        place = r0 + lax.broadcasted_iota(jnp.int32, (1, block), 1)
        start = seg_starts(len_ref, segs, place)
        first = seg_starts(len_ref, segs, r0) // block

        def key_step(j, dq):
            c0 = pl.multiple_of(j * block, block)
            kb = qkv_ref[pl.ds(c0, block), hd : 2 * hd]
            vb = qkv_ref[pl.ds(c0, block), 2 * hd : 3 * hd]
            key_pos = key_rows + c0
            ok = (key_pos >= start) & (key_pos <= place)
            s = lax.dot_general(kb, q, NT, preferred_element_type=F32)
            p = jnp.where(ok, jnp.exp(s - lse), 0.0)
            dp = lax.dot_general(vb, do, NT, preferred_element_type=F32)
            ds = (p * (dp - delta)).astype(BF16)
            dv_ref[pl.ds(c0, block), :] += jnp.dot(p.astype(BF16), do, preferred_element_type=F32)
            dk_ref[pl.ds(c0, block), :] += jnp.dot(ds, q, preferred_element_type=F32)
            return dq + jnp.dot(kt_ref[:, pl.ds(c0, block)], ds, preferred_element_type=F32)

        dq = lax.fori_loop(first, i + 1, key_step, jnp.zeros((HEAD, block), F32))
        dq_ref[pl.ds(r0, block), :] = (dq * HEAD**-0.5).T
        return 0

    lax.fori_loop(0, steps, query_step, 0)

    def finish(i, _):
        at = pl.multiple_of(i * block, block)
        rows = pl.ds(at, block)
        d = [dq_ref[rows, :], dk_ref[rows, mine], dv_ref[rows, mine]]
        d = jnp.concatenate(d, axis=1).astype(BF16)
        if before_ref is not None:
            d = jnp.concatenate([before_ref[rows, :], d], axis=1)
        d_ref[rows, :] = d
        return 0

    lax.fori_loop(0, steps, finish, 0)


def takes(us):
    return pl.CostEstimate(flops=int(us * 1.1e9), bytes_accessed=1 << 20, transcendentals=0)


VM = pl.BlockSpec(memory_space=pltpu.VMEM)
SM = pl.BlockSpec(memory_space=pltpu.SMEM)
LIMIT = 40 << 20


def attention_forward(row, qkv, block):
    rows, wide = qkv.shape
    hd = wide // 3
    heads = hd // HEAD
    return pl.pallas_call(
        functools.partial(forward_kernel, heads, block, row.shape[0]),
        out_shape=(
            jax.ShapeDtypeStruct((rows, hd), BF16),
            jax.ShapeDtypeStruct((heads, rows), F32),
        ),
        in_specs=[SM, VM],
        out_specs=(VM, VM),
        scratch_shapes=[pltpu.VMEM((hd, rows), BF16)],
        compiler_params=pltpu.CompilerParams(vmem_limit_bytes=LIMIT),
        cost_estimate=takes(22),
        name="attention_forward",
    )(row, qkv)


def attention_backward(row, qkv, o, lse, do, block, h, before=()):
    rows, wide = qkv.shape
    hd = wide // 3
    heads = hd // HEAD
    return pl.pallas_call(
        functools.partial(backward_kernel, heads, h, block, row.shape[0]),
        out_shape=jax.ShapeDtypeStruct((rows, (h + 1) * 3 * HEAD), BF16),
        in_specs=[SM] + [VM] * (4 + len(before)),
        out_specs=VM,
        scratch_shapes=[
            pltpu.VMEM((HEAD, rows), BF16),
            pltpu.VMEM((rows, HEAD), F32),
            pltpu.VMEM((rows, hd), F32),
            pltpu.VMEM((rows, hd), F32),
        ],
        compiler_params=pltpu.CompilerParams(vmem_limit_bytes=LIMIT),
        cost_estimate=takes(16),
        name="attention_backward",
    )(row, qkv, o, lse, do, *before)


def tier_bounds(n):
    bounds = [(0, 1)]
    while bounds[-1][1] < n:
        bounds.append((bounds[-1][1], 2 * bounds[-1][1]))
    return bounds


def norm_parts(value):
    mean = jnp.mean(value, axis=-1, keepdims=True)
    centred = value - mean
    spread = jnp.mean(centred * centred, axis=-1, keepdims=True)
    scale = lax.rsqrt(spread + 1e-05)
    return centred * scale, scale


def project_kernel(at_ref, x_ref, gain_ref, shift_ref, w_ref, b_ref, *rest):
    x_out, qkv_out = rest[-2:]
    x = x_ref[...]
    n, _ = norm_parts(x.astype(F32))
    low = (n * gain_ref[...] + shift_ref[...]).astype(BF16)
    mixed = jnp.dot(low, w_ref[...], preferred_element_type=F32) + b_ref[...]
    x_out[...] = x
    qkv_out[...] = mixed.astype(BF16)


def project(at, x, gain, shift, w, b, total, held):
    rows, width = x.shape
    wide = w.shape[1]

    def fixed(shape):
        return pl.BlockSpec(shape, lambda i, at: (0, 0))

    given = () if held is None else held
    return pl.pallas_call(
        project_kernel,
        grid_spec=pltpu.PrefetchScalarGridSpec(
            num_scalar_prefetch=1,
            grid=(1,),
            in_specs=[
                fixed((rows, width)),
                fixed((1, width)),
                fixed((1, width)),
                fixed((width, wide)),
                fixed((1, wide)),
            ]
            + [pl.BlockSpec(memory_space=pl.ANY)] * len(given),
            out_specs=[
                pl.BlockSpec((rows, width), lambda i, at: (at[0], 0)),
                pl.BlockSpec((rows, wide), lambda i, at: (at[0], 0)),
            ],
        ),
        out_shape=(
            jax.ShapeDtypeStruct((total, width), BF16),
            jax.ShapeDtypeStruct((total, wide), BF16),
        ),
        input_output_aliases={6: 0, 7: 1} if given else {},
        cost_estimate=takes(2),
        compiler_params=pltpu.CompilerParams(vmem_limit_bytes=24 << 20),
        name="project",
    )(at.reshape(1), x, gain, shift, w, b, *given)


def attend_out_kernel(
    count_ref,
    merged_ref,
    x_ref,
    wout_ref,
    bout_ref,
    gain_ref,
    shift_ref,
    low_ref,
    middle_ref,
    stat_ref,
):
    rows = x_ref.shape[0]
    merged = jnp.concatenate([merged_ref[k] for k in range(merged_ref.shape[0])], axis=1)
    attn = jnp.dot(merged, wout_ref[...], preferred_element_type=F32) + bout_ref[...]
    middle = x_ref[...].astype(F32) + attn
    middle_ref[...] = middle
    n, _ = norm_parts(middle)
    low_ref[...] = (n * gain_ref[...] + shift_ref[...]).astype(BF16)
    valid = lax.broadcasted_iota(jnp.int32, (rows, 1), 0) < count_ref[0]
    stat_ref[...] = jnp.sum(jnp.where(valid, attn * attn, 0.0), axis=0, keepdims=True)


def attend_out(count, merged, x, wout, bout, gain, shift):
    rows, width = x.shape
    return pl.pallas_call(
        attend_out_kernel,
        in_specs=[SM] + [VM] * 6,
        out_specs=(VM,) * 3,
        out_shape=(
            jax.ShapeDtypeStruct((rows, width), BF16),
            jax.ShapeDtypeStruct((rows, width), F32),
            jax.ShapeDtypeStruct((1, width), F32),
        ),
        cost_estimate=takes(5),
        compiler_params=pltpu.CompilerParams(vmem_limit_bytes=40 << 20),
        name="attend_out",
    )(count, merged, x, wout, bout, gain, shift)


GELU = 0.7978845608028654


def feed_kernel(n_fsdp, rel_ref, count_ref, bfc_ref, wproj_ref, wfc_ref, *rest):
    low_refs, rest = rest[:n_fsdp], rest[n_fsdp:]
    dy_refs, rest = rest[:n_fsdp], rest[n_fsdp:]
    tiers = tier_bounds(n_fsdp)
    dtwo_refs, rest = rest[: len(tiers)], rest[len(tiers) :]
    hidden_ref, di_ref, dmlp_ref, low_s = rest
    step = pl.program_id(0)
    rows = low_s.shape[0]
    valid = lax.broadcasted_iota(jnp.int32, (rows, 1), 0) < count_ref[step]

    for k in range(n_fsdp):

        @pl.when(step == k)
        def _():
            low_s[...] = low_refs[k][...]
            dy = dy_refs[k][...]
            dmlp_ref[...] = jnp.where(valid, dy, jnp.zeros_like(dy))

    u = jnp.dot(low_s[...], wfc_ref[...], preferred_element_type=F32) + bfc_ref[...]
    dh = lax.dot_general(dmlp_ref[...], wproj_ref[...], NT, preferred_element_type=F32)
    square = u * u
    t = jnp.tanh(GELU * u * (1.0 + 0.044715 * square))
    side = 0.5 * (1.0 + t)
    hidden_ref[...] = (u * side).astype(BF16)
    slope = side + 0.5 * u * (1.0 - t * t) * (GELU * (1.0 + 3 * 0.044715 * square))
    di = (dh * slope).astype(BF16)
    di_ref[...] = di
    dtwo = lax.dot_general(di, wfc_ref[...], NT, preferred_element_type=F32)
    for (lo, hi), out_ref in zip(tiers, dtwo_refs):

        @pl.when((step >= lo) & (step < hi))
        def _():
            out_ref[...] = dtwo.astype(out_ref.dtype)


def feed(rel, counts, low_pieces, dy_pieces, wfc, wproj, bfc):
    rows, width = low_pieces[0].shape
    n_fsdp = len(low_pieces)
    wide = wproj.shape[0]
    tiers = tier_bounds(n_fsdp)

    def whole(*shape):
        return pl.BlockSpec(shape, lambda g, *_: (0,) * len(shape), pipeline_mode=pl.Buffered(1))

    def tier(lo, hi):
        return pl.BlockSpec((rows, width), lambda g, *_: (jnp.clip(g - lo, 0, hi - lo - 1), 0))

    each = pl.BlockSpec((rows, wide), lambda g, *_: (g, 0))
    return pl.pallas_call(
        functools.partial(feed_kernel, n_fsdp),
        grid_spec=pltpu.PrefetchScalarGridSpec(
            num_scalar_prefetch=2,
            grid=(n_fsdp,),
            in_specs=[
                whole(1, wide),
                whole(wide, width),
                pl.BlockSpec(
                    (width, wide), lambda g, rel, _: (0, rel[0]), pipeline_mode=pl.Buffered(1)
                ),
            ]
            + [whole(rows, width)] * (2 * n_fsdp),
            out_specs=[tier(lo, hi) for lo, hi in tiers]
            + [each, each, pl.BlockSpec((rows, width), lambda g, *_: (g, 0))],
            scratch_shapes=[pltpu.VMEM((rows, width), BF16)],
        ),
        out_shape=tuple(
            [
                jax.ShapeDtypeStruct(((hi - lo) * rows, width), F32 if lo == 0 else BF16)
                for lo, hi in tiers
            ]
            + [jax.ShapeDtypeStruct((n_fsdp * rows, wide), BF16)] * 2
            + [jax.ShapeDtypeStruct((n_fsdp * rows, width), BF16)]
        ),
        cost_estimate=takes(20),
        compiler_params=pltpu.CompilerParams(vmem_limit_bytes=52 << 20),
        name="feed",
    )(rel, counts, bfc, wproj, wfc, *low_pieces, *dy_pieces)


def feed_grads_kernel(n_fsdp, hidden_ref, di_ref, dmlp_ref, wproj_ref, *rest):
    low_refs, rest = rest[:n_fsdp], rest[n_fsdp:]
    tiers = tier_bounds(n_fsdp)
    mlp_refs, rest = rest[: len(tiers)], rest[len(tiers) :]
    gproj_ref, gfc_ref, gbfc_ref = rest[:3]
    scratch = rest[3:]
    step = pl.program_id(0)
    rows, wide = hidden_ref.shape
    n_seq, _, thin, _ = gfc_ref.shape
    width = dmlp_ref.shape[1]
    share = width // n_fsdp

    hidden = hidden_ref[...]
    di = di_ref[...]
    mlp = jnp.dot(hidden, wproj_ref[...], preferred_element_type=F32)
    for (lo, hi), out_ref in zip(tiers, mlp_refs):

        @pl.when((step >= lo) & (step < hi))
        def _():
            out_ref[...] = mlp.astype(out_ref.dtype)

    sums = jnp.sum(di.astype(F32), axis=0, keepdims=True)

    @pl.when(step == 0)
    def _():
        gbfc_ref[...] = sums

    @pl.when(step > 0)
    def _():
        gbfc_ref[...] += sums

    def store_fc(i, g):
        for k in range(n_seq):
            gfc_ref[k, i] = g[k * thin : (k + 1) * thin]

    if len(scratch) == 3:
        low_s, proj_s, fc_s = scratch

        @pl.when(step == 0)
        def _():
            proj_s[...] = jnp.zeros_like(proj_s)
            fc_s[...] = jnp.zeros_like(fc_s)

        for k in range(n_fsdp):

            @pl.when(step == k)
            def _():
                low_s[...] = low_refs[k][...]

        proj_s[...] += jnp.dot(hidden.T, dmlp_ref[...], preferred_element_type=F32)
        fc_s[...] += jnp.dot(low_s[...].T, di, preferred_element_type=F32)

        @pl.when(step == n_fsdp - 1)
        def _():
            gproj_ref[...] = proj_s[...].astype(BF16)
            for i in range(n_fsdp):
                store_fc(i, fc_s[i * share : (i + 1) * share, :].astype(BF16))

        return

    hiddent_s, di_s, dmlp_s, lowt_s = scratch
    for k in range(n_fsdp):

        @pl.when(step == k)
        def _():
            at = slice(k * rows, (k + 1) * rows)
            hiddent_s[:, at] = hidden.T
            di_s[at, :] = di
            dmlp_s[at, :] = dmlp_ref[...]
            lowt_s[:, at] = low_refs[k][...].T

    @pl.when(step == n_fsdp - 1)
    def _():
        tile = min(256, wide)

        def proj_tile(i, _):
            at = pl.multiple_of(i * tile, tile)
            g = jnp.dot(hiddent_s[pl.ds(at, tile), :], dmlp_s[...], preferred_element_type=F32)
            gproj_ref[pl.ds(at, tile), :] = g.astype(BF16)
            return 0

        lax.fori_loop(0, wide // tile, proj_tile, 0)

        def fc_tile(i, _):
            at = pl.multiple_of(i * share, share)
            g = jnp.dot(lowt_s[pl.ds(at, share), :], di_s[...], preferred_element_type=F32)
            store_fc(i, g.astype(BF16))
            return 0

        lax.fori_loop(0, n_fsdp, fc_tile, 0)


def feed_grads(hidden, di, dmlp, wproj, low_pieces, n_seq):
    rows, width = low_pieces[0].shape
    n_fsdp = len(low_pieces)
    wide = wproj.shape[0]
    total = n_fsdp * rows
    thin = width // n_fsdp // n_seq
    tiers = tier_bounds(n_fsdp)
    if total > 2048:
        scratch = [pltpu.VMEM((rows, width), BF16)]
        scratch += [pltpu.VMEM((wide, width), F32), pltpu.VMEM((width, wide), F32)]
    else:
        scratch = [pltpu.VMEM((wide, total), BF16), pltpu.VMEM((total, wide), BF16)]
        scratch += [pltpu.VMEM((total, width), BF16), pltpu.VMEM((width, total), BF16)]

    def whole(*shape):
        return pl.BlockSpec(shape, lambda g: (0,) * len(shape), pipeline_mode=pl.Buffered(1))

    def last(*shape):
        return pl.BlockSpec(shape, lambda g: (0,) * len(shape))

    def tier(lo, hi):
        return pl.BlockSpec((rows, width), lambda g: (jnp.clip(g - lo, 0, hi - lo - 1), 0))

    each = pl.BlockSpec((rows, wide), lambda g: (g, 0))
    return pl.pallas_call(
        functools.partial(feed_grads_kernel, n_fsdp),
        grid=(n_fsdp,),
        in_specs=[each, each, pl.BlockSpec((rows, width), lambda g: (g, 0)), whole(wide, width)]
        + [whole(rows, width)] * n_fsdp,
        out_specs=[tier(lo, hi) for lo, hi in tiers]
        + [last(wide, width), last(n_seq, n_fsdp, thin, wide), last(1, wide)],
        out_shape=tuple(
            [
                jax.ShapeDtypeStruct(((hi - lo) * rows, width), F32 if lo == 0 else BF16)
                for lo, hi in tiers
            ]
            + [
                jax.ShapeDtypeStruct((wide, width), BF16),
                jax.ShapeDtypeStruct((n_seq, n_fsdp, thin, wide), BF16),
                jax.ShapeDtypeStruct((1, wide), F32),
            ]
        ),
        scratch_shapes=scratch,
        cost_estimate=takes(18),
        compiler_params=pltpu.CompilerParams(vmem_limit_bytes=52 << 20),
        name="feed_grads",
    )(hidden, di, dmlp, wproj, *low_pieces)


def middle_back_kernel(
    n_fsdp,
    terms,
    count_ref,
    merged_ref,
    middle_ref,
    dy_ref,
    gain_ref,
    wout_ref,
    later_ref,
    *rest,
):
    term_refs, rest = rest[:terms], rest[terms:]
    gout_ref, d_middle_ref, d_merged_ref, vec_ref, passed_ref = rest
    passed_ref[...] = later_ref[...]
    n_seq, rows, hd = merged_ref.shape
    thin = gout_ref.shape[2]
    valid = lax.broadcasted_iota(jnp.int32, (rows, 1), 0) < count_ref[0]
    n, scale = norm_parts(middle_ref[...])
    d_two = functools.reduce(jnp.add, [ref[...].astype(F32) for ref in term_refs])
    d_result = jnp.where(valid, dy_ref[...].astype(F32), 0.0)
    e = d_two * gain_ref[...]
    d_middle = d_result + scale * (
        e - jnp.mean(e, axis=-1, keepdims=True) - n * jnp.mean(e * n, axis=-1, keepdims=True)
    )
    d_middle_ref[...] = d_middle
    d_attn = d_middle.astype(BF16)
    d_merged = lax.dot_general(d_attn, wout_ref[...], NT, preferred_element_type=F32).astype(BF16)
    for k in range(n_seq):
        d_merged_ref[k] = d_merged[:, k * hd : (k + 1) * hd]
    vec_ref[0:1, :] = jnp.sum(d_attn.astype(F32), axis=0, keepdims=True)
    vec_ref[1:2, :] = jnp.sum(d_two * n, axis=0, keepdims=True)
    vec_ref[2:3, :] = jnp.sum(d_two, axis=0, keepdims=True)
    vec_ref[3:4, :] = jnp.sum(d_result, axis=0, keepdims=True)
    merged = jnp.concatenate([merged_ref[k] for k in range(n_seq)], axis=1)
    gout = jnp.dot(merged.T, d_attn, preferred_element_type=F32).astype(BF16)
    for f in range(n_fsdp):
        for k in range(n_seq):
            at = (f * n_seq + k) * thin
            gout_ref[k, f] = gout[at : at + thin]


def middle_back(n_fsdp, count, merged, middle, dy, gain, wout, later, terms):
    rows, width = middle.shape
    n_seq = merged.shape[0]
    thin = width // n_fsdp // n_seq
    return pl.pallas_call(
        functools.partial(middle_back_kernel, n_fsdp, len(terms)),
        in_specs=[SM] + [VM] * (6 + len(terms)),
        out_specs=(VM,) * 5,
        out_shape=(
            jax.ShapeDtypeStruct((n_seq, n_fsdp, thin, width), BF16),
            jax.ShapeDtypeStruct((rows, width), F32),
            jax.ShapeDtypeStruct(merged.shape, BF16),
            jax.ShapeDtypeStruct((4, width), F32),
            jax.ShapeDtypeStruct(later.shape, BF16),
        ),
        cost_estimate=takes(7),
        compiler_params=pltpu.CompilerParams(vmem_limit_bytes=48 << 20),
        name="middle_back",
    )(count, merged, middle, dy, gain, wout, later, *terms)


def finish_kernel(count_ref, middle_ref, bproj_ref, *rest):
    term_refs, output_ref, stat_ref = rest[:-2], rest[-2], rest[-1]
    rows = middle_ref.shape[0]
    valid = lax.broadcasted_iota(jnp.int32, (rows, 1), 0) < count_ref[0]
    branch = functools.reduce(jnp.add, [ref[...].astype(F32) for ref in term_refs])
    branch = branch + bproj_ref[...]
    result = middle_ref[...] + branch
    output_ref[...] = jnp.where(valid, result, 0.0).astype(BF16)
    stat_ref[0:1, :] = jnp.sum(jnp.where(valid, result * result, 0.0), axis=0, keepdims=True)
    stat_ref[1:2, :] = jnp.sum(jnp.where(valid, branch * branch, 0.0), axis=0, keepdims=True)


def finish(count, middle, bproj, terms):
    rows, width = middle.shape
    return pl.pallas_call(
        finish_kernel,
        in_specs=[SM] + [VM] * (2 + len(terms)),
        out_specs=(VM,) * 2,
        out_shape=(
            jax.ShapeDtypeStruct((rows, width), BF16),
            jax.ShapeDtypeStruct((2, width), F32),
        ),
        cost_estimate=takes(3),
        compiler_params=pltpu.CompilerParams(vmem_limit_bytes=32 << 20),
        name="finish",
    )(count, middle, bproj, *terms)


def qkv_grad_kernel(x_ref, d_ref, w_ref, gain_ref, shift_ref, g_ref, vec_ref, sum_ref, acc):
    step = pl.program_id(0)
    n, _ = norm_parts(x_ref[...].astype(F32))
    low = (n * gain_ref[...] + shift_ref[...]).astype(BF16)
    d = d_ref[...]
    part = lax.dot_general(d, w_ref[...], NT, preferred_element_type=F32)
    gain_part = jnp.sum(part * n, axis=0, keepdims=True)
    shift_part = jnp.sum(part, axis=0, keepdims=True)
    sum_part = jnp.sum(d.astype(F32), axis=0, keepdims=True)
    g = jnp.dot(low.T, d, preferred_element_type=F32)

    @pl.when(step == 0)
    def _():
        acc[...] = g
        vec_ref[0:1, :] = gain_part
        vec_ref[1:2, :] = shift_part
        sum_ref[...] = sum_part

    @pl.when(step > 0)
    def _():
        acc[...] += g
        vec_ref[0:1, :] += gain_part
        vec_ref[1:2, :] += shift_part
        sum_ref[...] += sum_part

    @pl.when(step == pl.num_programs(0) - 1)
    def _():
        g_ref[...] = acc[...].astype(BF16)


def qkv_grads(x_all, d_own, w_own, gain, shift, block):
    total, width = x_all.shape
    wide = w_own.shape[1]

    def whole(*shape):
        return pl.BlockSpec(shape, lambda g: (0,) * len(shape))

    return pl.pallas_call(
        qkv_grad_kernel,
        grid=(total // block,),
        in_specs=[
            pl.BlockSpec((block, width), lambda g: (g, 0)),
            pl.BlockSpec((block, wide), lambda g: (g, 0)),
            whole(width, wide),
            whole(1, width),
            whole(1, width),
        ],
        out_specs=[whole(width, wide), whole(2, width), whole(1, wide)],
        out_shape=(
            jax.ShapeDtypeStruct((width, wide), BF16),
            jax.ShapeDtypeStruct((2, width), F32),
            jax.ShapeDtypeStruct((1, wide), F32),
        ),
        scratch_shapes=[pltpu.VMEM((width, wide), F32)],
        cost_estimate=takes(13),
        compiler_params=pltpu.CompilerParams(vmem_limit_bytes=40 << 20),
        name="qkv_grads",
    )(x_all, d_own, w_own, gain, shift)


def input_grad_kernel(d_ref, x_ref, gain_ref, d_middle_ref, w_ref, out_ref, d_s, one_s):
    step = pl.program_id(0)
    steps, _, share = one_s.shape

    @pl.when(step == 0)
    def _():
        d_s[...] = jnp.concatenate([d_ref[k] for k in range(d_ref.shape[0])], axis=1)

    one_s[step] = lax.dot_general(d_s[...], w_ref[...], NT, preferred_element_type=F32)

    @pl.when(step == steps - 1)
    def _():
        n, scale = norm_parts(x_ref[...].astype(F32))
        d_one = jnp.concatenate([one_s[k] for k in range(steps)], axis=1)
        e = d_one * gain_ref[...]
        out_ref[...] = d_middle_ref[...] + scale * (
            e - jnp.mean(e, axis=-1, keepdims=True) - n * jnp.mean(e * n, axis=-1, keepdims=True)
        )


def input_gradient(d_packed, w_all, x, gain, d_middle):
    rows, width = x.shape
    n_seq, _, each = d_packed.shape
    wide = w_all.shape[1]
    steps = 4

    def whole(*shape):
        return pl.BlockSpec(shape, lambda g: (0,) * len(shape), pipeline_mode=pl.Buffered(1))

    return pl.pallas_call(
        input_grad_kernel,
        grid=(steps,),
        in_specs=[
            whole(n_seq, rows, each),
            whole(rows, width),
            whole(1, width),
            whole(rows, width),
            pl.BlockSpec((width // steps, wide), lambda g: (g, 0)),
        ],
        out_specs=whole(rows, width),
        out_shape=jax.ShapeDtypeStruct((rows, width), F32),
        scratch_shapes=[
            pltpu.VMEM((rows, wide), BF16),
            pltpu.VMEM((steps, rows, width // steps), F32),
        ],
        cost_estimate=takes(8),
        compiler_params=pltpu.CompilerParams(vmem_limit_bytes=40 << 20),
        name="input_gradient",
    )(d_packed, x, gain, d_middle, w_all)


def place_kernel(layout, count, order_ref, rel_ref, *refs):
    outs = refs[len(refs) - len(layout) :]
    step = pl.program_id(0)
    for k in range(count):

        @pl.when(step == k)
        def _():
            thin = refs[k].shape[0]
            at = 0
            for (kind, wide, blocks), out in zip(layout, outs):
                each = wide // blocks
                for a in range(blocks):
                    part = refs[k][:, at : at + each].astype(F32)
                    at += each
                    if kind == "rel":
                        lanes = pl.ds(pl.multiple_of(rel_ref[a] * each, each), each)
                        out[0, :, lanes] = part
                    elif len(out.shape) == 3:
                        out[0, a * thin : (a + 1) * thin, :] = part
                    else:
                        out[a * thin : (a + 1) * thin, :] = part


def place(order, rel, pieces, layout, n, held=None):
    thin = pieces[0].shape[0]
    shapes = []
    specs = []
    for kind, wide, blocks in layout:
        each = wide // blocks
        if kind == "cols" and each % 128 == 0:
            shapes.append((blocks * thin, n * each))
            specs.append(pl.BlockSpec((blocks * thin, each), lambda g, order, _: (0, order[g])))
            continue
        size = (thin, wide) if kind == "rel" else (blocks * thin, each)
        shapes.append((n,) + size)
        specs.append(pl.BlockSpec((1,) + size, lambda g, order, _: (order[g], 0, 0)))
    given = () if held is None else tuple(held)
    first = 2 + len(pieces)
    return pl.pallas_call(
        functools.partial(place_kernel, layout, len(pieces)),
        grid_spec=pltpu.PrefetchScalarGridSpec(
            num_scalar_prefetch=2,
            grid=(len(pieces),),
            in_specs=[
                pl.BlockSpec(p.shape, lambda g, *_: (0, 0), pipeline_mode=pl.Buffered(1))
                for p in pieces
            ]
            + [pl.BlockSpec(memory_space=pl.ANY)] * len(given),
            out_specs=specs,
        ),
        out_shape=tuple(jax.ShapeDtypeStruct(shape, F32) for shape in shapes),
        input_output_aliases={first + k: k for k in range(len(given))},
        cost_estimate=takes(len(pieces)),
        compiler_params=pltpu.CompilerParams(vmem_limit_bytes=48 << 20),
        name="place",
    )(order, rel, *pieces, *given)


def flat_matrices(placed, layout):
    results = []
    for (kind, _, _), out in zip(layout, placed):
        if len(out.shape) == 3 and kind == "cols":
            out = out.transpose(1, 0, 2).reshape(out.shape[1], -1)
        elif len(out.shape) == 3:
            out = out.reshape(-1, out.shape[2])
        results.append(out)
    return results


class Ring:
    def __init__(self, axis):
        self.axis = axis
        self.n = n = lax.axis_size(axis)
        me = lax.axis_index(axis)
        self.pos = jnp.where(me % 2 == 0, me // 2, n - 1 - me // 2)
        order = list(range(0, n, 2)) + list(range(1, n, 2))[::-1]
        self.up = [(order[i], order[(i + 1) % n]) for i in range(n)]
        self.down = [(b, a) for a, b in self.up]
        self.walk = [0]
        for step in range(1, n // 2):
            self.walk += [-step, step]
        self.walk.append(n // 2)
        p = (self.pos + jnp.asarray(self.walk, jnp.int32) + n) % n
        self.order = jnp.where(p < n // 2, 2 * p, 2 * (n - 1 - p) + 1)

    def shard(self, distance):
        n = self.n
        p = (self.pos + distance + n) % n
        return jnp.where(p < n // 2, 2 * p, 2 * (n - 1 - p) + 1)

    def send_up(self, value):
        return lax.ppermute(value, self.axis, self.up)

    def send_down(self, value):
        return lax.ppermute(value, self.axis, self.down)

    def gather(self, value):
        half = value.shape[0] // 2
        above = below = value
        out = [value]
        for _ in range(1, self.n // 2):
            below, above = yield self.send_up(below), self.send_down(above)
            out += [below, above]
        return out + list((yield self.send_up(below[:half]), self.send_down(above[half:])))

    def reduce(self, *values):
        rows = values[0].shape[0] // self.n
        half = rows // 2
        mid = self.n // 2

        def term(distance, first=0, count=rows):
            at = self.shard(distance) * rows + first
            parts = [lax.dynamic_slice_in_dim(v, at, count, 0).astype(F32) for v in values]
            return parts[0] if len(parts) == 1 else jnp.concatenate(parts, axis=1)

        up = self.send_up(term(mid, 0, half).astype(BF16))
        down = self.send_down(term(mid, half, rows - half).astype(BF16))
        for step in range(mid - 1, 0, -1):
            up, down = yield up, down
            mine = term(step)
            other = term(-step)
            if step == mid - 1:
                mine = jnp.concatenate([mine[:half] + up.astype(F32), mine[half:]], axis=0)
                other = jnp.concatenate([other[:half], other[half:] + down.astype(F32)], axis=0)
            else:
                mine = mine + up.astype(F32)
                other = other + down.astype(F32)
            up = self.send_up(mine.astype(BF16))
            down = self.send_down(other.astype(BF16))
        up, down = yield up, down
        return (term(0) + up.astype(F32) + down.astype(F32)).astype(BF16)


class Walk:
    def __init__(self, steps):
        self.steps = steps
        self.result = None
        self.moving = next(steps)

    def go(self, arrived):
        try:
            self.moving = self.steps.send(arrived)
        except StopIteration as end:
            self.moving = None
            self.result = end.value


def milestone(*values):
    return lax.optimization_barrier(values)


def bits(n):
    return [1 << b for b in range(n.bit_length() - 1)]


def swap(value, axis, bit):
    n = lax.axis_size(axis)
    return lax.ppermute(value, axis, [(i, i ^ bit) for i in range(n)])


def reach(n):
    masks = [0]
    for bit in reversed(bits(n)):
        masks = masks + [m | bit for m in masks]
    return masks


def cube_gather(value, axis):
    held = [value]
    for bit in reversed(bits(lax.axis_size(axis))):
        held = held + [swap(block, axis, bit) for block in held]
    return held


class Scatter:
    def __init__(self, tiers, axis):
        self.axis = axis
        self.left = self.top = len(tiers) - 1
        self.size = tiers[0].shape[0]
        self.terms = [[t] for t in tiers]
        self.moving = None

    def send(self):
        parts = self.terms[self.left]
        away = parts[0] if len(parts) == 1 else add_up(parts).astype(BF16)
        self.moving = swap(away, self.axis, 1 << (self.top - self.left))

    def take(self):
        for j, (lo, hi) in enumerate(tier_bounds(1 << (self.left - 1))):
            self.terms[j].append(self.moving[lo * self.size : hi * self.size])
        self.left -= 1


def add_up(terms):
    return functools.reduce(jnp.add, [t.astype(F32) for t in terms])


def cube_exchange(value, axis, dim):
    me = lax.axis_index(axis)
    n = lax.axis_size(axis)
    size = value.shape[dim] // n
    out = []
    for mask in reach(n):
        block = lax.dynamic_slice_in_dim(value, (me ^ mask) * size, size, dim)
        if mask:
            block = lax.ppermute(block, axis, [(i, i ^ mask) for i in range(n)])
        out.append(block)
    return out


def shards(
    tokens,
    cotangent,
    lengths,
    deal,
    ln1_gain,
    ln1_shift,
    w_qkv,
    bias_qv,
    w_out,
    bias_out,
    ln2_gain,
    ln2_shift,
    w_fc,
    bias_fc,
    w_proj,
    bias_proj,
):
    x = tokens[0]
    dy = cotangent[0]
    rows, width = x.shape
    ring = Ring("seq")
    n_seq = ring.n
    n_fsdp = lax.axis_size("fsdp")
    me_seq = lax.axis_index("seq")
    me_fsdp = lax.axis_index("fsdp")
    total_rows = rows * n_seq
    heads = H // n_seq
    hd = heads * HEAD
    wide = w_fc.shape[1]
    share = w_qkv.shape[0]
    groups = jnp.arange(n_fsdp, dtype=jnp.int32)
    picked = (deal[:, None] == groups[None, :]).astype(jnp.int32)
    home_rows = jnp.sum(picked[:, :, None] * lengths[None], axis=1)
    row = jnp.sum(jnp.where((groups == me_fsdp)[:, None], home_rows, 0), axis=0)
    last = lengths.shape[1] - 1
    masks = reach(n_fsdp)
    rel = me_fsdp ^ jnp.asarray(masks, jnp.int32)

    own_cols = lax.dynamic_slice_in_dim(w_qkv, me_seq * 3 * hd, 3 * hd, 1)
    small = (ln1_gain, ln1_shift, bias_qv, bias_out, ln2_gain, ln2_shift, bias_proj)
    small = jnp.concatenate(small)
    extra = -(-small.shape[0] // (3 * hd * 16)) * 16
    tail = jnp.pad(small, (0, extra * 3 * hd - small.shape[0])).reshape(extra, 3 * hd)

    walk = Walk(ring.gather(x))
    moved, mine, w_out = milestone(walk.moving, (own_cols, tail), w_out)
    walk.go(moved)
    wout = lax.all_gather(w_out, "fsdp", axis=0, tiled=True)
    packs = [jnp.concatenate(mine, axis=0)]
    held = None
    for bit in reversed(bits(n_fsdp)):
        packs = packs + [swap(p, "fsdp", bit) for p in packs]

    def projected(blocks):
        nonlocal held
        for k in blocks:
            if k < n_seq - 1:
                at = ring.shard(ring.walk[k])
            else:
                at = ring.shard(n_seq // 2) * 2 + (k - n_seq + 1)
            held = project(
                at, pieces[k], gain_one, shift_one, w_roles, b_own, total_rows, held
            )

    moved_first = moved
    moved, packs, w_fc = milestone(walk.moving, packs, w_fc)
    walk.go(moved)
    wfc = lax.all_gather(w_fc, "fsdp", axis=0, tiled=True)

    w_own = jnp.zeros((width, 3 * hd), BF16)
    vectors = jnp.zeros((n_fsdp, tail.size), BF16)
    for k, p in enumerate(packs):
        index = me_fsdp ^ masks[k]
        w_own = lax.dynamic_update_slice_in_dim(w_own, p[:share], index * share, 0)
        vectors = lax.dynamic_update_slice_in_dim(vectors, p[share:].reshape(1, -1), index, 0)
    w_roles = w_own.reshape(width, heads, 3, HEAD).transpose(0, 2, 1, 3).reshape(width, 3 * hd)
    cut = []
    at = 0
    for count in (share, share, 2 * share, share, share, share, share):
        cut.append(vectors[:, at : at + count].reshape(1, -1).astype(F32))
        at += count
    gain_one, shift_one, bqv, bout, gain_two, shift_two, bproj = cut
    b_own = lax.dynamic_index_in_dim(bqv.reshape(n_seq, heads, 2, HEAD), me_seq, 0, keepdims=False)
    b_own = jnp.concatenate(
        [b_own[:, 0].reshape(1, hd), jnp.zeros((1, hd), F32), b_own[:, 1].reshape(1, hd)], axis=1
    )

    pieces = [x] + list(moved_first) + list(moved)
    done = 0
    while walk.result is None:
        ready = len(pieces)
        projected(range(done, ready))
        done = ready
        moved, held = milestone(walk.moving, held)
        walk.go(moved)
        pieces += list(moved)
    projected(range(done, len(pieces)))
    x_all, qkv = held

    attended, lse = attention_forward(row, qkv, rows)
    dy_first, attended = milestone(dy, attended)
    dy_pieces = cube_gather(dy_first, "fsdp")
    merged = lax.all_to_all(
        attended.reshape(n_seq, rows, hd), "seq", split_axis=0, concat_axis=0, tiled=True
    )
    merged, dy_pieces = milestone(merged, dy_pieces)

    ends = jnp.sum(home_rows[:, :last], axis=1)
    ends = jnp.sum(jnp.where(rel[:, None] == groups[None, :], ends[None, :], 0), axis=1)
    counts = jnp.clip(ends - me_seq * rows, 0, rows)
    low, middle, square_attn = attend_out(
        counts, merged, x, wout, bout, gain_two, shift_two
    )
    low_pieces = cube_gather(low, "fsdp")
    tiers = len(tier_bounds(n_fsdp))
    results = feed(
        rel, counts, low_pieces, dy_pieces, wfc, w_proj, bias_fc.astype(F32)[None]
    )
    d_two, (hidden, d_inner, d_mlp) = results[:tiers], results[tiers:]

    d_two = Scatter(d_two, "fsdp")
    while d_two.left > 1:
        d_two.send()
        d_two.moving, hidden = milestone(d_two.moving, hidden)
        d_two.take()
    d_two.send()
    results = feed_grads(hidden, d_inner, d_mlp, w_proj, low_pieces, n_seq)
    d_two.moving, results = milestone(d_two.moving, results)
    d_two.take()
    mlp, (gproj, gfc, gbfc) = results[:tiers], results[tiers:]
    gout, d_middle, d_merged, sums_two, w_qkv = middle_back(
        n_fsdp, counts, merged, middle, dy, gain_two, wout, w_qkv, d_two.terms[0]
    )
    w_all = lax.all_gather(w_qkv, "fsdp", axis=0, tiled=True)

    thin = share // n_seq
    blocks = wide // width
    gfc = gfc.reshape(n_seq * n_fsdp * thin, wide // n_fsdp)
    gout = gout.reshape(n_seq * n_fsdp * thin, width)
    d_merged, gproj, gfc, gout, mlp = milestone(d_merged, gproj, gfc, gout, mlp)
    d_heads = lax.all_to_all(d_merged, "seq", split_axis=0, concat_axis=0, tiled=True)
    together = gfc.shape[0] == gproj.shape[0]
    walk = Walk(ring.reduce(gproj, gfc, gout) if together else ring.reduce(gfc, gout))
    mlp = Scatter(mlp, "fsdp")
    while mlp.left > 1:
        mlp.send()
        mlp.moving, d_heads = milestone(mlp.moving, d_heads)
        mlp.take()
    mlp.send()
    moved, d_heads = milestone(walk.moving, d_heads)

    d_own = ()
    for h in range(heads):
        walk.go(moved)
        d_own = (
            attention_backward(
                row, qkv, attended, lse, d_heads.reshape(total_rows, hd), rows, h, d_own
            ),
        )
        moved, d_own, mlp.moving = milestone(walk.moving, d_own, mlp.moving)
    mlp.take()
    d_own = d_own[0]
    d_packed = lax.all_to_all(
        d_own.reshape(n_seq, rows, 3 * hd), "seq", split_axis=0, concat_axis=0, tiled=True
    )
    walk.go(moved)
    grad_qkv, sums_one, d_sums = qkv_grads(x_all, d_own, w_own, gain_one, shift_one, rows)
    while walk.result is None:
        moved, grad_qkv = milestone(walk.moving, grad_qkv)
        walk.go(moved)
    mine = walk.result
    if together:
        mine_proj, mine = mine[:, :width], mine[:, width:]
    else:
        walk = Walk(ring.reduce(gproj))
        while walk.result is None:
            walk.go(walk.moving)
        mine_proj = walk.result
    mine_proj = mine_proj.reshape(blocks, thin, width).transpose(1, 0, 2).reshape(thin, wide)
    mine = cube_exchange(mine, "fsdp", 0)
    parts = [
        lax.dynamic_slice_in_dim(grad_qkv, (me_fsdp ^ mask) * share, share, 0) for mask in masks
    ]
    parts = [jnp.concatenate(parts[lo:hi], axis=0) for lo, hi in tier_bounds(n_fsdp)]
    parts = Scatter(parts, "fsdp")
    while parts.left:
        parts.send()
        if parts.left > 1:
            parts.moving, mine = milestone(parts.moving, mine)
        parts.take()
    mine_fc = [m[:, : wide // n_fsdp] for m in mine]
    mine_out = add_up([m[:, wide // n_fsdp :] for m in mine]).astype(BF16)
    share_qkv = add_up(parts.terms[0]).astype(BF16)
    beside = share_qkv.reshape(n_seq, thin, 3 * hd).transpose(1, 0, 2).reshape(thin, -1)
    mine = jnp.concatenate([mine_proj] + mine_fc + [mine_out, beside], axis=1)

    mine, d_packed = milestone(mine, d_packed)
    walk = Walk(ring.gather(mine))
    output, square_ends = finish(counts, middle, bproj, mlp.terms[0])
    grad_bfc = lax.dynamic_update_slice_in_dim(
        jnp.zeros((n_fsdp, wide // n_fsdp), F32), gbfc, me_fsdp, 0
    )
    d_sums = d_sums.reshape(heads, 3, HEAD)
    d_sums = jnp.stack([d_sums[:, 0], d_sums[:, 2]], axis=1).reshape(1, 2 * hd)
    grad_bqv = lax.dynamic_update_slice_in_dim(
        jnp.zeros((n_seq, 2 * hd), F32), d_sums, me_seq, 0
    )
    squares = jnp.concatenate([square_ends[:1], square_attn, square_ends[1:]], axis=0)
    sums = jnp.concatenate(
        [
            sums_two.reshape(-1),
            grad_bfc.reshape(-1),
            jnp.sum(squares, axis=1),
            counts[:1].astype(F32),
            sums_one.reshape(-1),
            grad_bqv.reshape(-1),
        ]
    )
    hops = [(axis, bit) for axis in ("fsdp", "seq") for bit in bits(lax.axis_size(axis))]
    input_grad = None
    arrived = [mine]
    layout = (
        ("rows", wide, blocks),
        ("rel", wide, n_fsdp),
        ("rows", width, 1),
        ("cols", 3 * width, n_seq),
    )
    placed = None
    for step in range(n_seq // 2):
        count = -(-len(hops) // (n_seq // 2 - step))
        for axis, bit in hops[:count]:
            sums = sums + swap(sums, axis, bit)
        hops = hops[count:]
        if step == min(1, n_seq // 2 - 1):
            input_grad = input_gradient(d_packed, w_all, x, gain_one, d_middle)
        if step == n_seq // 2 - 1:
            placed = place(ring.order[: n_seq - 1], rel, arrived, layout, n_seq)
        moved, sums, output, input_grad, placed = milestone(
            walk.moving, sums, output, input_grad, placed
        )
        arrived += moved
        walk.go(moved)
    last_piece = [jnp.concatenate(walk.result[-2:], axis=0)]
    placed = place(ring.order[n_seq - 1 :], rel, last_piece, layout, n_seq, placed)
    grad_proj, grad_fc, grad_out, grad_wqkv = flat_matrices(placed, layout)

    def own_share(vector):
        count = vector.shape[0] // n_fsdp
        return lax.dynamic_slice_in_dim(vector, me_fsdp * count, count, 0)

    early = sums[: 4 * width + wide + 4]
    late = sums[4 * width + wide + 4 :]
    sum_bout, sum_g2, sum_s2, sum_bproj = [early[k * width : (k + 1) * width] for k in range(4)]
    sum_bfc = early[4 * width : 4 * width + wide]
    squared = early[4 * width + wide :]
    stats = jnp.sqrt(squared[:3] / (squared[3] * width))
    return (
        output[None],
        input_grad[None],
        own_share(late[:width]),
        own_share(late[width : 2 * width]),
        grad_wqkv,
        own_share(late[2 * width :]),
        grad_out,
        own_share(sum_bout),
        own_share(sum_g2),
        own_share(sum_s2),
        grad_fc,
        own_share(sum_bfc),
        grad_proj,
        own_share(sum_bproj),
        stats,
    )


def solution(mesh):
    rows_split = P("fsdp", "seq", None)
    matrix = P("fsdp", None)
    vector = P("fsdp")
    params = (
        vector,
        vector,
        matrix,
        vector,
        matrix,
        vector,
        vector,
        vector,
        matrix,
        vector,
        matrix,
        vector,
    )
    return jax.shard_map(
        shards,
        mesh=mesh,
        in_specs=(rows_split, rows_split, P(), P()) + params,
        out_specs=(rows_split, rows_split) + params + (P(),),
        check_vma=False,
    )
```

```python
import functools

import jax
import jax.numpy as jnp
from jax import lax
from jax.experimental import pallas as pl
from jax.experimental.pallas import tpu as pltpu
from jax.sharding import PartitionSpec as P

H = 16
HEAD = 64
NT = (((1,), (1,)), ((), ()))
TN = (((0,), (0,)), ((), ()))
F32 = jnp.float32
BF16 = jnp.bfloat16


def seg_starts(len_ref, segs, place):
    start = jnp.zeros_like(place)
    end = jnp.int32(0)
    for k in range(segs - 1):
        end = end + len_ref[k]
        start = jnp.where(place >= end, end, start)
    return start


def head_part(block, h, heads):
    if heads == 1:
        return block
    lane = lax.broadcasted_iota(jnp.int32, block.shape, 1)
    return jnp.where((lane >= h * HEAD) & (lane < (h + 1) * HEAD), block, jnp.zeros_like(block))


def beside(block, heads):
    return jnp.concatenate([head_part(block, h, heads) for h in range(heads)], axis=0)


def diagonal(wide, heads):
    block = wide.shape[1] // heads
    parts = [
        wide[h * HEAD : (h + 1) * HEAD, h * block : (h + 1) * block] for h in range(heads)
    ]
    return jnp.concatenate(parts, axis=0)


DIRECT = 4


def visit(i, block, segs, len_ref, direct, loop):
    r0 = pl.multiple_of(i * block, block)
    place = r0 + lax.broadcasted_iota(jnp.int32, (1, block), 1)
    start = seg_starts(len_ref, segs, place)
    first = seg_starts(len_ref, segs, r0) // block
    for n in range(1, DIRECT + 1):

        @pl.when(i - first + 1 == n)
        def _():
            direct(n, r0, place, start, pl.multiple_of((i - n + 1) * block, block))

    @pl.when(i - first + 1 > DIRECT)
    def _():
        loop(r0, place, start, first)


def seen(c0, count, place, start, heads):
    key_pos = c0 + lax.broadcasted_iota(jnp.int32, (count, place.shape[1]), 0)
    ok = (key_pos >= start) & (key_pos <= place)
    return jnp.concatenate([ok] * heads, axis=1)


def forward_kernel(heads, block, segs, len_ref, qkv_ref, o_ref, lse_ref, vt_ref):
    hd = heads * HEAD
    steps = qkv_ref.shape[0] // block

    def flip(i, _):
        at = pl.multiple_of(i * block, block)
        vt_ref[:, pl.ds(at, block)] = qkv_ref[pl.ds(at, block), 2 * hd : 3 * hd].T
        return 0

    lax.fori_loop(0, steps, flip, 0)

    def queries(r0):
        return beside(qkv_ref[pl.ds(r0, block), 0:hd] * jnp.asarray(HEAD**-0.5, BF16), heads)

    def store(r0, top, total, acc):
        lse = top + jnp.log(total)
        for h in range(heads):
            lse_ref[h : h + 1, pl.ds(r0, block)] = lse[:, h * block : (h + 1) * block]
        o_ref[pl.ds(r0, block), :] = diagonal(acc / total, heads).T.astype(BF16)

    def direct(n, r0, place, start, c0):
        keys = pl.ds(c0, n * block)
        s = lax.dot_general(qkv_ref[keys, hd : 2 * hd], queries(r0), NT, preferred_element_type=F32)
        s = jnp.where(seen(c0, n * block, place, start, heads), s, -1e30)
        top = jnp.max(s, axis=0, keepdims=True)
        p = jnp.exp(s - top)
        total = jnp.sum(p, axis=0, keepdims=True)
        acc = jnp.dot(vt_ref[:, keys], p.astype(BF16), preferred_element_type=F32)
        store(r0, top, total, acc)

    def loop(r0, place, start, first):
        q = queries(r0)

        def key_step(j, carry):
            top, total, acc = carry
            c0 = pl.multiple_of(j * block, block)
            keys = pl.ds(c0, block)
            s = lax.dot_general(qkv_ref[keys, hd : 2 * hd], q, NT, preferred_element_type=F32)
            s = jnp.where(seen(c0, block, place, start, heads), s, -1e30)
            new = jnp.maximum(top, jnp.max(s, axis=0, keepdims=True))
            p = jnp.exp(s - new)
            shrink = jnp.exp(top - new)
            total = total * shrink + jnp.sum(p, axis=0, keepdims=True)
            acc = acc * shrink + jnp.dot(
                vt_ref[:, keys], p.astype(BF16), preferred_element_type=F32
            )
            return new, total, acc

        wide = heads * block
        init = (
            jnp.full((1, wide), -1e30, F32),
            jnp.zeros((1, wide), F32),
            jnp.zeros((hd, wide), F32),
        )
        store(r0, *lax.fori_loop(first, r0 // block + 1, key_step, init))

    def query_step(i, _):
        visit(i, block, segs, len_ref, direct, loop)
        return 0

    lax.fori_loop(0, steps, query_step, 0)


def backward_kernel(
    heads,
    block,
    segs,
    len_ref,
    qkv_ref,
    o_ref,
    lse_ref,
    do_ref,
    d_ref,
    kt_ref,
    dq_ref,
    dk_ref,
    dv_ref,
):
    hd = heads * HEAD
    steps = qkv_ref.shape[0] // block

    def flip(i, _):
        at = pl.multiple_of(i * block, block)
        kt_ref[:, pl.ds(at, block)] = qkv_ref[pl.ds(at, block), hd : 2 * hd].T
        dk_ref[pl.ds(at, block), :] = jnp.zeros((block, hd), F32)
        dv_ref[pl.ds(at, block), :] = jnp.zeros((block, hd), F32)
        return 0

    lax.fori_loop(0, steps, flip, 0)

    def operands(r0):
        rows = pl.ds(r0, block)
        q = beside(qkv_ref[rows, 0:hd] * jnp.asarray(HEAD**-0.5, BF16), heads)
        do = do_ref[rows, :]
        both = (do.astype(F32) * o_ref[rows, :].astype(F32)).T
        delta = [
            jnp.sum(both[h * HEAD : (h + 1) * HEAD], axis=0, keepdims=True) for h in range(heads)
        ]
        lse = [lse_ref[h : h + 1, rows] for h in range(heads)]
        return q, beside(do, heads), jnp.concatenate(delta, axis=1), jnp.concatenate(lse, axis=1)

    def part(c0, count, place, start, q, do, delta, lse):
        keys = pl.ds(c0, count)
        s = lax.dot_general(qkv_ref[keys, hd : 2 * hd], q, NT, preferred_element_type=F32)
        p = jnp.where(seen(c0, count, place, start, heads), jnp.exp(s - lse), 0.0)
        dp = lax.dot_general(
            qkv_ref[keys, 2 * hd : 3 * hd], do, NT, preferred_element_type=F32
        )
        ds = (p * (dp - delta)).astype(BF16)
        dv_ref[keys, :] += jnp.dot(p.astype(BF16), do, preferred_element_type=F32)
        dk_ref[keys, :] += jnp.dot(ds, q, preferred_element_type=F32)
        return jnp.dot(kt_ref[:, keys], ds, preferred_element_type=F32)

    def store(r0, dq):
        dq_ref[pl.ds(r0, block), :] = (diagonal(dq, heads) * HEAD**-0.5).T

    def direct(n, r0, place, start, c0):
        store(r0, part(c0, n * block, place, start, *operands(r0)))

    def loop(r0, place, start, first):
        given = operands(r0)

        def key_step(j, dq):
            return dq + part(pl.multiple_of(j * block, block), block, place, start, *given)

        init = jnp.zeros((hd, heads * block), F32)
        store(r0, lax.fori_loop(first, r0 // block + 1, key_step, init))

    def query_step(i, _):
        visit(i, block, segs, len_ref, direct, loop)
        return 0

    lax.fori_loop(0, steps, query_step, 0)

    def finish_rows(i, _):
        rows = pl.ds(pl.multiple_of(i * block, block), block)
        roles = [ref[rows, :] for ref in (dq_ref, dk_ref, dv_ref)]
        parts = [v[:, h * HEAD : (h + 1) * HEAD] for h in range(heads) for v in roles]
        d_ref[rows, :] = jnp.concatenate(parts, axis=1).astype(BF16)
        return 0

    lax.fori_loop(0, steps, finish_rows, 0)


def takes(us):
    return pl.CostEstimate(flops=int(us * 3.30e9), bytes_accessed=1 << 20, transcendentals=0)


VM = pl.BlockSpec(memory_space=pltpu.VMEM)
SM = pl.BlockSpec(memory_space=pltpu.SMEM)
LIMIT = 32 << 20


def attention_forward(row, qkv, block):
    rows, wide = qkv.shape
    hd = wide // 3
    heads = hd // HEAD
    return pl.pallas_call(
        functools.partial(forward_kernel, heads, block, row.shape[0]),
        out_shape=(
            jax.ShapeDtypeStruct((rows, hd), BF16),
            jax.ShapeDtypeStruct((heads, rows), F32),
        ),
        in_specs=[SM, VM],
        out_specs=(VM, VM),
        scratch_shapes=[pltpu.VMEM((hd, rows), BF16)],
        compiler_params=pltpu.CompilerParams(vmem_limit_bytes=LIMIT),
        cost_estimate=takes(14),
        name="attention_forward",
    )(row, qkv)


def attention_backward(row, qkv, o, lse, do, block):
    rows, wide = qkv.shape
    hd = wide // 3
    heads = hd // HEAD
    return pl.pallas_call(
        functools.partial(backward_kernel, heads, block, row.shape[0]),
        out_shape=jax.ShapeDtypeStruct((rows, wide), BF16),
        in_specs=[SM] + [VM] * 4,
        out_specs=VM,
        scratch_shapes=[pltpu.VMEM((hd, rows), BF16)] + [pltpu.VMEM((rows, hd), F32)] * 3,
        compiler_params=pltpu.CompilerParams(vmem_limit_bytes=44 << 20),
        cost_estimate=takes(21),
        name="attention_backward",
    )(row, qkv, o, lse, do)


def tier_bounds(n):
    bounds = [(0, 1)]
    while bounds[-1][1] < n:
        bounds.append((bounds[-1][1], 2 * bounds[-1][1]))
    return bounds


def norm_parts(value):
    mean = jnp.mean(value, axis=-1, keepdims=True)
    centred = value - mean
    spread = jnp.mean(centred * centred, axis=-1, keepdims=True)
    scale = lax.rsqrt(spread + 1e-05)
    return centred * scale, scale


def project_kernel(at_ref, x_ref, gain_ref, shift_ref, w_ref, b_ref, *rest):
    x_out, qkv_out = rest[-2:]
    x = x_ref[...]
    n, _ = norm_parts(x.astype(F32))
    low = (n * gain_ref[...] + shift_ref[...]).astype(BF16)
    mixed = jnp.dot(low, w_ref[...], preferred_element_type=F32) + b_ref[...]
    x_out[...] = x
    qkv_out[...] = mixed.astype(BF16)


def project(at, x, gain, shift, w, b, total, held):
    rows, width = x.shape
    wide = w.shape[1]

    def fixed(shape):
        return pl.BlockSpec(shape, lambda i, at: (0, 0))

    given = () if held is None else held
    return pl.pallas_call(
        project_kernel,
        grid_spec=pltpu.PrefetchScalarGridSpec(
            num_scalar_prefetch=1,
            grid=(1,),
            in_specs=[
                fixed((rows, width)),
                fixed((1, width)),
                fixed((1, width)),
                fixed((width, wide)),
                fixed((1, wide)),
            ]
            + [pl.BlockSpec(memory_space=pl.ANY)] * len(given),
            out_specs=[
                pl.BlockSpec((rows, width), lambda i, at: (at[0], 0)),
                pl.BlockSpec((rows, wide), lambda i, at: (at[0], 0)),
            ],
        ),
        out_shape=(
            jax.ShapeDtypeStruct((total, width), BF16),
            jax.ShapeDtypeStruct((total, wide), BF16),
        ),
        input_output_aliases={6: 0, 7: 1} if given else {},
        cost_estimate=takes(2),
        compiler_params=pltpu.CompilerParams(vmem_limit_bytes=24 << 20),
        name="project",
    )(at.reshape(1), x, gain, shift, w, b, *given)


def attend_out_kernel(
    count_ref,
    merged_ref,
    x_ref,
    wout_ref,
    bout_ref,
    gain_ref,
    shift_ref,
    low_ref,
    middle_ref,
    stat_ref,
):
    rows = x_ref.shape[0]
    merged = jnp.concatenate([merged_ref[k] for k in range(merged_ref.shape[0])], axis=1)
    attn = jnp.dot(merged, wout_ref[...], preferred_element_type=F32) + bout_ref[...]
    middle = x_ref[...].astype(F32) + attn
    middle_ref[...] = middle
    n, _ = norm_parts(middle)
    low_ref[...] = (n * gain_ref[...] + shift_ref[...]).astype(BF16)
    valid = lax.broadcasted_iota(jnp.int32, (rows, 1), 0) < count_ref[0]
    stat_ref[...] = jnp.sum(jnp.where(valid, attn * attn, 0.0), axis=0, keepdims=True)


def attend_out(count, merged, x, wout, bout, gain, shift):
    rows, width = x.shape
    return pl.pallas_call(
        attend_out_kernel,
        in_specs=[SM] + [VM] * 6,
        out_specs=(VM,) * 3,
        out_shape=(
            jax.ShapeDtypeStruct((rows, width), BF16),
            jax.ShapeDtypeStruct((rows, width), F32),
            jax.ShapeDtypeStruct((1, width), F32),
        ),
        cost_estimate=takes(5),
        compiler_params=pltpu.CompilerParams(vmem_limit_bytes=40 << 20),
        name="attend_out",
    )(count, merged, x, wout, bout, gain, shift)


GELU = 0.7978845608028654


def feed_kernel(
    packs, rel_ref, which_ref, count_ref, bfc_ref, wproj_ref, wfc_ref, dy_ref, *rest
):
    low_refs, rest = rest[:packs], rest[packs:]
    tiers = tier_bounds(packs)
    dtwo_refs, rest = rest[: len(tiers)], rest[len(tiers) :]
    hidden_ref, di_ref, dmlp_ref, low_s = rest
    step = pl.program_id(0)
    rows = low_s.shape[0]
    valid = lax.broadcasted_iota(jnp.int32, (rows, 1), 0) < count_ref[step]

    for k in range(packs):

        @pl.when(step == k)
        def _():
            low_s[...] = low_refs[k][...]

    dy = dy_ref[...]
    dmlp_ref[...] = jnp.where(valid, dy, jnp.zeros_like(dy))

    u = jnp.dot(low_s[...], wfc_ref[...], preferred_element_type=F32) + bfc_ref[...]
    dh = lax.dot_general(dmlp_ref[...], wproj_ref[...], NT, preferred_element_type=F32)
    square = u * u
    t = jnp.tanh(GELU * u * (1.0 + 0.044715 * square))
    side = 0.5 * (1.0 + t)
    hidden_ref[...] = (u * side).astype(BF16)
    slope = side + 0.5 * u * (1.0 - t * t) * (GELU * (1.0 + 3 * 0.044715 * square))
    di = (dh * slope).astype(BF16)
    di_ref[...] = di
    dtwo = lax.dot_general(di, wfc_ref[...], NT, preferred_element_type=F32)
    for (lo, hi), out_ref in zip(tiers, dtwo_refs):

        @pl.when((step >= lo) & (step < hi))
        def _():
            out_ref[...] = dtwo.astype(out_ref.dtype)


def feed(rel, which, counts, low_pieces, dy_all, wfc, wproj, bfc, own):
    rows, width = low_pieces[0].shape
    packs = len(low_pieces)
    wide = wproj.shape[0]
    tiers = tier_bounds(packs)

    def whole(*shape):
        return pl.BlockSpec(shape, lambda g, *_: (0,) * len(shape), pipeline_mode=pl.Buffered(1))

    def tier(lo, hi):
        return pl.BlockSpec((rows, width), lambda g, *_: (jnp.clip(g - lo, 0, hi - lo - 1), 0))

    each = pl.BlockSpec((rows, wide), lambda g, *_: (g, 0))
    return pl.pallas_call(
        functools.partial(feed_kernel, packs),
        grid_spec=pltpu.PrefetchScalarGridSpec(
            num_scalar_prefetch=3,
            grid=(packs,),
            in_specs=[
                whole(1, wide),
                whole(wide, width),
                pl.BlockSpec(
                    (width, wide), lambda g, rel, *_: (0, rel[0]), pipeline_mode=pl.Buffered(1)
                ),
                pl.BlockSpec((rows, width), lambda g, rel, which, _: (which[g], 0)),
            ]
            + [whole(rows, width)] * packs,
            out_specs=[tier(lo, hi) for lo, hi in tiers]
            + [each, each, pl.BlockSpec((rows, width), lambda g, *_: (g, 0))],
            scratch_shapes=[pltpu.VMEM((rows, width), BF16)],
        ),
        out_shape=tuple(
            [
                jax.ShapeDtypeStruct(((hi - lo) * rows, width), F32 if lo == 0 and own else BF16)
                for lo, hi in tiers
            ]
            + [jax.ShapeDtypeStruct((packs * rows, wide), BF16)] * 2
            + [jax.ShapeDtypeStruct((packs * rows, width), BF16)]
        ),
        cost_estimate=takes(10),
        compiler_params=pltpu.CompilerParams(vmem_limit_bytes=52 << 20),
        name="feed",
    )(rel, which, counts, bfc, wproj, wfc, dy_all, *low_pieces)


def feed_grads_kernel(
    near, n_fsdp, hid_a, hid_b, di_a, di_b, dmlp_a, dmlp_b, *rest
):
    low_refs, rest = rest[:n_fsdp], rest[n_fsdp:]
    gproj_ref, gfc_ref, gbfc_ref = rest[:3]
    scratch = rest[3:]
    step = pl.program_id(0)
    rows, wide = hid_a.shape
    n_seq, _, thin, _ = gfc_ref.shape
    share = n_seq * thin

    @pl.when(step == 0)
    def _():
        gbfc_ref[...] = jnp.zeros_like(gbfc_ref)

    def store_fc(i, g):
        for k in range(n_seq):
            gfc_ref[k, i] = g[k * thin : (k + 1) * thin]

    for k in range(n_fsdp):
        hid_ref, di_ref, dmlp_ref = (hid_a, di_a, dmlp_a) if k < near else (hid_b, di_b, dmlp_b)

        @pl.when(step == k)
        def _():
            di = di_ref[...]
            gbfc_ref[...] += jnp.sum(di.astype(F32), axis=0, keepdims=True)
            if len(scratch) == 2:
                proj_s, fc_s = scratch
                proj = jnp.dot(hid_ref[...].T, dmlp_ref[...], preferred_element_type=F32)
                fc = jnp.dot(low_refs[k][...].T, di, preferred_element_type=F32)
                proj_s[...] = proj if k == 0 else proj_s[...] + proj
                fc_s[...] = fc if k == 0 else fc_s[...] + fc
            else:
                hiddent_s, di_s, dmlp_s, lowt_s = scratch
                at = slice(k * rows, (k + 1) * rows)
                hiddent_s[:, at] = hid_ref[...].T
                di_s[at, :] = di
                dmlp_s[at, :] = dmlp_ref[...]
                lowt_s[:, at] = low_refs[k][...].T

    @pl.when(step == n_fsdp - 1)
    def _():
        if len(scratch) == 2:
            proj_s, fc_s = scratch
            gproj_ref[...] = proj_s[...].astype(BF16)
            for i in range(n_fsdp):
                store_fc(i, fc_s[i * share : (i + 1) * share, :].astype(BF16))
            return
        hiddent_s, di_s, dmlp_s, lowt_s = scratch
        tile = min(256, wide)

        def proj_tile(i, _):
            at = pl.multiple_of(i * tile, tile)
            g = jnp.dot(hiddent_s[pl.ds(at, tile), :], dmlp_s[...], preferred_element_type=F32)
            gproj_ref[pl.ds(at, tile), :] = g.astype(BF16)
            return 0

        lax.fori_loop(0, wide // tile, proj_tile, 0)

        def fc_tile(i, _):
            at = pl.multiple_of(i * share, share)
            g = jnp.dot(lowt_s[pl.ds(at, share), :], di_s[...], preferred_element_type=F32)
            store_fc(i, g.astype(BF16))
            return 0

        lax.fori_loop(0, n_fsdp, fc_tile, 0)


def feed_grads(near, far, low_pieces, n_seq):
    rows, width = low_pieces[0].shape
    n_fsdp = len(low_pieces)
    wide = near[0].shape[1]
    total = n_fsdp * rows
    count = near[0].shape[0] // rows
    thin = width // n_fsdp // n_seq
    if total > 2048:
        scratch = [pltpu.VMEM((wide, width), F32), pltpu.VMEM((width, wide), F32)]
    else:
        scratch = [pltpu.VMEM((wide, total), BF16), pltpu.VMEM((total, wide), BF16)]
        scratch += [pltpu.VMEM((total, width), BF16), pltpu.VMEM((width, total), BF16)]

    def whole(*shape):
        return pl.BlockSpec(shape, lambda g: (0,) * len(shape), pipeline_mode=pl.Buffered(1))

    def last(*shape):
        return pl.BlockSpec(shape, lambda g: (0,) * len(shape))

    def of_near(columns):
        return pl.BlockSpec((rows, columns), lambda g: (jnp.minimum(g, count - 1), 0))

    def of_far(columns):
        return pl.BlockSpec((rows, columns), lambda g: (jnp.maximum(g - count, 0), 0))

    pairs = [(of_near(wide), of_far(wide))] * 2 + [(of_near(width), of_far(width))]
    return pl.pallas_call(
        functools.partial(feed_grads_kernel, count, n_fsdp),
        grid=(n_fsdp,),
        in_specs=[spec for pair in pairs for spec in pair] + [whole(rows, width)] * n_fsdp,
        out_specs=[last(wide, width), last(n_seq, n_fsdp, thin, wide), last(1, wide)],
        out_shape=(
            jax.ShapeDtypeStruct((wide, width), BF16),
            jax.ShapeDtypeStruct((n_seq, n_fsdp, thin, wide), BF16),
            jax.ShapeDtypeStruct((1, wide), F32),
        ),
        scratch_shapes=scratch,
        cost_estimate=takes(15),
        compiler_params=pltpu.CompilerParams(vmem_limit_bytes=48 << 20),
        name="feed_grads",
    )(near[0], far[0], near[1], far[1], near[2], far[2], *low_pieces)


def feed_out_kernel(packs, hidden_ref, wproj_ref, *mlp_refs):
    step = pl.program_id(0)
    mlp = jnp.dot(hidden_ref[...], wproj_ref[...], preferred_element_type=F32)
    for (lo, hi), out_ref in zip(tier_bounds(packs), mlp_refs):

        @pl.when((step >= lo) & (step < hi))
        def _():
            out_ref[...] = mlp.astype(out_ref.dtype)


def feed_out(hidden, wproj, rows, own):
    wide, width = wproj.shape
    packs = hidden.shape[0] // rows
    tiers = tier_bounds(packs)

    def tier(lo, hi):
        return pl.BlockSpec((rows, width), lambda g: (jnp.clip(g - lo, 0, hi - lo - 1), 0))

    return pl.pallas_call(
        functools.partial(feed_out_kernel, packs),
        grid=(packs,),
        in_specs=[
            pl.BlockSpec((rows, wide), lambda g: (g, 0)),
            pl.BlockSpec((wide, width), lambda g: (0, 0), pipeline_mode=pl.Buffered(1)),
        ],
        out_specs=[tier(lo, hi) for lo, hi in tiers],
        out_shape=tuple(
            jax.ShapeDtypeStruct(((hi - lo) * rows, width), F32 if lo == 0 and own else BF16)
            for lo, hi in tiers
        ),
        cost_estimate=takes(0.3),
        compiler_params=pltpu.CompilerParams(vmem_limit_bytes=20 << 20),
        name="feed_out",
    )(hidden, wproj)


def middle_back_kernel(
    n_fsdp,
    terms,
    rel_ref,
    count_ref,
    merged_ref,
    middle_ref,
    dy_ref,
    gain_ref,
    wout_ref,
    *rest,
):
    tiers = tier_bounds(n_fsdp)
    term_refs, rest = rest[:terms], rest[terms:]
    gout_refs, rest = rest[: len(tiers)], rest[len(tiers) :]
    d_middle_ref, d_merged_ref, vec_ref, flip_s, order_s = rest
    n_seq, rows, hd = merged_ref.shape
    share = flip_s.shape[0] // n_fsdp
    valid = lax.broadcasted_iota(jnp.int32, (rows, 1), 0) < count_ref[0]
    n, scale = norm_parts(middle_ref[...])
    d_two = functools.reduce(jnp.add, [ref[...].astype(F32) for ref in term_refs])
    d_result = jnp.where(valid, dy_ref[...].astype(F32), 0.0)
    e = d_two * gain_ref[...]
    d_middle = d_result + scale * (
        e - jnp.mean(e, axis=-1, keepdims=True) - n * jnp.mean(e * n, axis=-1, keepdims=True)
    )
    d_middle_ref[...] = d_middle
    d_attn = d_middle.astype(BF16)
    d_merged = lax.dot_general(d_attn, wout_ref[...], NT, preferred_element_type=F32).astype(BF16)
    for k in range(n_seq):
        d_merged_ref[k] = d_merged[:, k * hd : (k + 1) * hd]
    vec_ref[0:1, :] = jnp.sum(d_attn.astype(F32), axis=0, keepdims=True)
    vec_ref[1:2, :] = jnp.sum(d_two * n, axis=0, keepdims=True)
    vec_ref[2:3, :] = jnp.sum(d_two, axis=0, keepdims=True)
    vec_ref[3:4, :] = jnp.sum(d_result, axis=0, keepdims=True)
    merged = jnp.concatenate([merged_ref[k] for k in range(n_seq)], axis=1)
    flip_s[...] = merged.T
    for k in range(n_fsdp):
        at = pl.multiple_of(rel_ref[k] * share, share)
        order_s[k * share : (k + 1) * share, :] = flip_s[pl.ds(at, share), :]
    gout = jnp.dot(order_s[...], d_attn, preferred_element_type=F32).astype(BF16)
    for (lo, hi), out_ref in zip(tiers, gout_refs):
        out_ref[...] = gout[lo * share : hi * share]


def middle_back(rel, count, merged, middle, dy, gain, wout, terms):
    rows, width = middle.shape
    n_fsdp = rel.shape[0]
    share = width // n_fsdp
    tiers = tier_bounds(n_fsdp)
    return pl.pallas_call(
        functools.partial(middle_back_kernel, n_fsdp, len(terms)),
        in_specs=[SM] * 2 + [VM] * (5 + len(terms)),
        out_specs=(VM,) * (len(tiers) + 3),
        out_shape=tuple(
            [jax.ShapeDtypeStruct(((hi - lo) * share, width), BF16) for lo, hi in tiers]
            + [
                jax.ShapeDtypeStruct((rows, width), F32),
                jax.ShapeDtypeStruct(merged.shape, BF16),
                jax.ShapeDtypeStruct((4, width), F32),
            ]
        ),
        scratch_shapes=[pltpu.VMEM((width, rows), BF16)] * 2,
        cost_estimate=takes(7),
        compiler_params=pltpu.CompilerParams(vmem_limit_bytes=36 << 20),
        name="middle_back",
    )(rel, count, merged, middle, dy, gain, wout, *terms)


def finish_kernel(count_ref, middle_ref, bproj_ref, *rest):
    term_refs, output_ref, stat_ref = rest[:-2], rest[-2], rest[-1]
    rows = middle_ref.shape[0]
    valid = lax.broadcasted_iota(jnp.int32, (rows, 1), 0) < count_ref[0]
    branch = functools.reduce(jnp.add, [ref[...].astype(F32) for ref in term_refs])
    branch = branch + bproj_ref[...]
    result = middle_ref[...] + branch
    output_ref[...] = jnp.where(valid, result, 0.0).astype(BF16)
    stat_ref[0:1, :] = jnp.sum(jnp.where(valid, result * result, 0.0), axis=0, keepdims=True)
    stat_ref[1:2, :] = jnp.sum(jnp.where(valid, branch * branch, 0.0), axis=0, keepdims=True)


def finish(count, middle, bproj, terms):
    rows, width = middle.shape
    return pl.pallas_call(
        finish_kernel,
        in_specs=[SM] + [VM] * (2 + len(terms)),
        out_specs=(VM,) * 2,
        out_shape=(
            jax.ShapeDtypeStruct((rows, width), BF16),
            jax.ShapeDtypeStruct((2, width), F32),
        ),
        cost_estimate=takes(3),
        compiler_params=pltpu.CompilerParams(vmem_limit_bytes=32 << 20),
        name="finish",
    )(count, middle, bproj, *terms)


def qkv_grad_kernel(x_ref, d_ref, w_ref, gain_ref, shift_ref, g_ref, vec_ref, sum_ref, acc):
    step = pl.program_id(0)
    n, _ = norm_parts(x_ref[...].astype(F32))
    low = (n * gain_ref[...] + shift_ref[...]).astype(BF16)
    d = d_ref[...]
    part = lax.dot_general(d, w_ref[...], NT, preferred_element_type=F32)
    gain_part = jnp.sum(part * n, axis=0, keepdims=True)
    shift_part = jnp.sum(part, axis=0, keepdims=True)
    sum_part = jnp.sum(d.astype(F32), axis=0, keepdims=True)
    g = jnp.dot(low.T, d, preferred_element_type=F32)

    @pl.when(step == 0)
    def _():
        acc[...] = g
        vec_ref[0:1, :] = gain_part
        vec_ref[1:2, :] = shift_part
        sum_ref[...] = sum_part

    @pl.when(step > 0)
    def _():
        acc[...] += g
        vec_ref[0:1, :] += gain_part
        vec_ref[1:2, :] += shift_part
        sum_ref[...] += sum_part

    @pl.when(step == pl.num_programs(0) - 1)
    def _():
        g_ref[...] = acc[...].astype(BF16)


def qkv_grads(x_all, d_own, w_own, gain, shift, block):
    total, width = x_all.shape
    wide = w_own.shape[1]

    def whole(*shape):
        return pl.BlockSpec(shape, lambda g: (0,) * len(shape))

    return pl.pallas_call(
        qkv_grad_kernel,
        grid=(total // block,),
        in_specs=[
            pl.BlockSpec((block, width), lambda g: (g, 0)),
            pl.BlockSpec((block, wide), lambda g: (g, 0)),
            whole(width, wide),
            whole(1, width),
            whole(1, width),
        ],
        out_specs=[whole(width, wide), whole(2, width), whole(1, wide)],
        out_shape=(
            jax.ShapeDtypeStruct((width, wide), BF16),
            jax.ShapeDtypeStruct((2, width), F32),
            jax.ShapeDtypeStruct((1, wide), F32),
        ),
        scratch_shapes=[pltpu.VMEM((width, wide), F32)],
        cost_estimate=takes(13),
        compiler_params=pltpu.CompilerParams(vmem_limit_bytes=40 << 20),
        name="qkv_grads",
    )(x_all, d_own, w_own, gain, shift)


def input_grad_kernel(d_ref, x_ref, gain_ref, d_middle_ref, w_ref, out_ref, d_s, one_s):
    step = pl.program_id(0)
    steps, _, share = one_s.shape

    @pl.when(step == 0)
    def _():
        d_s[...] = jnp.concatenate([d_ref[k] for k in range(d_ref.shape[0])], axis=1)

    one_s[step] = lax.dot_general(d_s[...], w_ref[...], NT, preferred_element_type=F32)

    @pl.when(step == steps - 1)
    def _():
        n, scale = norm_parts(x_ref[...].astype(F32))
        d_one = jnp.concatenate([one_s[k] for k in range(steps)], axis=1)
        e = d_one * gain_ref[...]
        out_ref[...] = d_middle_ref[...] + scale * (
            e - jnp.mean(e, axis=-1, keepdims=True) - n * jnp.mean(e * n, axis=-1, keepdims=True)
        )


def input_gradient(d_packed, w_all, x, gain, d_middle):
    rows, width = x.shape
    n_seq, _, each = d_packed.shape
    wide = w_all.shape[1]
    steps = 4

    def whole(*shape):
        return pl.BlockSpec(shape, lambda g: (0,) * len(shape), pipeline_mode=pl.Buffered(1))

    return pl.pallas_call(
        input_grad_kernel,
        grid=(steps,),
        in_specs=[
            whole(n_seq, rows, each),
            whole(rows, width),
            whole(1, width),
            whole(rows, width),
            pl.BlockSpec((width // steps, wide), lambda g: (g, 0)),
        ],
        out_specs=whole(rows, width),
        out_shape=jax.ShapeDtypeStruct((rows, width), F32),
        scratch_shapes=[
            pltpu.VMEM((rows, wide), BF16),
            pltpu.VMEM((steps, rows, width // steps), F32),
        ],
        cost_estimate=takes(8),
        compiler_params=pltpu.CompilerParams(vmem_limit_bytes=32 << 20),
        name="input_gradient",
    )(d_packed, x, gain, d_middle, w_all)


def place_kernel(layout, count, order_ref, rel_ref, *refs):
    outs = refs[len(refs) - len(layout) :]
    step = pl.program_id(0)
    for k in range(count):

        @pl.when(step == k)
        def _():
            thin = refs[k].shape[0]
            at = 0
            for (kind, wide, blocks), out in zip(layout, outs):
                each = wide // blocks
                for a in range(blocks):
                    part = refs[k][:, at : at + each].astype(F32)
                    at += each
                    if kind == "rel":
                        lanes = pl.ds(pl.multiple_of(rel_ref[a] * each, each), each)
                        out[0, :, lanes] = part
                    elif len(out.shape) == 3:
                        out[0, a * thin : (a + 1) * thin, :] = part
                    else:
                        out[a * thin : (a + 1) * thin, :] = part


def place(order, rel, pieces, layout, n, held=None):
    thin = pieces[0].shape[0]
    shapes = []
    specs = []
    for kind, wide, blocks in layout:
        each = wide // blocks
        if kind == "cols" and each % 128 == 0:
            shapes.append((blocks * thin, n * each))
            specs.append(pl.BlockSpec((blocks * thin, each), lambda g, order, _: (0, order[g])))
            continue
        size = (thin, wide) if kind == "rel" else (blocks * thin, each)
        shapes.append((n,) + size)
        specs.append(pl.BlockSpec((1,) + size, lambda g, order, _: (order[g], 0, 0)))
    given = () if held is None else tuple(held)
    first = 2 + len(pieces)
    return pl.pallas_call(
        functools.partial(place_kernel, layout, len(pieces)),
        grid_spec=pltpu.PrefetchScalarGridSpec(
            num_scalar_prefetch=2,
            grid=(len(pieces),),
            in_specs=[
                pl.BlockSpec(p.shape, lambda g, *_: (0, 0), pipeline_mode=pl.Buffered(1))
                for p in pieces
            ]
            + [pl.BlockSpec(memory_space=pl.ANY)] * len(given),
            out_specs=specs,
        ),
        out_shape=tuple(jax.ShapeDtypeStruct(shape, F32) for shape in shapes),
        input_output_aliases={first + k: k for k in range(len(given))},
        cost_estimate=takes(len(pieces)),
        compiler_params=pltpu.CompilerParams(vmem_limit_bytes=48 << 20),
        name="place",
    )(order, rel, *pieces, *given)


def flat_matrices(placed, layout):
    results = []
    for (kind, _, _), out in zip(layout, placed):
        if len(out.shape) == 3 and kind == "cols":
            out = out.transpose(1, 0, 2).reshape(out.shape[1], -1)
        elif len(out.shape) == 3:
            out = out.reshape(-1, out.shape[2])
        results.append(out)
    return results


class Ring:
    def __init__(self, axis):
        self.axis = axis
        self.n = n = lax.axis_size(axis)
        me = lax.axis_index(axis)
        self.pos = jnp.where(me % 2 == 0, me // 2, n - 1 - me // 2)
        order = list(range(0, n, 2)) + list(range(1, n, 2))[::-1]
        self.up = [(order[i], order[(i + 1) % n]) for i in range(n)]
        self.down = [(b, a) for a, b in self.up]
        self.walk = [0]
        for step in range(1, n // 2):
            self.walk += [-step, step]
        self.walk.append(n // 2)
        p = (self.pos + jnp.asarray(self.walk, jnp.int32) + n) % n
        self.order = jnp.where(p < n // 2, 2 * p, 2 * (n - 1 - p) + 1)

    def shard(self, distance):
        n = self.n
        p = (self.pos + distance + n) % n
        return jnp.where(p < n // 2, 2 * p, 2 * (n - 1 - p) + 1)

    def send_up(self, value):
        return lax.ppermute(value, self.axis, self.up)

    def send_down(self, value):
        return lax.ppermute(value, self.axis, self.down)

    def gather(self, value):
        half = value.shape[0] // 2
        above = below = value
        out = [value]
        for _ in range(1, self.n // 2):
            below, above = yield self.send_up(below), self.send_down(above)
            out += [below, above]
        return out + list((yield self.send_up(below[:half]), self.send_down(above[half:])))

    def reduce(self, *values):
        rows = values[0].shape[0] // self.n
        half = rows // 2
        mid = self.n // 2

        def term(distance, first=0, count=rows):
            at = self.shard(distance) * rows + first
            parts = [lax.dynamic_slice_in_dim(v, at, count, 0).astype(F32) for v in values]
            return parts[0] if len(parts) == 1 else jnp.concatenate(parts, axis=1)

        up = self.send_up(term(mid, 0, half).astype(BF16))
        down = self.send_down(term(mid, half, rows - half).astype(BF16))
        for step in range(mid - 1, 0, -1):
            up, down = yield up, down
            mine = term(step)
            other = term(-step)
            if step == mid - 1:
                mine = jnp.concatenate([mine[:half] + up.astype(F32), mine[half:]], axis=0)
                other = jnp.concatenate([other[:half], other[half:] + down.astype(F32)], axis=0)
            else:
                mine = mine + up.astype(F32)
                other = other + down.astype(F32)
            up = self.send_up(mine.astype(BF16))
            down = self.send_down(other.astype(BF16))
        up, down = yield up, down
        return (term(0) + up.astype(F32) + down.astype(F32)).astype(BF16)


class Walk:
    def __init__(self, steps):
        self.steps = steps
        self.result = None
        self.moving = next(steps)

    def go(self, arrived):
        try:
            self.moving = self.steps.send(arrived)
        except StopIteration as end:
            self.moving = None
            self.result = end.value


def milestone(*values):
    return lax.optimization_barrier(values)


def bits(n):
    return [1 << b for b in range(n.bit_length() - 1)]


def swap(value, axis, bit):
    n = lax.axis_size(axis)
    return lax.ppermute(value, axis, [(i, i ^ bit) for i in range(n)])


def reach(n):
    masks = [0]
    for bit in reversed(bits(n)):
        masks = masks + [m | bit for m in masks]
    return masks


def cube_gather(value, axis, n=None):
    held = [value]
    for bit in reversed(bits(n or lax.axis_size(axis))):
        held = held + [swap(block, axis, bit) for block in held]
    return held


class Scatter:
    def __init__(self, tiers, axis):
        self.axis = axis
        tiers = list(tiers)
        self.left = self.top = len(tiers) - 1
        self.size = tiers[0].shape[0]
        self.terms = [[t] for t in tiers]
        self.moving = None

    def send(self):
        parts = self.terms[self.left]
        away = parts[0] if len(parts) == 1 else add_up(parts).astype(BF16)
        self.moving = swap(away, self.axis, 1 << (self.top - self.left))

    def take(self):
        for j, (lo, hi) in enumerate(tier_bounds(1 << (self.left - 1))):
            self.terms[j].append(self.moving[lo * self.size : hi * self.size])
        self.left -= 1


def add_up(terms):
    return functools.reduce(jnp.add, [t.astype(F32) for t in terms])


def cube_exchange(value, axis, dim):
    me = lax.axis_index(axis)
    n = lax.axis_size(axis)
    size = value.shape[dim] // n
    out = []
    for mask in reach(n):
        block = lax.dynamic_slice_in_dim(value, (me ^ mask) * size, size, dim)
        if mask:
            block = lax.ppermute(block, axis, [(i, i ^ mask) for i in range(n)])
        out.append(block)
    return out


def shards(
    tokens,
    cotangent,
    lengths,
    deal,
    ln1_gain,
    ln1_shift,
    w_qkv,
    bias_qv,
    w_out,
    bias_out,
    ln2_gain,
    ln2_shift,
    w_fc,
    bias_fc,
    w_proj,
    bias_proj,
):
    x = tokens[0]
    dy = cotangent[0]
    rows, width = x.shape
    ring = Ring("seq")
    n_seq = ring.n
    n_fsdp = lax.axis_size("fsdp")
    me_seq = lax.axis_index("seq")
    me_fsdp = lax.axis_index("fsdp")
    total_rows = rows * n_seq
    heads = H // n_seq
    hd = heads * HEAD
    wide = w_fc.shape[1]
    share = w_qkv.shape[0]
    groups = jnp.arange(n_fsdp, dtype=jnp.int32)
    picked = (deal[:, None] == groups[None, :]).astype(jnp.int32)
    home_rows = jnp.sum(picked[:, :, None] * lengths[None], axis=1)
    row = jnp.sum(jnp.where((groups == me_fsdp)[:, None], home_rows, 0), axis=0)
    last = lengths.shape[1] - 1
    masks = reach(n_fsdp)
    rel = me_fsdp ^ jnp.asarray(masks, jnp.int32)

    own_cols = lax.dynamic_slice_in_dim(w_qkv, me_seq * 3 * hd, 3 * hd, 1)
    small = (ln1_gain, ln1_shift, bias_qv, bias_out, ln2_gain, ln2_shift, bias_proj)
    small = jnp.concatenate(small)
    extra = -(-small.shape[0] // (3 * hd * 16)) * 16
    tail = jnp.pad(small, (0, extra * 3 * hd - small.shape[0])).reshape(extra, 3 * hd)

    walk = Walk(ring.gather(x))
    wfc = lax.all_gather(w_fc, "fsdp", axis=0, tiled=True)
    dy_all = lax.all_gather(dy, "fsdp", axis=0, tiled=True)
    moved, mine = milestone(walk.moving, (own_cols, tail))
    walk.go(moved)
    packs = [jnp.concatenate(mine, axis=0)]
    held = None
    for bit in reversed(bits(n_fsdp)):
        packs = packs + [swap(p, "fsdp", bit) for p in packs]

    def projected(blocks):
        nonlocal held
        for k in blocks:
            if k < n_seq - 1:
                at = ring.shard(ring.walk[k])
            else:
                at = ring.shard(n_seq // 2) * 2 + (k - n_seq + 1)
            held = project(
                at, pieces[k], gain_one, shift_one, w_roles, b_own, total_rows, held
            )

    moved_first = moved
    moved, packs, w_out = milestone(walk.moving, packs, w_out)
    walk.go(moved)
    top = n_fsdp // 2
    wout_far = swap(w_out, "fsdp", top)

    w_own = jnp.zeros((width, 3 * hd), BF16)
    vectors = jnp.zeros((n_fsdp, tail.size), BF16)
    for k, p in enumerate(packs):
        index = me_fsdp ^ masks[k]
        w_own = lax.dynamic_update_slice_in_dim(w_own, p[:share], index * share, 0)
        vectors = lax.dynamic_update_slice_in_dim(vectors, p[share:].reshape(1, -1), index, 0)
    w_roles = w_own.reshape(width, heads, 3, HEAD).transpose(0, 2, 1, 3).reshape(width, 3 * hd)
    cut = []
    at = 0
    for count in (share, share, 2 * share, share, share, share, share):
        cut.append(vectors[:, at : at + count].reshape(1, -1).astype(F32))
        at += count
    gain_one, shift_one, bqv, bout, gain_two, shift_two, bproj = cut
    b_own = lax.dynamic_index_in_dim(bqv.reshape(n_seq, heads, 2, HEAD), me_seq, 0, keepdims=False)
    b_own = jnp.concatenate(
        [b_own[:, 0].reshape(1, hd), jnp.zeros((1, hd), F32), b_own[:, 1].reshape(1, hd)], axis=1
    )

    pieces = [x] + list(moved_first) + list(moved)
    done = 0
    while walk.result is None:
        ready = len(pieces)
        projected(range(done, ready))
        done = ready
        moved, held, wout_far = milestone(walk.moving, held, wout_far)
        walk.go(moved)
        pieces += list(moved)
    projected(range(done, len(pieces)))
    x_all, qkv = held

    attended, lse = attention_forward(row, qkv, rows)
    wout = jnp.zeros((width, width), BF16)
    wout_pieces = cube_gather(w_out, "fsdp", top) + cube_gather(wout_far, "fsdp", top)
    for k, mask in enumerate(reach(top) + [m | top for m in reach(top)]):
        wout = lax.dynamic_update_slice_in_dim(wout, wout_pieces[k], (me_fsdp ^ mask) * share, 0)
    merged = lax.all_to_all(
        attended.reshape(n_seq, rows, hd), "seq", split_axis=0, concat_axis=0, tiled=True
    )

    merged, wout = milestone(merged, wout)

    ends = jnp.sum(home_rows[:, :last], axis=1)

    def valid_counts(index):
        of = jnp.sum(jnp.where(index[:, None] == groups[None, :], ends[None, :], 0), axis=1)
        return jnp.clip(of - me_seq * rows, 0, rows)

    near = me_fsdp ^ jnp.asarray(reach(top), jnp.int32)
    far = near ^ top
    near_far = jnp.concatenate([near, far])
    counts = valid_counts(near)
    low, middle, square_attn = attend_out(
        counts, merged, x, wout, bout, gain_two, shift_two
    )

    bfc = bias_fc.astype(F32)[None]
    low_far = swap(low, "fsdp", top)
    low_near = cube_gather(low, "fsdp", top)
    halves = len(tier_bounds(top))
    results = feed(rel, near, counts, low_near, dy_all, wfc, w_proj, bfc, True)
    two_near, feed_near = Scatter(results[:halves], "fsdp"), results[halves:]
    low_far, feed_near = milestone(low_far, feed_near)
    while two_near.left:
        two_near.send()
        two_near.take()
    low_far = cube_gather(low_far, "fsdp", top)
    results = feed(rel, far, valid_counts(far), low_far, dy_all, wfc, w_proj, bfc, False)
    two_far, feed_far = Scatter(results[:halves], "fsdp"), results[halves:]
    while two_far.left:
        two_far.send()
        two_far.moving, feed_far, two_near.terms = milestone(
            two_far.moving, feed_far, two_near.terms
        )
        two_far.take()

    far_two = swap(add_up(two_far.terms[0]).astype(BF16), "fsdp", top)
    gproj, gfc, gbfc = feed_grads(feed_near, feed_far, low_near + low_far, n_seq)
    far_two, gproj, gfc = milestone(far_two, gproj, gfc)

    thin = share // n_seq
    blocks = wide // width
    gfc = gfc.reshape(n_seq * n_fsdp * thin, wide // n_fsdp)
    together = gfc.shape[0] == gproj.shape[0]
    walk = Walk(ring.reduce(gproj, gfc) if together else ring.reduce(gfc))
    results = middle_back(
        rel, counts, merged, middle, dy, gain_two, wout, two_near.terms[0] + [far_two]
    )
    tiers = len(tier_bounds(n_fsdp))
    gout, (d_middle, d_merged, sums_two) = results[:tiers], results[tiers:]
    moved, d_merged, gout = milestone(walk.moving, d_merged, gout)

    d_heads = lax.all_to_all(d_merged, "seq", split_axis=0, concat_axis=0, tiled=True)
    walk.go(moved)
    gout = Scatter(gout, "fsdp")
    hidden = (feed_near[0], feed_far[0])
    while gout.left > 1:
        gout.send()
        gout.moving, hidden = milestone(gout.moving, hidden)
        gout.take()
    gout.send()
    mlp_near = Scatter(feed_out(hidden[0], w_proj, rows, True), "fsdp")
    mlp_far = Scatter(feed_out(hidden[1], w_proj, rows, False), "fsdp")
    while mlp_near.left:
        mlp_near.send()
        mlp_far.send()
        mlp_near.take()
        mlp_far.take()
    mlp_far = add_up(mlp_far.terms[0]).astype(BF16)
    gout.moving, mlp_far, mlp_near.terms = milestone(gout.moving, mlp_far, mlp_near.terms)
    gout.take()
    out_walk = Walk(ring.reduce(add_up(gout.terms[0])))
    moved, d_heads, out_moved = milestone(walk.moving, d_heads, out_walk.moving)

    walk.go(moved)
    out_walk.go(out_moved)
    mlp_far = swap(mlp_far, "fsdp", top)
    d_own = attention_backward(row, qkv, attended, lse, d_heads.reshape(total_rows, hd), rows)
    moved, out_moved, d_own, mlp_far = milestone(walk.moving, out_walk.moving, d_own, mlp_far)
    d_packed = lax.all_to_all(
        d_own.reshape(n_seq, rows, 3 * hd), "seq", split_axis=0, concat_axis=0, tiled=True
    )
    walk.go(moved)
    out_walk.go(out_moved)
    w_qkv = milestone(w_qkv, d_own)[0]
    w_all = lax.all_gather(w_qkv, "fsdp", axis=0, tiled=True)
    grad_qkv, sums_one, d_sums = qkv_grads(x_all, d_own, w_own, gain_one, shift_one, rows)
    while walk.result is None:
        moved, out_moved, grad_qkv, sums_one, d_sums, mlp_far = milestone(
            walk.moving, out_walk.moving, grad_qkv, sums_one, d_sums, mlp_far
        )
        walk.go(moved)
        out_walk.go(out_moved)
    mine = walk.result
    if together:
        mine_proj, mine_fc = mine[:, :width], mine[:, width:]
    else:
        mine_fc = mine
        walk = Walk(ring.reduce(gproj))
        while walk.result is None:
            walk.go(walk.moving)
        mine_proj = walk.result
    mine_proj = mine_proj.reshape(blocks, thin, width).transpose(1, 0, 2).reshape(thin, wide)
    mine_fc = cube_exchange(mine_fc, "fsdp", 0)
    parts = [
        lax.dynamic_slice_in_dim(grad_qkv, (me_fsdp ^ mask) * share, share, 0) for mask in masks
    ]
    parts = [jnp.concatenate(parts[lo:hi], axis=0) for lo, hi in tier_bounds(n_fsdp)]
    parts = Scatter(parts, "fsdp")
    while parts.left > 1:
        parts.send()
        parts.take()
    while out_walk.result is None:
        parts.terms, mine_fc, out_moved = milestone(parts.terms, mine_fc, out_walk.moving)
        out_walk.go(out_moved)
    parts.send()
    parts.take()
    share_qkv = add_up(parts.terms[0]).astype(BF16)
    beside_it = share_qkv.reshape(n_seq, thin, 3 * hd).transpose(1, 0, 2).reshape(thin, -1)
    mine = jnp.concatenate([mine_proj] + mine_fc + [out_walk.result, beside_it], axis=1)

    mine, d_packed, mlp_far, sums_one, d_sums = milestone(
        mine, d_packed, mlp_far, sums_one, d_sums
    )
    walk = Walk(ring.gather(mine))
    output, square_ends = finish(counts, middle, bproj, mlp_near.terms[0] + [mlp_far])
    squares = jnp.concatenate([square_ends[:1], square_attn, square_ends[1:]], axis=0)
    squares = jnp.concatenate([jnp.sum(squares, axis=1), counts[:1].astype(F32)])[None]
    squares = jnp.concatenate([squares, jnp.zeros((n_fsdp - 1, 4), F32)], axis=0)
    grad_bfc = lax.dynamic_update_slice_in_dim(
        jnp.zeros((n_fsdp, wide // n_fsdp), F32), gbfc, me_fsdp, 0
    )
    d_sums = d_sums.reshape(heads, 3, HEAD)
    d_sums = jnp.stack([d_sums[:, 0], d_sums[:, 2]], axis=1).reshape(1, 2 * hd)
    grad_bqv = lax.dynamic_update_slice_in_dim(
        jnp.zeros((n_seq, 2 * hd), F32), d_sums, me_seq, 0
    )
    vectors = [sums_one[0], sums_one[1], grad_bqv, *[sums_two[k] for k in range(4)], grad_bfc]
    vectors = [v.reshape(n_fsdp, -1) for v in vectors]
    sums = jnp.concatenate(vectors + [squares], axis=1)
    for bit in bits(n_fsdp):
        sums = sums + swap(sums, "fsdp", bit)
    hops = bits(n_seq)
    arrived = [mine]

    layout = (
        ("rows", wide, blocks),
        ("rel", wide, n_fsdp),
        ("rows", width, 1),
        ("cols", 3 * width, n_seq),
    )
    steps = n_seq // 2
    input_grad = placed = own = squares = None
    for step in range(steps):
        ahead = steps - step
        count = -(-len(hops) // max(1, ahead - 1))
        for bit in hops[:count]:
            sums = sums + swap(sums, "seq", bit)
        hops = hops[count:]
        if ahead == min(3, steps):
            input_grad = input_gradient(d_packed, w_all, x, gain_one, d_middle)
        if ahead == 1:
            own = lax.dynamic_slice_in_dim(sums, me_fsdp, 1, 0)[0]
            squares = sums[0, -4:]
            placed = place(ring.order, rel, arrived, layout, n_seq)
        moved, sums, input_grad, placed, own, squares, output = milestone(
            walk.moving, sums, input_grad, placed, own, squares, output
        )
        if ahead > 1:
            arrived += list(moved)
        walk.go(moved)
    stats = jnp.sqrt(squares[:3] / (squares[3] * width))
    farthest = ring.shard(n_seq // 2).reshape(1)
    last_piece = [jnp.concatenate(walk.result[-2:], axis=0)]
    placed = place(farthest, rel, last_piece, layout, n_seq, placed)
    grad_proj, grad_fc, grad_out, grad_wqkv = flat_matrices(placed, layout)

    shares = []
    at = 0
    for vector in vectors:
        shares.append(own[at : at + vector.shape[1]])
        at += vector.shape[1]
    g1, s1, bqv, bout, g2, s2, bproj, bfc = shares
    return (
        output[None],
        input_grad[None],
        g1,
        s1,
        grad_wqkv,
        bqv,
        grad_out,
        bout,
        g2,
        s2,
        grad_fc,
        bfc,
        grad_proj,
        bproj,
        stats,
    )


def solution(mesh):
    rows_split = P("fsdp", "seq", None)
    matrix = P("fsdp", None)
    vector = P("fsdp")
    params = (
        vector,
        vector,
        matrix,
        vector,
        matrix,
        vector,
        vector,
        vector,
        matrix,
        vector,
        matrix,
        vector,
    )
    return jax.shard_map(
        shards,
        mesh=mesh,
        in_specs=(rows_split, rows_split, P(), P()) + params,
        out_specs=(rows_split, rows_split) + params + (P(),),
        check_vma=False,
    )
```

```python
import functools

import jax
import jax.numpy as jnp
from jax import lax
from jax.experimental import pallas as pl
from jax.experimental.pallas import tpu as pltpu
from jax.sharding import PartitionSpec as P

H = 16
HEAD = 64
NT = (((1,), (1,)), ((), ()))
TN = (((0,), (0,)), ((), ()))
F32 = jnp.float32
BF16 = jnp.bfloat16


def seg_starts(len_ref, segs, place):
    start = jnp.zeros_like(place)
    end = jnp.int32(0)
    for k in range(segs - 1):
        end = end + len_ref[k]
        start = jnp.where(place >= end, end, start)
    return start


def head_part(block, h, heads):
    if heads == 1:
        return block
    lane = lax.broadcasted_iota(jnp.int32, block.shape, 1)
    return jnp.where((lane >= h * HEAD) & (lane < (h + 1) * HEAD), block, jnp.zeros_like(block))


def beside(block, heads):
    return jnp.concatenate([head_part(block, h, heads) for h in range(heads)], axis=0)


def diagonal(wide, heads):
    block = wide.shape[1] // heads
    parts = [
        wide[h * HEAD : (h + 1) * HEAD, h * block : (h + 1) * block] for h in range(heads)
    ]
    return jnp.concatenate(parts, axis=0)


DIRECT = 4


def visit(i, block, segs, len_ref, direct, loop):
    r0 = pl.multiple_of(i * block, block)
    place = r0 + lax.broadcasted_iota(jnp.int32, (1, block), 1)
    start = seg_starts(len_ref, segs, place)
    first = seg_starts(len_ref, segs, r0) // block
    for n in range(1, DIRECT + 1):

        @pl.when(i - first + 1 == n)
        def _():
            direct(n, r0, place, start, pl.multiple_of((i - n + 1) * block, block))

    @pl.when(i - first + 1 > DIRECT)
    def _():
        loop(r0, place, start, first)


def seen(c0, count, place, start, heads):
    key_pos = c0 + lax.broadcasted_iota(jnp.int32, (count, place.shape[1]), 0)
    ok = (key_pos >= start) & (key_pos <= place)
    return jnp.concatenate([ok] * heads, axis=1)


def forward_kernel(heads, block, segs, len_ref, qkv_ref, o_ref, lse_ref, vt_ref):
    hd = heads * HEAD
    steps = qkv_ref.shape[0] // block

    def flip(i, _):
        at = pl.multiple_of(i * block, block)
        vt_ref[:, pl.ds(at, block)] = qkv_ref[pl.ds(at, block), 2 * hd : 3 * hd].T
        return 0

    lax.fori_loop(0, steps, flip, 0)

    def queries(r0):
        return beside(qkv_ref[pl.ds(r0, block), 0:hd] * jnp.asarray(HEAD**-0.5, BF16), heads)

    def store(r0, top, total, acc):
        lse = top + jnp.log(total)
        for h in range(heads):
            lse_ref[h : h + 1, pl.ds(r0, block)] = lse[:, h * block : (h + 1) * block]
        o_ref[pl.ds(r0, block), :] = diagonal(acc / total, heads).T.astype(BF16)

    def direct(n, r0, place, start, c0):
        keys = pl.ds(c0, n * block)
        s = lax.dot_general(qkv_ref[keys, hd : 2 * hd], queries(r0), NT, preferred_element_type=F32)
        s = jnp.where(seen(c0, n * block, place, start, heads), s, -1e30)
        top = jnp.max(s, axis=0, keepdims=True)
        p = jnp.exp(s - top)
        total = jnp.sum(p, axis=0, keepdims=True)
        acc = jnp.dot(vt_ref[:, keys], p.astype(BF16), preferred_element_type=F32)
        store(r0, top, total, acc)

    def loop(r0, place, start, first):
        q = queries(r0)

        def key_step(j, carry):
            top, total, acc = carry
            c0 = pl.multiple_of(j * block, block)
            keys = pl.ds(c0, block)
            s = lax.dot_general(qkv_ref[keys, hd : 2 * hd], q, NT, preferred_element_type=F32)
            s = jnp.where(seen(c0, block, place, start, heads), s, -1e30)
            new = jnp.maximum(top, jnp.max(s, axis=0, keepdims=True))
            p = jnp.exp(s - new)
            shrink = jnp.exp(top - new)
            total = total * shrink + jnp.sum(p, axis=0, keepdims=True)
            acc = acc * shrink + jnp.dot(
                vt_ref[:, keys], p.astype(BF16), preferred_element_type=F32
            )
            return new, total, acc

        wide = heads * block
        init = (
            jnp.full((1, wide), -1e30, F32),
            jnp.zeros((1, wide), F32),
            jnp.zeros((hd, wide), F32),
        )
        store(r0, *lax.fori_loop(first, r0 // block + 1, key_step, init))

    def query_step(i, _):
        visit(i, block, segs, len_ref, direct, loop)
        return 0

    lax.fori_loop(0, steps, query_step, 0)


def backward_kernel(
    heads,
    block,
    segs,
    len_ref,
    qkv_ref,
    o_ref,
    lse_ref,
    do_ref,
    d_ref,
    kt_ref,
    dq_ref,
    dk_ref,
    dv_ref,
):
    hd = heads * HEAD
    steps = qkv_ref.shape[0] // block

    def flip(i, _):
        at = pl.multiple_of(i * block, block)
        kt_ref[:, pl.ds(at, block)] = qkv_ref[pl.ds(at, block), hd : 2 * hd].T
        dk_ref[pl.ds(at, block), :] = jnp.zeros((block, hd), F32)
        dv_ref[pl.ds(at, block), :] = jnp.zeros((block, hd), F32)
        return 0

    lax.fori_loop(0, steps, flip, 0)

    def operands(r0):
        rows = pl.ds(r0, block)
        q = beside(qkv_ref[rows, 0:hd] * jnp.asarray(HEAD**-0.5, BF16), heads)
        do = do_ref[rows, :]
        both = (do.astype(F32) * o_ref[rows, :].astype(F32)).T
        delta = [
            jnp.sum(both[h * HEAD : (h + 1) * HEAD], axis=0, keepdims=True) for h in range(heads)
        ]
        lse = [lse_ref[h : h + 1, rows] for h in range(heads)]
        return q, beside(do, heads), jnp.concatenate(delta, axis=1), jnp.concatenate(lse, axis=1)

    def part(c0, count, place, start, q, do, delta, lse):
        keys = pl.ds(c0, count)
        s = lax.dot_general(qkv_ref[keys, hd : 2 * hd], q, NT, preferred_element_type=F32)
        p = jnp.where(seen(c0, count, place, start, heads), jnp.exp(s - lse), 0.0)
        dp = lax.dot_general(
            qkv_ref[keys, 2 * hd : 3 * hd], do, NT, preferred_element_type=F32
        )
        ds = (p * (dp - delta)).astype(BF16)
        dv_ref[keys, :] += jnp.dot(p.astype(BF16), do, preferred_element_type=F32)
        dk_ref[keys, :] += jnp.dot(ds, q, preferred_element_type=F32)
        return jnp.dot(kt_ref[:, keys], ds, preferred_element_type=F32)

    def store(r0, dq):
        dq_ref[pl.ds(r0, block), :] = (diagonal(dq, heads) * HEAD**-0.5).T

    def direct(n, r0, place, start, c0):
        store(r0, part(c0, n * block, place, start, *operands(r0)))

    def loop(r0, place, start, first):
        given = operands(r0)

        def key_step(j, dq):
            return dq + part(pl.multiple_of(j * block, block), block, place, start, *given)

        init = jnp.zeros((hd, heads * block), F32)
        store(r0, lax.fori_loop(first, r0 // block + 1, key_step, init))

    def query_step(i, _):
        visit(i, block, segs, len_ref, direct, loop)
        return 0

    lax.fori_loop(0, steps, query_step, 0)

    def finish_rows(i, _):
        rows = pl.ds(pl.multiple_of(i * block, block), block)
        roles = [ref[rows, :] for ref in (dq_ref, dk_ref, dv_ref)]
        parts = [v[:, h * HEAD : (h + 1) * HEAD] for h in range(heads) for v in roles]
        d_ref[rows, :] = jnp.concatenate(parts, axis=1).astype(BF16)
        return 0

    lax.fori_loop(0, steps, finish_rows, 0)


def takes(us):
    return pl.CostEstimate(flops=int(us * 3.30e9), bytes_accessed=1 << 20, transcendentals=0)


VM = pl.BlockSpec(memory_space=pltpu.VMEM)
SM = pl.BlockSpec(memory_space=pltpu.SMEM)
LIMIT = 32 << 20


def attention_forward(row, qkv, block):
    rows, wide = qkv.shape
    hd = wide // 3
    heads = hd // HEAD
    return pl.pallas_call(
        functools.partial(forward_kernel, heads, block, row.shape[0]),
        out_shape=(
            jax.ShapeDtypeStruct((rows, hd), BF16),
            jax.ShapeDtypeStruct((heads, rows), F32),
        ),
        in_specs=[SM, VM],
        out_specs=(VM, VM),
        scratch_shapes=[pltpu.VMEM((hd, rows), BF16)],
        compiler_params=pltpu.CompilerParams(vmem_limit_bytes=LIMIT),
        cost_estimate=takes(14),
        name="attention_forward",
    )(row, qkv)


def attention_backward(row, qkv, o, lse, do, block):
    rows, wide = qkv.shape
    hd = wide // 3
    heads = hd // HEAD
    return pl.pallas_call(
        functools.partial(backward_kernel, heads, block, row.shape[0]),
        out_shape=jax.ShapeDtypeStruct((rows, wide), BF16),
        in_specs=[SM] + [VM] * 4,
        out_specs=VM,
        scratch_shapes=[pltpu.VMEM((hd, rows), BF16)] + [pltpu.VMEM((rows, hd), F32)] * 3,
        compiler_params=pltpu.CompilerParams(vmem_limit_bytes=44 << 20),
        cost_estimate=takes(21),
        name="attention_backward",
    )(row, qkv, o, lse, do)


def tier_bounds(n):
    bounds = [(0, 1)]
    while bounds[-1][1] < n:
        bounds.append((bounds[-1][1], 2 * bounds[-1][1]))
    return bounds


def norm_parts(value):
    mean = jnp.mean(value, axis=-1, keepdims=True)
    centred = value - mean
    spread = jnp.mean(centred * centred, axis=-1, keepdims=True)
    scale = lax.rsqrt(spread + 1e-05)
    return centred * scale, scale


def project_kernel(at_ref, x_ref, gain_ref, shift_ref, w_ref, b_ref, *rest):
    x_out, qkv_out = rest[-2:]
    x = x_ref[...]
    n, _ = norm_parts(x.astype(F32))
    low = (n * gain_ref[...] + shift_ref[...]).astype(BF16)
    mixed = jnp.dot(low, w_ref[...], preferred_element_type=F32) + b_ref[...]
    x_out[...] = x
    qkv_out[...] = mixed.astype(BF16)


def project(at, x, gain, shift, w, b, total, held):
    rows, width = x.shape
    wide = w.shape[1]

    def fixed(shape):
        return pl.BlockSpec(shape, lambda i, at: (0, 0))

    given = () if held is None else held
    return pl.pallas_call(
        project_kernel,
        grid_spec=pltpu.PrefetchScalarGridSpec(
            num_scalar_prefetch=1,
            grid=(1,),
            in_specs=[
                fixed((rows, width)),
                fixed((1, width)),
                fixed((1, width)),
                fixed((width, wide)),
                fixed((1, wide)),
            ]
            + [pl.BlockSpec(memory_space=pl.ANY)] * len(given),
            out_specs=[
                pl.BlockSpec((rows, width), lambda i, at: (at[0], 0)),
                pl.BlockSpec((rows, wide), lambda i, at: (at[0], 0)),
            ],
        ),
        out_shape=(
            jax.ShapeDtypeStruct((total, width), BF16),
            jax.ShapeDtypeStruct((total, wide), BF16),
        ),
        input_output_aliases={6: 0, 7: 1} if given else {},
        cost_estimate=takes(2),
        compiler_params=pltpu.CompilerParams(vmem_limit_bytes=24 << 20),
        name="project",
    )(at.reshape(1), x, gain, shift, w, b, *given)


def attend_out_kernel(
    count_ref,
    merged_ref,
    x_ref,
    wout_ref,
    bout_ref,
    gain_ref,
    shift_ref,
    low_ref,
    middle_ref,
    stat_ref,
):
    rows = x_ref.shape[0]
    merged = jnp.concatenate([merged_ref[k] for k in range(merged_ref.shape[0])], axis=1)
    attn = jnp.dot(merged, wout_ref[...], preferred_element_type=F32) + bout_ref[...]
    middle = x_ref[...].astype(F32) + attn
    middle_ref[...] = middle
    n, _ = norm_parts(middle)
    low_ref[...] = (n * gain_ref[...] + shift_ref[...]).astype(BF16)
    valid = lax.broadcasted_iota(jnp.int32, (rows, 1), 0) < count_ref[0]
    stat_ref[...] = jnp.sum(jnp.where(valid, attn * attn, 0.0), axis=0, keepdims=True)


def attend_out(count, merged, x, wout, bout, gain, shift):
    rows, width = x.shape
    return pl.pallas_call(
        attend_out_kernel,
        in_specs=[SM] + [VM] * 6,
        out_specs=(VM,) * 3,
        out_shape=(
            jax.ShapeDtypeStruct((rows, width), BF16),
            jax.ShapeDtypeStruct((rows, width), F32),
            jax.ShapeDtypeStruct((1, width), F32),
        ),
        cost_estimate=takes(5),
        compiler_params=pltpu.CompilerParams(vmem_limit_bytes=40 << 20),
        name="attend_out",
    )(count, merged, x, wout, bout, gain, shift)


GELU = 0.7978845608028654


def feed_kernel(
    packs, rel_ref, which_ref, count_ref, bfc_ref, wproj_ref, wfc_ref, dy_ref, *rest
):
    low_refs, rest = rest[:packs], rest[packs:]
    tiers = tier_bounds(packs)
    dtwo_refs, rest = rest[: len(tiers)], rest[len(tiers) :]
    hidden_ref, di_ref, dmlp_ref, low_s = rest
    step = pl.program_id(0)
    rows = low_s.shape[0]
    valid = lax.broadcasted_iota(jnp.int32, (rows, 1), 0) < count_ref[step]

    for k in range(packs):

        @pl.when(step == k)
        def _():
            low_s[...] = low_refs[k][...]

    dy = dy_ref[...]
    dmlp_ref[...] = jnp.where(valid, dy, jnp.zeros_like(dy))

    u = jnp.dot(low_s[...], wfc_ref[...], preferred_element_type=F32) + bfc_ref[...]
    dh = lax.dot_general(dmlp_ref[...], wproj_ref[...], NT, preferred_element_type=F32)
    square = u * u
    t = jnp.tanh(GELU * u * (1.0 + 0.044715 * square))
    side = 0.5 * (1.0 + t)
    hidden_ref[...] = (u * side).astype(BF16)
    slope = side + 0.5 * u * (1.0 - t * t) * (GELU * (1.0 + 3 * 0.044715 * square))
    di = (dh * slope).astype(BF16)
    di_ref[...] = di
    dtwo = lax.dot_general(di, wfc_ref[...], NT, preferred_element_type=F32)
    for (lo, hi), out_ref in zip(tiers, dtwo_refs):

        @pl.when((step >= lo) & (step < hi))
        def _():
            out_ref[...] = dtwo.astype(out_ref.dtype)


def feed(rel, which, counts, low_pieces, dy_all, wfc, wproj, bfc, own):
    rows, width = low_pieces[0].shape
    packs = len(low_pieces)
    wide = wproj.shape[0]
    tiers = tier_bounds(packs)

    def whole(*shape):
        return pl.BlockSpec(shape, lambda g, *_: (0,) * len(shape), pipeline_mode=pl.Buffered(1))

    def tier(lo, hi):
        return pl.BlockSpec((rows, width), lambda g, *_: (jnp.clip(g - lo, 0, hi - lo - 1), 0))

    each = pl.BlockSpec((rows, wide), lambda g, *_: (g, 0))
    return pl.pallas_call(
        functools.partial(feed_kernel, packs),
        grid_spec=pltpu.PrefetchScalarGridSpec(
            num_scalar_prefetch=3,
            grid=(packs,),
            in_specs=[
                whole(1, wide),
                whole(wide, width),
                pl.BlockSpec(
                    (width, wide), lambda g, rel, *_: (0, rel[0]), pipeline_mode=pl.Buffered(1)
                ),
                pl.BlockSpec((rows, width), lambda g, rel, which, _: (which[g], 0)),
            ]
            + [whole(rows, width)] * packs,
            out_specs=[tier(lo, hi) for lo, hi in tiers]
            + [each, each, pl.BlockSpec((rows, width), lambda g, *_: (g, 0))],
            scratch_shapes=[pltpu.VMEM((rows, width), BF16)],
        ),
        out_shape=tuple(
            [
                jax.ShapeDtypeStruct(((hi - lo) * rows, width), F32 if lo == 0 and own else BF16)
                for lo, hi in tiers
            ]
            + [jax.ShapeDtypeStruct((packs * rows, wide), BF16)] * 2
            + [jax.ShapeDtypeStruct((packs * rows, width), BF16)]
        ),
        cost_estimate=takes(10),
        compiler_params=pltpu.CompilerParams(vmem_limit_bytes=52 << 20),
        name="feed",
    )(rel, which, counts, bfc, wproj, wfc, dy_all, *low_pieces)


def feed_grads_kernel(
    near, n_fsdp, hid_a, hid_b, di_a, di_b, dmlp_a, dmlp_b, *rest
):
    low_refs, rest = rest[:n_fsdp], rest[n_fsdp:]
    gproj_ref, gfc_ref, gbfc_ref = rest[:3]
    scratch = rest[3:]
    step = pl.program_id(0)
    rows, wide = hid_a.shape
    n_seq, _, thin, _ = gfc_ref.shape
    share = n_seq * thin

    @pl.when(step == 0)
    def _():
        gbfc_ref[...] = jnp.zeros_like(gbfc_ref)

    def store_fc(i, g):
        for k in range(n_seq):
            gfc_ref[k, i] = g[k * thin : (k + 1) * thin]

    for k in range(n_fsdp):
        hid_ref, di_ref, dmlp_ref = (hid_a, di_a, dmlp_a) if k < near else (hid_b, di_b, dmlp_b)

        @pl.when(step == k)
        def _():
            di = di_ref[...]
            gbfc_ref[...] += jnp.sum(di.astype(F32), axis=0, keepdims=True)
            if len(scratch) == 2:
                proj_s, fc_s = scratch
                proj = jnp.dot(hid_ref[...].T, dmlp_ref[...], preferred_element_type=F32)
                fc = jnp.dot(low_refs[k][...].T, di, preferred_element_type=F32)
                proj_s[...] = proj if k == 0 else proj_s[...] + proj
                fc_s[...] = fc if k == 0 else fc_s[...] + fc
            else:
                hiddent_s, di_s, dmlp_s, lowt_s = scratch
                at = slice(k * rows, (k + 1) * rows)
                hiddent_s[:, at] = hid_ref[...].T
                di_s[at, :] = di
                dmlp_s[at, :] = dmlp_ref[...]
                lowt_s[:, at] = low_refs[k][...].T

    @pl.when(step == n_fsdp - 1)
    def _():
        if len(scratch) == 2:
            proj_s, fc_s = scratch
            gproj_ref[...] = proj_s[...].astype(BF16)
            for i in range(n_fsdp):
                store_fc(i, fc_s[i * share : (i + 1) * share, :].astype(BF16))
            return
        hiddent_s, di_s, dmlp_s, lowt_s = scratch
        tile = min(256, wide)

        def proj_tile(i, _):
            at = pl.multiple_of(i * tile, tile)
            g = jnp.dot(hiddent_s[pl.ds(at, tile), :], dmlp_s[...], preferred_element_type=F32)
            gproj_ref[pl.ds(at, tile), :] = g.astype(BF16)
            return 0

        lax.fori_loop(0, wide // tile, proj_tile, 0)

        def fc_tile(i, _):
            at = pl.multiple_of(i * share, share)
            g = jnp.dot(lowt_s[pl.ds(at, share), :], di_s[...], preferred_element_type=F32)
            store_fc(i, g.astype(BF16))
            return 0

        lax.fori_loop(0, n_fsdp, fc_tile, 0)


def feed_grads(near, far, low_pieces, n_seq):
    rows, width = low_pieces[0].shape
    n_fsdp = len(low_pieces)
    wide = near[0].shape[1]
    total = n_fsdp * rows
    count = near[0].shape[0] // rows
    thin = width // n_fsdp // n_seq
    if total > 2048:
        scratch = [pltpu.VMEM((wide, width), F32), pltpu.VMEM((width, wide), F32)]
    else:
        scratch = [pltpu.VMEM((wide, total), BF16), pltpu.VMEM((total, wide), BF16)]
        scratch += [pltpu.VMEM((total, width), BF16), pltpu.VMEM((width, total), BF16)]

    def whole(*shape):
        return pl.BlockSpec(shape, lambda g: (0,) * len(shape), pipeline_mode=pl.Buffered(1))

    def last(*shape):
        return pl.BlockSpec(shape, lambda g: (0,) * len(shape))

    def of_near(columns):
        return pl.BlockSpec((rows, columns), lambda g: (jnp.minimum(g, count - 1), 0))

    def of_far(columns):
        return pl.BlockSpec((rows, columns), lambda g: (jnp.maximum(g - count, 0), 0))

    pairs = [(of_near(wide), of_far(wide))] * 2 + [(of_near(width), of_far(width))]
    return pl.pallas_call(
        functools.partial(feed_grads_kernel, count, n_fsdp),
        grid=(n_fsdp,),
        in_specs=[spec for pair in pairs for spec in pair] + [whole(rows, width)] * n_fsdp,
        out_specs=[last(wide, width), last(n_seq, n_fsdp, thin, wide), last(1, wide)],
        out_shape=(
            jax.ShapeDtypeStruct((wide, width), BF16),
            jax.ShapeDtypeStruct((n_seq, n_fsdp, thin, wide), BF16),
            jax.ShapeDtypeStruct((1, wide), F32),
        ),
        scratch_shapes=scratch,
        cost_estimate=takes(15),
        compiler_params=pltpu.CompilerParams(vmem_limit_bytes=48 << 20),
        name="feed_grads",
    )(near[0], far[0], near[1], far[1], near[2], far[2], *low_pieces)


def feed_out_kernel(packs, hidden_ref, wproj_ref, *mlp_refs):
    step = pl.program_id(0)
    mlp = jnp.dot(hidden_ref[...], wproj_ref[...], preferred_element_type=F32)
    for (lo, hi), out_ref in zip(tier_bounds(packs), mlp_refs):

        @pl.when((step >= lo) & (step < hi))
        def _():
            out_ref[...] = mlp.astype(out_ref.dtype)


def feed_out(hidden, wproj, rows, own):
    wide, width = wproj.shape
    packs = hidden.shape[0] // rows
    tiers = tier_bounds(packs)

    def tier(lo, hi):
        return pl.BlockSpec((rows, width), lambda g: (jnp.clip(g - lo, 0, hi - lo - 1), 0))

    return pl.pallas_call(
        functools.partial(feed_out_kernel, packs),
        grid=(packs,),
        in_specs=[
            pl.BlockSpec((rows, wide), lambda g: (g, 0)),
            pl.BlockSpec((wide, width), lambda g: (0, 0), pipeline_mode=pl.Buffered(1)),
        ],
        out_specs=[tier(lo, hi) for lo, hi in tiers],
        out_shape=tuple(
            jax.ShapeDtypeStruct(((hi - lo) * rows, width), F32 if lo == 0 and own else BF16)
            for lo, hi in tiers
        ),
        cost_estimate=takes(0.3),
        compiler_params=pltpu.CompilerParams(vmem_limit_bytes=20 << 20),
        name="feed_out",
    )(hidden, wproj)


def middle_back_kernel(
    n_fsdp,
    terms,
    rel_ref,
    count_ref,
    merged_ref,
    middle_ref,
    dy_ref,
    gain_ref,
    wout_ref,
    *rest,
):
    tiers = tier_bounds(n_fsdp)
    term_refs, rest = rest[:terms], rest[terms:]
    gout_refs, rest = rest[: len(tiers)], rest[len(tiers) :]
    d_middle_ref, d_merged_ref, vec_ref, flip_s, order_s = rest
    n_seq, rows, hd = merged_ref.shape
    share = flip_s.shape[0] // n_fsdp
    valid = lax.broadcasted_iota(jnp.int32, (rows, 1), 0) < count_ref[0]
    n, scale = norm_parts(middle_ref[...])
    d_two = functools.reduce(jnp.add, [ref[...].astype(F32) for ref in term_refs])
    d_result = jnp.where(valid, dy_ref[...].astype(F32), 0.0)
    e = d_two * gain_ref[...]
    d_middle = d_result + scale * (
        e - jnp.mean(e, axis=-1, keepdims=True) - n * jnp.mean(e * n, axis=-1, keepdims=True)
    )
    d_middle_ref[...] = d_middle
    d_attn = d_middle.astype(BF16)
    d_merged = lax.dot_general(d_attn, wout_ref[...], NT, preferred_element_type=F32).astype(BF16)
    for k in range(n_seq):
        d_merged_ref[k] = d_merged[:, k * hd : (k + 1) * hd]
    vec_ref[0:1, :] = jnp.sum(d_attn.astype(F32), axis=0, keepdims=True)
    vec_ref[1:2, :] = jnp.sum(d_two * n, axis=0, keepdims=True)
    vec_ref[2:3, :] = jnp.sum(d_two, axis=0, keepdims=True)
    vec_ref[3:4, :] = jnp.sum(d_result, axis=0, keepdims=True)
    merged = jnp.concatenate([merged_ref[k] for k in range(n_seq)], axis=1)
    flip_s[...] = merged.T
    for k in range(n_fsdp):
        at = pl.multiple_of(rel_ref[k] * share, share)
        order_s[k * share : (k + 1) * share, :] = flip_s[pl.ds(at, share), :]
    gout = jnp.dot(order_s[...], d_attn, preferred_element_type=F32).astype(BF16)
    for (lo, hi), out_ref in zip(tiers, gout_refs):
        out_ref[...] = gout[lo * share : hi * share]


def middle_back(rel, count, merged, middle, dy, gain, wout, terms):
    rows, width = middle.shape
    n_fsdp = rel.shape[0]
    share = width // n_fsdp
    tiers = tier_bounds(n_fsdp)
    return pl.pallas_call(
        functools.partial(middle_back_kernel, n_fsdp, len(terms)),
        in_specs=[SM] * 2 + [VM] * (5 + len(terms)),
        out_specs=(VM,) * (len(tiers) + 3),
        out_shape=tuple(
            [jax.ShapeDtypeStruct(((hi - lo) * share, width), BF16) for lo, hi in tiers]
            + [
                jax.ShapeDtypeStruct((rows, width), F32),
                jax.ShapeDtypeStruct(merged.shape, BF16),
                jax.ShapeDtypeStruct((4, width), F32),
            ]
        ),
        scratch_shapes=[pltpu.VMEM((width, rows), BF16)] * 2,
        cost_estimate=takes(7),
        compiler_params=pltpu.CompilerParams(vmem_limit_bytes=36 << 20),
        name="middle_back",
    )(rel, count, merged, middle, dy, gain, wout, *terms)


def finish_kernel(count_ref, middle_ref, bproj_ref, *rest):
    term_refs, output_ref, stat_ref = rest[:-2], rest[-2], rest[-1]
    rows = middle_ref.shape[0]
    valid = lax.broadcasted_iota(jnp.int32, (rows, 1), 0) < count_ref[0]
    branch = functools.reduce(jnp.add, [ref[...].astype(F32) for ref in term_refs])
    branch = branch + bproj_ref[...]
    result = middle_ref[...] + branch
    output_ref[...] = jnp.where(valid, result, 0.0).astype(BF16)
    stat_ref[0:1, :] = jnp.sum(jnp.where(valid, result * result, 0.0), axis=0, keepdims=True)
    stat_ref[1:2, :] = jnp.sum(jnp.where(valid, branch * branch, 0.0), axis=0, keepdims=True)


def finish(count, middle, bproj, terms):
    rows, width = middle.shape
    return pl.pallas_call(
        finish_kernel,
        in_specs=[SM] + [VM] * (2 + len(terms)),
        out_specs=(VM,) * 2,
        out_shape=(
            jax.ShapeDtypeStruct((rows, width), BF16),
            jax.ShapeDtypeStruct((2, width), F32),
        ),
        cost_estimate=takes(3),
        compiler_params=pltpu.CompilerParams(vmem_limit_bytes=32 << 20),
        name="finish",
    )(count, middle, bproj, *terms)


def qkv_grad_kernel(x_ref, d_ref, w_ref, gain_ref, shift_ref, g_ref, vec_ref, sum_ref, acc):
    step = pl.program_id(0)
    n, _ = norm_parts(x_ref[...].astype(F32))
    low = (n * gain_ref[...] + shift_ref[...]).astype(BF16)
    d = d_ref[...]
    part = lax.dot_general(d, w_ref[...], NT, preferred_element_type=F32)
    gain_part = jnp.sum(part * n, axis=0, keepdims=True)
    shift_part = jnp.sum(part, axis=0, keepdims=True)
    sum_part = jnp.sum(d.astype(F32), axis=0, keepdims=True)
    g = jnp.dot(low.T, d, preferred_element_type=F32)

    @pl.when(step == 0)
    def _():
        acc[...] = g
        vec_ref[0:1, :] = gain_part
        vec_ref[1:2, :] = shift_part
        sum_ref[...] = sum_part

    @pl.when(step > 0)
    def _():
        acc[...] += g
        vec_ref[0:1, :] += gain_part
        vec_ref[1:2, :] += shift_part
        sum_ref[...] += sum_part

    @pl.when(step == pl.num_programs(0) - 1)
    def _():
        g_ref[...] = acc[...].astype(BF16)


def qkv_grads(x_all, d_own, w_own, gain, shift, block):
    total, width = x_all.shape
    wide = w_own.shape[1]

    def whole(*shape):
        return pl.BlockSpec(shape, lambda g: (0,) * len(shape))

    return pl.pallas_call(
        qkv_grad_kernel,
        grid=(total // block,),
        in_specs=[
            pl.BlockSpec((block, width), lambda g: (g, 0)),
            pl.BlockSpec((block, wide), lambda g: (g, 0)),
            whole(width, wide),
            whole(1, width),
            whole(1, width),
        ],
        out_specs=[whole(width, wide), whole(2, width), whole(1, wide)],
        out_shape=(
            jax.ShapeDtypeStruct((width, wide), BF16),
            jax.ShapeDtypeStruct((2, width), F32),
            jax.ShapeDtypeStruct((1, wide), F32),
        ),
        scratch_shapes=[pltpu.VMEM((width, wide), F32)],
        cost_estimate=takes(13),
        compiler_params=pltpu.CompilerParams(vmem_limit_bytes=40 << 20),
        name="qkv_grads",
    )(x_all, d_own, w_own, gain, shift)


def input_grad_kernel(d_ref, x_ref, gain_ref, d_middle_ref, w_ref, out_ref, d_s, one_s):
    step = pl.program_id(0)
    steps, _, share = one_s.shape

    @pl.when(step == 0)
    def _():
        d_s[...] = jnp.concatenate([d_ref[k] for k in range(d_ref.shape[0])], axis=1)

    one_s[step] = lax.dot_general(d_s[...], w_ref[...], NT, preferred_element_type=F32)

    @pl.when(step == steps - 1)
    def _():
        n, scale = norm_parts(x_ref[...].astype(F32))
        d_one = jnp.concatenate([one_s[k] for k in range(steps)], axis=1)
        e = d_one * gain_ref[...]
        out_ref[...] = d_middle_ref[...] + scale * (
            e - jnp.mean(e, axis=-1, keepdims=True) - n * jnp.mean(e * n, axis=-1, keepdims=True)
        )


def input_gradient(d_packed, w_all, x, gain, d_middle):
    rows, width = x.shape
    n_seq, _, each = d_packed.shape
    wide = w_all.shape[1]
    steps = 4

    def whole(*shape):
        return pl.BlockSpec(shape, lambda g: (0,) * len(shape), pipeline_mode=pl.Buffered(1))

    return pl.pallas_call(
        input_grad_kernel,
        grid=(steps,),
        in_specs=[
            whole(n_seq, rows, each),
            whole(rows, width),
            whole(1, width),
            whole(rows, width),
            pl.BlockSpec((width // steps, wide), lambda g: (g, 0)),
        ],
        out_specs=whole(rows, width),
        out_shape=jax.ShapeDtypeStruct((rows, width), F32),
        scratch_shapes=[
            pltpu.VMEM((rows, wide), BF16),
            pltpu.VMEM((steps, rows, width // steps), F32),
        ],
        cost_estimate=takes(8),
        compiler_params=pltpu.CompilerParams(vmem_limit_bytes=32 << 20),
        name="input_gradient",
    )(d_packed, x, gain, d_middle, w_all)


def place_kernel(layout, groups, order_ref, rel_ref, *refs):
    outs = refs[len(refs) - len(layout) :]
    step = pl.program_id(0)
    for k, group in enumerate(groups):

        @pl.when(step == k)
        def _():
            thin = sum(refs[i].shape[0] for i in group)
            at = 0

            def columns(each):
                parts = [refs[i][:, at : at + each].astype(F32) for i in group]
                return parts[0] if len(parts) == 1 else jnp.concatenate(parts, axis=0)

            for (kind, wide, blocks), out in zip(layout, outs):
                each = wide // blocks
                for a in range(blocks):
                    part = columns(each)
                    at += each
                    if kind == "rel":
                        lanes = pl.ds(pl.multiple_of(rel_ref[a] * each, each), each)
                        out[0, :, lanes] = part
                    elif len(out.shape) == 3:
                        out[0, a * thin : (a + 1) * thin, :] = part
                    else:
                        out[a * thin : (a + 1) * thin, :] = part


def place(order, rel, pieces, layout, n, held=None):
    halves = held is not None
    groups = [range(len(pieces))] if halves else [[k] for k in range(len(pieces))]
    thin = sum(pieces[k].shape[0] for k in groups[0])
    shapes = []
    specs = []
    for kind, wide, blocks in layout:
        each = wide // blocks
        if kind == "cols" and each % 128 == 0:
            shapes.append((blocks * thin, n * each))
            specs.append(pl.BlockSpec((blocks * thin, each), lambda g, order, _: (0, order[g])))
            continue
        size = (thin, wide) if kind == "rel" else (blocks * thin, each)
        shapes.append((n,) + size)
        specs.append(pl.BlockSpec((1,) + size, lambda g, order, _: (order[g], 0, 0)))
    given = () if held is None else tuple(held)
    first = 2 + len(pieces)
    return pl.pallas_call(
        functools.partial(place_kernel, layout, groups),
        grid_spec=pltpu.PrefetchScalarGridSpec(
            num_scalar_prefetch=2,
            grid=(len(groups),),
            in_specs=[
                pl.BlockSpec(p.shape, lambda g, *_: (0, 0), pipeline_mode=pl.Buffered(1))
                for p in pieces
            ]
            + [pl.BlockSpec(memory_space=pl.ANY)] * len(given),
            out_specs=specs,
        ),
        out_shape=tuple(jax.ShapeDtypeStruct(shape, F32) for shape in shapes),
        input_output_aliases={first + k: k for k in range(len(given))},
        cost_estimate=takes(len(pieces)),
        compiler_params=pltpu.CompilerParams(vmem_limit_bytes=48 << 20),
        name="place",
    )(order, rel, *pieces, *given)


def flat_matrices(placed, layout):
    results = []
    for (kind, _, _), out in zip(layout, placed):
        if len(out.shape) == 3 and kind == "cols":
            out = out.transpose(1, 0, 2).reshape(out.shape[1], -1)
        elif len(out.shape) == 3:
            out = out.reshape(-1, out.shape[2])
        results.append(out)
    return results


class Ring:
    def __init__(self, axis):
        self.axis = axis
        self.n = n = lax.axis_size(axis)
        me = lax.axis_index(axis)
        self.pos = jnp.where(me % 2 == 0, me // 2, n - 1 - me // 2)
        order = list(range(0, n, 2)) + list(range(1, n, 2))[::-1]
        self.up = [(order[i], order[(i + 1) % n]) for i in range(n)]
        self.down = [(b, a) for a, b in self.up]
        self.walk = [0]
        for step in range(1, n // 2):
            self.walk += [-step, step]
        self.walk.append(n // 2)
        p = (self.pos + jnp.asarray(self.walk, jnp.int32) + n) % n
        self.order = jnp.where(p < n // 2, 2 * p, 2 * (n - 1 - p) + 1)

    def shard(self, distance):
        n = self.n
        p = (self.pos + distance + n) % n
        return jnp.where(p < n // 2, 2 * p, 2 * (n - 1 - p) + 1)

    def send_up(self, value):
        return lax.ppermute(value, self.axis, self.up)

    def send_down(self, value):
        return lax.ppermute(value, self.axis, self.down)

    def gather(self, value):
        half = value.shape[0] // 2
        above = below = value
        out = [value]
        for _ in range(1, self.n // 2):
            below, above = yield self.send_up(below), self.send_down(above)
            out += [below, above]
        return out + list((yield self.send_up(below[:half]), self.send_down(above[half:])))

    def reduce(self, *values):
        rows = values[0].shape[0] // self.n
        half = rows // 2
        mid = self.n // 2

        def term(distance, first=0, count=rows):
            at = self.shard(distance) * rows + first
            parts = [lax.dynamic_slice_in_dim(v, at, count, 0).astype(F32) for v in values]
            return parts[0] if len(parts) == 1 else jnp.concatenate(parts, axis=1)

        up = self.send_up(term(mid, 0, half).astype(BF16))
        down = self.send_down(term(mid, half, rows - half).astype(BF16))
        for step in range(mid - 1, 0, -1):
            up, down = yield up, down
            mine = term(step)
            other = term(-step)
            if step == mid - 1:
                mine = jnp.concatenate([mine[:half] + up.astype(F32), mine[half:]], axis=0)
                other = jnp.concatenate([other[:half], other[half:] + down.astype(F32)], axis=0)
            else:
                mine = mine + up.astype(F32)
                other = other + down.astype(F32)
            up = self.send_up(mine.astype(BF16))
            down = self.send_down(other.astype(BF16))
        up, down = yield up, down
        return (term(0) + up.astype(F32) + down.astype(F32)).astype(BF16)


class Walk:
    def __init__(self, steps):
        self.steps = steps
        self.result = None
        self.moving = next(steps)

    def go(self, arrived):
        try:
            self.moving = self.steps.send(arrived)
        except StopIteration as end:
            self.moving = None
            self.result = end.value


def milestone(*values):
    return lax.optimization_barrier(values)


def bits(n):
    return [1 << b for b in range(n.bit_length() - 1)]


def swap(value, axis, bit):
    n = lax.axis_size(axis)
    return lax.ppermute(value, axis, [(i, i ^ bit) for i in range(n)])


def reach(n):
    masks = [0]
    for bit in reversed(bits(n)):
        masks = masks + [m | bit for m in masks]
    return masks


def cube_gather(value, axis, n=None):
    held = [value]
    for bit in reversed(bits(n or lax.axis_size(axis))):
        held = held + [swap(block, axis, bit) for block in held]
    return held


class Scatter:
    def __init__(self, tiers, axis):
        self.axis = axis
        tiers = list(tiers)
        self.left = self.top = len(tiers) - 1
        self.size = tiers[0].shape[0]
        self.terms = [[t] for t in tiers]
        self.moving = None

    def send(self):
        parts = self.terms[self.left]
        away = parts[0] if len(parts) == 1 else add_up(parts).astype(BF16)
        self.moving = swap(away, self.axis, 1 << (self.top - self.left))

    def take(self):
        for j, (lo, hi) in enumerate(tier_bounds(1 << (self.left - 1))):
            self.terms[j].append(self.moving[lo * self.size : hi * self.size])
        self.left -= 1


def add_up(terms):
    return functools.reduce(jnp.add, [t.astype(F32) for t in terms])


def cube_exchange(value, axis, dim):
    me = lax.axis_index(axis)
    n = lax.axis_size(axis)
    size = value.shape[dim] // n
    out = []
    for mask in reach(n):
        block = lax.dynamic_slice_in_dim(value, (me ^ mask) * size, size, dim)
        if mask:
            block = lax.ppermute(block, axis, [(i, i ^ mask) for i in range(n)])
        out.append(block)
    return out


def shards(
    tokens,
    cotangent,
    lengths,
    deal,
    ln1_gain,
    ln1_shift,
    w_qkv,
    bias_qv,
    w_out,
    bias_out,
    ln2_gain,
    ln2_shift,
    w_fc,
    bias_fc,
    w_proj,
    bias_proj,
):
    x = tokens[0]
    dy = cotangent[0]
    rows, width = x.shape
    ring = Ring("seq")
    n_seq = ring.n
    n_fsdp = lax.axis_size("fsdp")
    me_seq = lax.axis_index("seq")
    me_fsdp = lax.axis_index("fsdp")
    total_rows = rows * n_seq
    heads = H // n_seq
    hd = heads * HEAD
    wide = w_fc.shape[1]
    share = w_qkv.shape[0]
    groups = jnp.arange(n_fsdp, dtype=jnp.int32)
    picked = (deal[:, None] == groups[None, :]).astype(jnp.int32)
    home_rows = jnp.sum(picked[:, :, None] * lengths[None], axis=1)
    row = jnp.sum(jnp.where((groups == me_fsdp)[:, None], home_rows, 0), axis=0)
    last = lengths.shape[1] - 1
    masks = reach(n_fsdp)
    rel = me_fsdp ^ jnp.asarray(masks, jnp.int32)

    own_cols = lax.dynamic_slice_in_dim(w_qkv, me_seq * 3 * hd, 3 * hd, 1)
    small = (ln1_gain, ln1_shift, bias_qv, bias_out, ln2_gain, ln2_shift, bias_proj)
    small = jnp.concatenate(small)
    extra = -(-small.shape[0] // (3 * hd * 16)) * 16
    tail = jnp.pad(small, (0, extra * 3 * hd - small.shape[0])).reshape(extra, 3 * hd)

    walk = Walk(ring.gather(x))
    wfc = lax.all_gather(w_fc, "fsdp", axis=0, tiled=True)
    dy_all = lax.all_gather(dy, "fsdp", axis=0, tiled=True)
    moved, mine = milestone(walk.moving, (own_cols, tail))
    walk.go(moved)
    packs = [jnp.concatenate(mine, axis=0)]
    held = None
    for bit in reversed(bits(n_fsdp)):
        packs = packs + [swap(p, "fsdp", bit) for p in packs]

    def projected(blocks):
        nonlocal held
        for k in blocks:
            if k < n_seq - 1:
                at = ring.shard(ring.walk[k])
            else:
                at = ring.shard(n_seq // 2) * 2 + (k - n_seq + 1)
            held = project(
                at, pieces[k], gain_one, shift_one, w_roles, b_own, total_rows, held
            )

    moved_first = moved
    moved, packs, w_out = milestone(walk.moving, packs, w_out)
    walk.go(moved)
    top = n_fsdp // 2
    wout_far = swap(w_out, "fsdp", top)

    w_own = jnp.zeros((width, 3 * hd), BF16)
    vectors = jnp.zeros((n_fsdp, tail.size), BF16)
    for k, p in enumerate(packs):
        index = me_fsdp ^ masks[k]
        w_own = lax.dynamic_update_slice_in_dim(w_own, p[:share], index * share, 0)
        vectors = lax.dynamic_update_slice_in_dim(vectors, p[share:].reshape(1, -1), index, 0)
    w_roles = w_own.reshape(width, heads, 3, HEAD).transpose(0, 2, 1, 3).reshape(width, 3 * hd)
    cut = []
    at = 0
    for count in (share, share, 2 * share, share, share, share, share):
        cut.append(vectors[:, at : at + count].reshape(1, -1).astype(F32))
        at += count
    gain_one, shift_one, bqv, bout, gain_two, shift_two, bproj = cut
    b_own = lax.dynamic_index_in_dim(bqv.reshape(n_seq, heads, 2, HEAD), me_seq, 0, keepdims=False)
    b_own = jnp.concatenate(
        [b_own[:, 0].reshape(1, hd), jnp.zeros((1, hd), F32), b_own[:, 1].reshape(1, hd)], axis=1
    )

    pieces = [x] + list(moved_first) + list(moved)
    done = 0
    while walk.result is None:
        ready = len(pieces)
        projected(range(done, ready))
        done = ready
        moved, held = milestone(walk.moving, held)
        walk.go(moved)
        pieces += list(moved)
    projected(range(done, len(pieces)))
    held, wout_far = milestone(held, wout_far)
    x_all, qkv = held

    attended, lse = attention_forward(row, qkv, rows)
    wout = jnp.zeros((width, width), BF16)
    wout_pieces = cube_gather(w_out, "fsdp", top) + cube_gather(wout_far, "fsdp", top)
    for k, mask in enumerate(reach(top) + [m | top for m in reach(top)]):
        wout = lax.dynamic_update_slice_in_dim(wout, wout_pieces[k], (me_fsdp ^ mask) * share, 0)
    merged = lax.all_to_all(
        attended.reshape(n_seq, rows, hd), "seq", split_axis=0, concat_axis=0, tiled=True
    )

    merged, wout = milestone(merged, wout)

    ends = jnp.sum(home_rows[:, :last], axis=1)

    def valid_counts(index):
        of = jnp.sum(jnp.where(index[:, None] == groups[None, :], ends[None, :], 0), axis=1)
        return jnp.clip(of - me_seq * rows, 0, rows)

    near = me_fsdp ^ jnp.asarray(reach(top), jnp.int32)
    far = near ^ top
    near_far = jnp.concatenate([near, far])
    counts = valid_counts(near)
    low, middle, square_attn = attend_out(
        counts, merged, x, wout, bout, gain_two, shift_two
    )

    bfc = bias_fc.astype(F32)[None]
    low_far = swap(low, "fsdp", top)
    low_near = cube_gather(low, "fsdp", top)
    halves = len(tier_bounds(top))
    results = feed(rel, near, counts, low_near, dy_all, wfc, w_proj, bfc, True)
    two_near, feed_near = Scatter(results[:halves], "fsdp"), results[halves:]
    low_far, feed_near = milestone(low_far, feed_near)
    while two_near.left:
        two_near.send()
        two_near.take()
    low_far = cube_gather(low_far, "fsdp", top)
    results = feed(rel, far, valid_counts(far), low_far, dy_all, wfc, w_proj, bfc, False)
    two_far, feed_far = Scatter(results[:halves], "fsdp"), results[halves:]
    while two_far.left:
        two_far.send()
        two_far.moving, feed_far, two_near.terms = milestone(
            two_far.moving, feed_far, two_near.terms
        )
        two_far.take()

    far_two = swap(add_up(two_far.terms[0]).astype(BF16), "fsdp", top)
    gproj, gfc, gbfc = feed_grads(feed_near, feed_far, low_near + low_far, n_seq)
    far_two, gproj, gfc = milestone(far_two, gproj, gfc)

    thin = share // n_seq
    blocks = wide // width
    gfc = gfc.reshape(n_seq * n_fsdp * thin, wide // n_fsdp)
    together = gfc.shape[0] == gproj.shape[0]
    walk = Walk(ring.reduce(gproj, gfc) if together else ring.reduce(gfc))
    results = middle_back(
        rel, counts, merged, middle, dy, gain_two, wout, two_near.terms[0] + [far_two]
    )
    tiers = len(tier_bounds(n_fsdp))
    gout, (d_middle, d_merged, sums_two) = results[:tiers], results[tiers:]
    moved, d_merged, gout = milestone(walk.moving, d_merged, gout)

    d_heads = lax.all_to_all(d_merged, "seq", split_axis=0, concat_axis=0, tiled=True)
    walk.go(moved)
    gout = Scatter(gout, "fsdp")
    hidden = (feed_near[0], feed_far[0])
    while gout.left > 1:
        gout.send()
        gout.moving, hidden = milestone(gout.moving, hidden)
        gout.take()
    gout.send()
    mlp_near = Scatter(feed_out(hidden[0], w_proj, rows, True), "fsdp")
    mlp_far = Scatter(feed_out(hidden[1], w_proj, rows, False), "fsdp")
    while mlp_near.left:
        mlp_near.send()
        mlp_far.send()
        mlp_near.take()
        mlp_far.take()
    mlp_far = add_up(mlp_far.terms[0]).astype(BF16)
    gout.moving, mlp_far, mlp_near.terms = milestone(gout.moving, mlp_far, mlp_near.terms)
    gout.take()
    out_walk = Walk(ring.reduce(add_up(gout.terms[0])))
    moved, d_heads, out_moved = milestone(walk.moving, d_heads, out_walk.moving)

    walk.go(moved)
    out_walk.go(out_moved)
    mlp_far = swap(mlp_far, "fsdp", top)
    d_own = attention_backward(row, qkv, attended, lse, d_heads.reshape(total_rows, hd), rows)
    moved, out_moved, d_own, mlp_far = milestone(walk.moving, out_walk.moving, d_own, mlp_far)
    d_packed = lax.all_to_all(
        d_own.reshape(n_seq, rows, 3 * hd), "seq", split_axis=0, concat_axis=0, tiled=True
    )
    walk.go(moved)
    out_walk.go(out_moved)
    w_qkv = milestone(w_qkv, d_own)[0]
    w_all = lax.all_gather(w_qkv, "fsdp", axis=0, tiled=True)
    grad_qkv, sums_one, d_sums = qkv_grads(x_all, d_own, w_own, gain_one, shift_one, rows)
    while walk.result is None:
        moved, out_moved, grad_qkv, sums_one, d_sums, mlp_far = milestone(
            walk.moving, out_walk.moving, grad_qkv, sums_one, d_sums, mlp_far
        )
        walk.go(moved)
        out_walk.go(out_moved)
    mine = walk.result
    if together:
        mine_proj, mine_fc = mine[:, :width], mine[:, width:]
    else:
        mine_fc = mine
        walk = Walk(ring.reduce(gproj))
        while walk.result is None:
            walk.go(walk.moving)
        mine_proj = walk.result
    mine_proj = mine_proj.reshape(blocks, thin, width).transpose(1, 0, 2).reshape(thin, wide)
    mine_fc = cube_exchange(mine_fc, "fsdp", 0)
    parts = [
        lax.dynamic_slice_in_dim(grad_qkv, (me_fsdp ^ mask) * share, share, 0) for mask in masks
    ]
    parts = [jnp.concatenate(parts[lo:hi], axis=0) for lo, hi in tier_bounds(n_fsdp)]
    parts = Scatter(parts, "fsdp")
    while parts.left > 1:
        parts.send()
        parts.take()
    while out_walk.result is None:
        parts.terms, mine_fc, out_moved = milestone(parts.terms, mine_fc, out_walk.moving)
        out_walk.go(out_moved)
    parts.send()
    parts.take()
    share_qkv = add_up(parts.terms[0]).astype(BF16)
    beside_it = share_qkv.reshape(n_seq, thin, 3 * hd).transpose(1, 0, 2).reshape(thin, -1)
    mine = jnp.concatenate([mine_proj] + mine_fc + [out_walk.result, beside_it], axis=1)

    mine, d_packed, mlp_far, sums_one, d_sums = milestone(
        mine, d_packed, mlp_far, sums_one, d_sums
    )
    walk = Walk(ring.gather(mine))
    output, square_ends = finish(counts, middle, bproj, mlp_near.terms[0] + [mlp_far])
    squares = jnp.concatenate([square_ends[:1], square_attn, square_ends[1:]], axis=0)
    squares = jnp.concatenate([jnp.sum(squares, axis=1), counts[:1].astype(F32)])[None]
    squares = jnp.concatenate([squares, jnp.zeros((n_fsdp - 1, 4), F32)], axis=0)
    grad_bfc = lax.dynamic_update_slice_in_dim(
        jnp.zeros((n_fsdp, wide // n_fsdp), F32), gbfc, me_fsdp, 0
    )
    d_sums = d_sums.reshape(heads, 3, HEAD)
    d_sums = jnp.stack([d_sums[:, 0], d_sums[:, 2]], axis=1).reshape(1, 2 * hd)
    grad_bqv = lax.dynamic_update_slice_in_dim(
        jnp.zeros((n_seq, 2 * hd), F32), d_sums, me_seq, 0
    )
    vectors = [sums_one[0], sums_one[1], grad_bqv, *[sums_two[k] for k in range(4)], grad_bfc]
    vectors = [v.reshape(n_fsdp, -1) for v in vectors]
    sums = jnp.concatenate(vectors + [squares], axis=1)
    for bit in bits(n_fsdp):
        sums = sums + swap(sums, "fsdp", bit)
    hops = bits(n_seq)
    arrived = [mine]

    layout = (
        ("rows", wide, blocks),
        ("rel", wide, n_fsdp),
        ("rows", width, 1),
        ("cols", 3 * width, n_seq),
    )
    steps = n_seq // 2
    input_grad = placed = own = squares = None
    for step in range(steps):
        ahead = steps - step
        count = -(-len(hops) // max(1, ahead - 2))
        for bit in hops[:count]:
            sums = sums + swap(sums, "seq", bit)
        hops = hops[count:]
        if ahead == min(3, steps):
            input_grad = input_gradient(d_packed, w_all, x, gain_one, d_middle)
        if ahead == min(2, steps):
            own = lax.dynamic_slice_in_dim(sums, me_fsdp, 1, 0)[0]
            squared = sums[0, -4:]
            squares = jnp.sqrt(squared[:3] / (squared[3] * width))
        if ahead == 1:
            placed = place(ring.order, rel, arrived, layout, n_seq)
        moved, sums, input_grad, placed, own, squares, output = milestone(
            walk.moving, sums, input_grad, placed, own, squares, output
        )
        if ahead > 1:
            arrived += list(moved)
        walk.go(moved)
    stats = squares
    farthest = ring.shard(n_seq // 2).reshape(1)
    placed = place(farthest, rel, walk.result[-2:], layout, n_seq, placed)
    grad_proj, grad_fc, grad_out, grad_wqkv = flat_matrices(placed, layout)

    shares = []
    at = 0
    for vector in vectors:
        shares.append(own[at : at + vector.shape[1]])
        at += vector.shape[1]
    g1, s1, bqv, bout, g2, s2, bproj, bfc = shares
    return (
        output[None],
        input_grad[None],
        g1,
        s1,
        grad_wqkv,
        bqv,
        grad_out,
        bout,
        g2,
        s2,
        grad_fc,
        bfc,
        grad_proj,
        bproj,
        stats,
    )


def solution(mesh):
    rows_split = P("fsdp", "seq", None)
    matrix = P("fsdp", None)
    vector = P("fsdp")
    params = (
        vector,
        vector,
        matrix,
        vector,
        matrix,
        vector,
        vector,
        vector,
        matrix,
        vector,
        matrix,
        vector,
    )
    return jax.shard_map(
        shards,
        mesh=mesh,
        in_specs=(rows_split, rows_split, P(), P()) + params,
        out_specs=(rows_split, rows_split) + params + (P(),),
        check_vma=False,
    )
```

```python
import functools

import jax
import jax.numpy as jnp
from jax import lax
from jax.experimental import pallas as pl
from jax.experimental.pallas import tpu as pltpu
from jax.sharding import PartitionSpec as P

H = 16
HEAD = 64
NT = (((1,), (1,)), ((), ()))
TN = (((0,), (0,)), ((), ()))
F32 = jnp.float32
BF16 = jnp.bfloat16


def seg_starts(len_ref, segs, place):
    start = jnp.zeros_like(place)
    end = jnp.int32(0)
    for k in range(segs - 1):
        end = end + len_ref[k]
        start = jnp.where(place >= end, end, start)
    return start


def head_part(block, h, heads):
    if heads == 1:
        return block
    lane = lax.broadcasted_iota(jnp.int32, block.shape, 1)
    return jnp.where((lane >= h * HEAD) & (lane < (h + 1) * HEAD), block, jnp.zeros_like(block))


def beside(block, heads):
    return jnp.concatenate([head_part(block, h, heads) for h in range(heads)], axis=0)


def diagonal(wide, heads):
    block = wide.shape[1] // heads
    parts = [
        wide[h * HEAD : (h + 1) * HEAD, h * block : (h + 1) * block] for h in range(heads)
    ]
    return jnp.concatenate(parts, axis=0)


DIRECT = 4


def visit(i, block, segs, len_ref, direct, loop):
    r0 = pl.multiple_of(i * block, block)
    place = r0 + lax.broadcasted_iota(jnp.int32, (1, block), 1)
    start = seg_starts(len_ref, segs, place)
    first = seg_starts(len_ref, segs, r0) // block
    for n in range(1, DIRECT + 1):

        @pl.when(i - first + 1 == n)
        def _():
            direct(n, r0, place, start, pl.multiple_of((i - n + 1) * block, block))

    @pl.when(i - first + 1 > DIRECT)
    def _():
        loop(r0, place, start, first)


def seen(c0, count, place, start, heads):
    key_pos = c0 + lax.broadcasted_iota(jnp.int32, (count, place.shape[1]), 0)
    ok = (key_pos >= start) & (key_pos <= place)
    return jnp.concatenate([ok] * heads, axis=1)


def forward_kernel(heads, block, segs, len_ref, qkv_ref, o_ref, lse_ref, vt_ref):
    hd = heads * HEAD
    steps = qkv_ref.shape[0] // block

    def flip(i, _):
        at = pl.multiple_of(i * block, block)
        vt_ref[:, pl.ds(at, block)] = qkv_ref[pl.ds(at, block), 2 * hd : 3 * hd].T
        return 0

    lax.fori_loop(0, steps, flip, 0)

    def queries(r0):
        return beside(qkv_ref[pl.ds(r0, block), 0:hd] * jnp.asarray(HEAD**-0.5, BF16), heads)

    def store(r0, top, total, acc):
        lse = top + jnp.log(total)
        for h in range(heads):
            lse_ref[h : h + 1, pl.ds(r0, block)] = lse[:, h * block : (h + 1) * block]
        o_ref[pl.ds(r0, block), :] = diagonal(acc / total, heads).T.astype(BF16)

    def direct(n, r0, place, start, c0):
        keys = pl.ds(c0, n * block)
        s = lax.dot_general(qkv_ref[keys, hd : 2 * hd], queries(r0), NT, preferred_element_type=F32)
        s = jnp.where(seen(c0, n * block, place, start, heads), s, -1e30)
        top = jnp.max(s, axis=0, keepdims=True)
        p = jnp.exp(s - top)
        total = jnp.sum(p, axis=0, keepdims=True)
        acc = jnp.dot(vt_ref[:, keys], p.astype(BF16), preferred_element_type=F32)
        store(r0, top, total, acc)

    def loop(r0, place, start, first):
        q = queries(r0)

        def key_step(j, carry):
            top, total, acc = carry
            c0 = pl.multiple_of(j * block, block)
            keys = pl.ds(c0, block)
            s = lax.dot_general(qkv_ref[keys, hd : 2 * hd], q, NT, preferred_element_type=F32)
            s = jnp.where(seen(c0, block, place, start, heads), s, -1e30)
            new = jnp.maximum(top, jnp.max(s, axis=0, keepdims=True))
            p = jnp.exp(s - new)
            shrink = jnp.exp(top - new)
            total = total * shrink + jnp.sum(p, axis=0, keepdims=True)
            acc = acc * shrink + jnp.dot(
                vt_ref[:, keys], p.astype(BF16), preferred_element_type=F32
            )
            return new, total, acc

        wide = heads * block
        init = (
            jnp.full((1, wide), -1e30, F32),
            jnp.zeros((1, wide), F32),
            jnp.zeros((hd, wide), F32),
        )
        store(r0, *lax.fori_loop(first, r0 // block + 1, key_step, init))

    def query_step(i, _):
        visit(i, block, segs, len_ref, direct, loop)
        return 0

    lax.fori_loop(0, steps, query_step, 0)


def backward_kernel(
    heads,
    block,
    segs,
    len_ref,
    qkv_ref,
    o_ref,
    lse_ref,
    do_ref,
    d_ref,
    kt_ref,
    dq_ref,
    dk_ref,
    dv_ref,
):
    hd = heads * HEAD
    steps = qkv_ref.shape[0] // block

    def flip(i, _):
        at = pl.multiple_of(i * block, block)
        kt_ref[:, pl.ds(at, block)] = qkv_ref[pl.ds(at, block), hd : 2 * hd].T
        dk_ref[pl.ds(at, block), :] = jnp.zeros((block, hd), F32)
        dv_ref[pl.ds(at, block), :] = jnp.zeros((block, hd), F32)
        return 0

    lax.fori_loop(0, steps, flip, 0)

    def operands(r0):
        rows = pl.ds(r0, block)
        q = beside(qkv_ref[rows, 0:hd] * jnp.asarray(HEAD**-0.5, BF16), heads)
        do = do_ref[rows, :]
        both = (do.astype(F32) * o_ref[rows, :].astype(F32)).T
        delta = [
            jnp.sum(both[h * HEAD : (h + 1) * HEAD], axis=0, keepdims=True) for h in range(heads)
        ]
        lse = [lse_ref[h : h + 1, rows] for h in range(heads)]
        return q, beside(do, heads), jnp.concatenate(delta, axis=1), jnp.concatenate(lse, axis=1)

    def part(c0, count, place, start, q, do, delta, lse):
        keys = pl.ds(c0, count)
        s = lax.dot_general(qkv_ref[keys, hd : 2 * hd], q, NT, preferred_element_type=F32)
        p = jnp.where(seen(c0, count, place, start, heads), jnp.exp(s - lse), 0.0)
        dp = lax.dot_general(
            qkv_ref[keys, 2 * hd : 3 * hd], do, NT, preferred_element_type=F32
        )
        ds = (p * (dp - delta)).astype(BF16)
        dv_ref[keys, :] += jnp.dot(p.astype(BF16), do, preferred_element_type=F32)
        dk_ref[keys, :] += jnp.dot(ds, q, preferred_element_type=F32)
        return jnp.dot(kt_ref[:, keys], ds, preferred_element_type=F32)

    def store(r0, dq):
        dq_ref[pl.ds(r0, block), :] = (diagonal(dq, heads) * HEAD**-0.5).T

    def direct(n, r0, place, start, c0):
        store(r0, part(c0, n * block, place, start, *operands(r0)))

    def loop(r0, place, start, first):
        given = operands(r0)

        def key_step(j, dq):
            return dq + part(pl.multiple_of(j * block, block), block, place, start, *given)

        init = jnp.zeros((hd, heads * block), F32)
        store(r0, lax.fori_loop(first, r0 // block + 1, key_step, init))

    def query_step(i, _):
        visit(i, block, segs, len_ref, direct, loop)
        return 0

    lax.fori_loop(0, steps, query_step, 0)

    def finish_rows(i, _):
        rows = pl.ds(pl.multiple_of(i * block, block), block)
        roles = [ref[rows, :] for ref in (dq_ref, dk_ref, dv_ref)]
        parts = [v[:, h * HEAD : (h + 1) * HEAD] for h in range(heads) for v in roles]
        d_ref[rows, :] = jnp.concatenate(parts, axis=1).astype(BF16)
        return 0

    lax.fori_loop(0, steps, finish_rows, 0)


def takes(us):
    return pl.CostEstimate(flops=int(us * 3.30e9), bytes_accessed=1 << 20, transcendentals=0)


VM = pl.BlockSpec(memory_space=pltpu.VMEM)
SM = pl.BlockSpec(memory_space=pltpu.SMEM)
LIMIT = 32 << 20


def attention_forward(row, qkv, block):
    rows, wide = qkv.shape
    hd = wide // 3
    heads = hd // HEAD
    return pl.pallas_call(
        functools.partial(forward_kernel, heads, block, row.shape[0]),
        out_shape=(
            jax.ShapeDtypeStruct((rows, hd), BF16),
            jax.ShapeDtypeStruct((heads, rows), F32),
        ),
        in_specs=[SM, VM],
        out_specs=(VM, VM),
        scratch_shapes=[pltpu.VMEM((hd, rows), BF16)],
        compiler_params=pltpu.CompilerParams(vmem_limit_bytes=LIMIT),
        cost_estimate=takes(14),
        name="attention_forward",
    )(row, qkv)


def attention_backward(row, qkv, o, lse, do, block):
    rows, wide = qkv.shape
    hd = wide // 3
    heads = hd // HEAD
    return pl.pallas_call(
        functools.partial(backward_kernel, heads, block, row.shape[0]),
        out_shape=jax.ShapeDtypeStruct((rows, wide), BF16),
        in_specs=[SM] + [VM] * 4,
        out_specs=VM,
        scratch_shapes=[pltpu.VMEM((hd, rows), BF16)] + [pltpu.VMEM((rows, hd), F32)] * 3,
        compiler_params=pltpu.CompilerParams(vmem_limit_bytes=44 << 20),
        cost_estimate=takes(21),
        name="attention_backward",
    )(row, qkv, o, lse, do)


def tier_bounds(n):
    bounds = [(0, 1)]
    while bounds[-1][1] < n:
        bounds.append((bounds[-1][1], 2 * bounds[-1][1]))
    return bounds


def norm_parts(value):
    mean = jnp.mean(value, axis=-1, keepdims=True)
    centred = value - mean
    spread = jnp.mean(centred * centred, axis=-1, keepdims=True)
    scale = lax.rsqrt(spread + 1e-05)
    return centred * scale, scale


def project_kernel(at_ref, x_ref, gain_ref, shift_ref, w_ref, b_ref, *rest):
    x_out, qkv_out = rest[-2:]
    x = x_ref[...]
    n, _ = norm_parts(x.astype(F32))
    low = (n * gain_ref[...] + shift_ref[...]).astype(BF16)
    mixed = jnp.dot(low, w_ref[...], preferred_element_type=F32) + b_ref[...]
    x_out[...] = x
    qkv_out[...] = mixed.astype(BF16)


def project(at, x, gain, shift, w, b, total, held):
    rows, width = x.shape
    wide = w.shape[1]

    def fixed(shape):
        return pl.BlockSpec(shape, lambda i, at: (0, 0))

    given = () if held is None else held
    return pl.pallas_call(
        project_kernel,
        grid_spec=pltpu.PrefetchScalarGridSpec(
            num_scalar_prefetch=1,
            grid=(1,),
            in_specs=[
                fixed((rows, width)),
                fixed((1, width)),
                fixed((1, width)),
                fixed((width, wide)),
                fixed((1, wide)),
            ]
            + [pl.BlockSpec(memory_space=pl.ANY)] * len(given),
            out_specs=[
                pl.BlockSpec((rows, width), lambda i, at: (at[0], 0)),
                pl.BlockSpec((rows, wide), lambda i, at: (at[0], 0)),
            ],
        ),
        out_shape=(
            jax.ShapeDtypeStruct((total, width), BF16),
            jax.ShapeDtypeStruct((total, wide), BF16),
        ),
        input_output_aliases={6: 0, 7: 1} if given else {},
        cost_estimate=takes(2),
        compiler_params=pltpu.CompilerParams(vmem_limit_bytes=24 << 20),
        name="project",
    )(at.reshape(1), x, gain, shift, w, b, *given)


def attend_out_kernel(
    count_ref,
    merged_ref,
    x_ref,
    wout_ref,
    bout_ref,
    gain_ref,
    shift_ref,
    low_ref,
    middle_ref,
    stat_ref,
):
    rows = x_ref.shape[0]
    merged = jnp.concatenate([merged_ref[k] for k in range(merged_ref.shape[0])], axis=1)
    attn = jnp.dot(merged, wout_ref[...], preferred_element_type=F32) + bout_ref[...]
    middle = x_ref[...].astype(F32) + attn
    middle_ref[...] = middle
    n, _ = norm_parts(middle)
    low_ref[...] = (n * gain_ref[...] + shift_ref[...]).astype(BF16)
    valid = lax.broadcasted_iota(jnp.int32, (rows, 1), 0) < count_ref[0]
    stat_ref[...] = jnp.sum(jnp.where(valid, attn * attn, 0.0), axis=0, keepdims=True)


def attend_out(count, merged, x, wout, bout, gain, shift):
    rows, width = x.shape
    return pl.pallas_call(
        attend_out_kernel,
        in_specs=[SM] + [VM] * 6,
        out_specs=(VM,) * 3,
        out_shape=(
            jax.ShapeDtypeStruct((rows, width), BF16),
            jax.ShapeDtypeStruct((rows, width), F32),
            jax.ShapeDtypeStruct((1, width), F32),
        ),
        cost_estimate=takes(5),
        compiler_params=pltpu.CompilerParams(vmem_limit_bytes=40 << 20),
        name="attend_out",
    )(count, merged, x, wout, bout, gain, shift)


GELU = 0.7978845608028654


def feed_kernel(
    packs, rel_ref, which_ref, count_ref, bfc_ref, wproj_ref, wfc_ref, dy_ref, *rest
):
    low_refs, rest = rest[:packs], rest[packs:]
    tiers = tier_bounds(packs)
    dtwo_refs, rest = rest[: len(tiers)], rest[len(tiers) :]
    hidden_ref, di_ref, dmlp_ref, low_s = rest
    step = pl.program_id(0)
    rows = low_s.shape[0]
    valid = lax.broadcasted_iota(jnp.int32, (rows, 1), 0) < count_ref[step]

    for k in range(packs):

        @pl.when(step == k)
        def _():
            low_s[...] = low_refs[k][...]

    dy = dy_ref[...]
    dmlp_ref[...] = jnp.where(valid, dy, jnp.zeros_like(dy))

    u = jnp.dot(low_s[...], wfc_ref[...], preferred_element_type=F32) + bfc_ref[...]
    dh = lax.dot_general(dmlp_ref[...], wproj_ref[...], NT, preferred_element_type=F32)
    square = u * u
    t = jnp.tanh(GELU * u * (1.0 + 0.044715 * square))
    side = 0.5 * (1.0 + t)
    hidden_ref[...] = (u * side).astype(BF16)
    slope = side + 0.5 * u * (1.0 - t * t) * (GELU * (1.0 + 3 * 0.044715 * square))
    di = (dh * slope).astype(BF16)
    di_ref[...] = di
    dtwo = lax.dot_general(di, wfc_ref[...], NT, preferred_element_type=F32)
    for (lo, hi), out_ref in zip(tiers, dtwo_refs):

        @pl.when((step >= lo) & (step < hi))
        def _():
            out_ref[...] = dtwo.astype(out_ref.dtype)


def feed(rel, which, counts, low_pieces, dy_all, wfc, wproj, bfc, own):
    rows, width = low_pieces[0].shape
    packs = len(low_pieces)
    wide = wproj.shape[0]
    tiers = tier_bounds(packs)

    def whole(*shape):
        return pl.BlockSpec(shape, lambda g, *_: (0,) * len(shape), pipeline_mode=pl.Buffered(1))

    def tier(lo, hi):
        return pl.BlockSpec((rows, width), lambda g, *_: (jnp.clip(g - lo, 0, hi - lo - 1), 0))

    each = pl.BlockSpec((rows, wide), lambda g, *_: (g, 0))
    return pl.pallas_call(
        functools.partial(feed_kernel, packs),
        grid_spec=pltpu.PrefetchScalarGridSpec(
            num_scalar_prefetch=3,
            grid=(packs,),
            in_specs=[
                whole(1, wide),
                whole(wide, width),
                pl.BlockSpec(
                    (width, wide), lambda g, rel, *_: (0, rel[0]), pipeline_mode=pl.Buffered(1)
                ),
                pl.BlockSpec((rows, width), lambda g, rel, which, _: (which[g], 0)),
            ]
            + [whole(rows, width)] * packs,
            out_specs=[tier(lo, hi) for lo, hi in tiers]
            + [each, each, pl.BlockSpec((rows, width), lambda g, *_: (g, 0))],
            scratch_shapes=[pltpu.VMEM((rows, width), BF16)],
        ),
        out_shape=tuple(
            [
                jax.ShapeDtypeStruct(((hi - lo) * rows, width), F32 if lo == 0 and own else BF16)
                for lo, hi in tiers
            ]
            + [jax.ShapeDtypeStruct((packs * rows, wide), BF16)] * 2
            + [jax.ShapeDtypeStruct((packs * rows, width), BF16)]
        ),
        cost_estimate=takes(10),
        compiler_params=pltpu.CompilerParams(vmem_limit_bytes=52 << 20),
        name="feed",
    )(rel, which, counts, bfc, wproj, wfc, dy_all, *low_pieces)


def feed_grads_kernel(
    near, n_fsdp, hid_a, hid_b, di_a, di_b, dmlp_a, dmlp_b, *rest
):
    low_refs, rest = rest[:n_fsdp], rest[n_fsdp:]
    gproj_ref, gfc_ref, gbfc_ref = rest[:3]
    scratch = rest[3:]
    step = pl.program_id(0)
    rows, wide = hid_a.shape
    n_seq, _, thin, _ = gfc_ref.shape
    share = n_seq * thin

    @pl.when(step == 0)
    def _():
        gbfc_ref[...] = jnp.zeros_like(gbfc_ref)

    def store_fc(i, g):
        for k in range(n_seq):
            gfc_ref[k, i] = g[k * thin : (k + 1) * thin]

    for k in range(n_fsdp):
        hid_ref, di_ref, dmlp_ref = (hid_a, di_a, dmlp_a) if k < near else (hid_b, di_b, dmlp_b)

        @pl.when(step == k)
        def _():
            di = di_ref[...]
            gbfc_ref[...] += jnp.sum(di.astype(F32), axis=0, keepdims=True)
            if len(scratch) == 2:
                proj_s, fc_s = scratch
                proj = jnp.dot(hid_ref[...].T, dmlp_ref[...], preferred_element_type=F32)
                fc = jnp.dot(low_refs[k][...].T, di, preferred_element_type=F32)
                proj_s[...] = proj if k == 0 else proj_s[...] + proj
                fc_s[...] = fc if k == 0 else fc_s[...] + fc
            else:
                hiddent_s, di_s, dmlp_s, lowt_s = scratch
                at = slice(k * rows, (k + 1) * rows)
                hiddent_s[:, at] = hid_ref[...].T
                di_s[at, :] = di
                dmlp_s[at, :] = dmlp_ref[...]
                lowt_s[:, at] = low_refs[k][...].T

    @pl.when(step == n_fsdp - 1)
    def _():
        if len(scratch) == 2:
            proj_s, fc_s = scratch
            gproj_ref[...] = proj_s[...].astype(BF16)
            for i in range(n_fsdp):
                store_fc(i, fc_s[i * share : (i + 1) * share, :].astype(BF16))
            return
        hiddent_s, di_s, dmlp_s, lowt_s = scratch
        tile = min(256, wide)

        def proj_tile(i, _):
            at = pl.multiple_of(i * tile, tile)
            g = jnp.dot(hiddent_s[pl.ds(at, tile), :], dmlp_s[...], preferred_element_type=F32)
            gproj_ref[pl.ds(at, tile), :] = g.astype(BF16)
            return 0

        lax.fori_loop(0, wide // tile, proj_tile, 0)

        def fc_tile(i, _):
            at = pl.multiple_of(i * share, share)
            g = jnp.dot(lowt_s[pl.ds(at, share), :], di_s[...], preferred_element_type=F32)
            store_fc(i, g.astype(BF16))
            return 0

        lax.fori_loop(0, n_fsdp, fc_tile, 0)


def feed_grads(near, far, low_pieces, n_seq):
    rows, width = low_pieces[0].shape
    n_fsdp = len(low_pieces)
    wide = near[0].shape[1]
    total = n_fsdp * rows
    count = near[0].shape[0] // rows
    thin = width // n_fsdp // n_seq
    if total > 2048:
        scratch = [pltpu.VMEM((wide, width), F32), pltpu.VMEM((width, wide), F32)]
    else:
        scratch = [pltpu.VMEM((wide, total), BF16), pltpu.VMEM((total, wide), BF16)]
        scratch += [pltpu.VMEM((total, width), BF16), pltpu.VMEM((width, total), BF16)]

    def whole(*shape):
        return pl.BlockSpec(shape, lambda g: (0,) * len(shape), pipeline_mode=pl.Buffered(1))

    def last(*shape):
        return pl.BlockSpec(shape, lambda g: (0,) * len(shape))

    def of_near(columns):
        return pl.BlockSpec((rows, columns), lambda g: (jnp.minimum(g, count - 1), 0))

    def of_far(columns):
        return pl.BlockSpec((rows, columns), lambda g: (jnp.maximum(g - count, 0), 0))

    pairs = [(of_near(wide), of_far(wide))] * 2 + [(of_near(width), of_far(width))]
    return pl.pallas_call(
        functools.partial(feed_grads_kernel, count, n_fsdp),
        grid=(n_fsdp,),
        in_specs=[spec for pair in pairs for spec in pair] + [whole(rows, width)] * n_fsdp,
        out_specs=[last(wide, width), last(n_seq, n_fsdp, thin, wide), last(1, wide)],
        out_shape=(
            jax.ShapeDtypeStruct((wide, width), BF16),
            jax.ShapeDtypeStruct((n_seq, n_fsdp, thin, wide), BF16),
            jax.ShapeDtypeStruct((1, wide), F32),
        ),
        scratch_shapes=scratch,
        cost_estimate=takes(15),
        compiler_params=pltpu.CompilerParams(vmem_limit_bytes=48 << 20),
        name="feed_grads",
    )(near[0], far[0], near[1], far[1], near[2], far[2], *low_pieces)


def feed_out_kernel(packs, hidden_ref, wproj_ref, *mlp_refs):
    step = pl.program_id(0)
    mlp = jnp.dot(hidden_ref[...], wproj_ref[...], preferred_element_type=F32)
    for (lo, hi), out_ref in zip(tier_bounds(packs), mlp_refs):

        @pl.when((step >= lo) & (step < hi))
        def _():
            out_ref[...] = mlp.astype(out_ref.dtype)


def feed_out(hidden, wproj, rows, own):
    wide, width = wproj.shape
    packs = hidden.shape[0] // rows
    tiers = tier_bounds(packs)

    def tier(lo, hi):
        return pl.BlockSpec((rows, width), lambda g: (jnp.clip(g - lo, 0, hi - lo - 1), 0))

    return pl.pallas_call(
        functools.partial(feed_out_kernel, packs),
        grid=(packs,),
        in_specs=[
            pl.BlockSpec((rows, wide), lambda g: (g, 0)),
            pl.BlockSpec((wide, width), lambda g: (0, 0), pipeline_mode=pl.Buffered(1)),
        ],
        out_specs=[tier(lo, hi) for lo, hi in tiers],
        out_shape=tuple(
            jax.ShapeDtypeStruct(((hi - lo) * rows, width), F32 if lo == 0 and own else BF16)
            for lo, hi in tiers
        ),
        cost_estimate=takes(0.3),
        compiler_params=pltpu.CompilerParams(vmem_limit_bytes=20 << 20),
        name="feed_out",
    )(hidden, wproj)


def middle_back_kernel(
    n_fsdp,
    terms,
    rel_ref,
    count_ref,
    merged_ref,
    middle_ref,
    dy_ref,
    gain_ref,
    wout_ref,
    *rest,
):
    tiers = tier_bounds(n_fsdp)
    term_refs, rest = rest[:terms], rest[terms:]
    gout_refs, rest = rest[: len(tiers)], rest[len(tiers) :]
    d_middle_ref, d_merged_ref, vec_ref, flip_s, order_s = rest
    n_seq, rows, hd = merged_ref.shape
    share = flip_s.shape[0] // n_fsdp
    valid = lax.broadcasted_iota(jnp.int32, (rows, 1), 0) < count_ref[0]
    n, scale = norm_parts(middle_ref[...])
    d_two = functools.reduce(jnp.add, [ref[...].astype(F32) for ref in term_refs])
    d_result = jnp.where(valid, dy_ref[...].astype(F32), 0.0)
    e = d_two * gain_ref[...]
    d_middle = d_result + scale * (
        e - jnp.mean(e, axis=-1, keepdims=True) - n * jnp.mean(e * n, axis=-1, keepdims=True)
    )
    d_middle_ref[...] = d_middle
    d_attn = d_middle.astype(BF16)
    d_merged = lax.dot_general(d_attn, wout_ref[...], NT, preferred_element_type=F32).astype(BF16)
    for k in range(n_seq):
        d_merged_ref[k] = d_merged[:, k * hd : (k + 1) * hd]
    vec_ref[0:1, :] = jnp.sum(d_attn.astype(F32), axis=0, keepdims=True)
    vec_ref[1:2, :] = jnp.sum(d_two * n, axis=0, keepdims=True)
    vec_ref[2:3, :] = jnp.sum(d_two, axis=0, keepdims=True)
    vec_ref[3:4, :] = jnp.sum(d_result, axis=0, keepdims=True)
    merged = jnp.concatenate([merged_ref[k] for k in range(n_seq)], axis=1)
    flip_s[...] = merged.T
    for k in range(n_fsdp):
        at = pl.multiple_of(rel_ref[k] * share, share)
        order_s[k * share : (k + 1) * share, :] = flip_s[pl.ds(at, share), :]
    gout = jnp.dot(order_s[...], d_attn, preferred_element_type=F32).astype(BF16)
    for (lo, hi), out_ref in zip(tiers, gout_refs):
        out_ref[...] = gout[lo * share : hi * share]


def middle_back(rel, count, merged, middle, dy, gain, wout, terms):
    rows, width = middle.shape
    n_fsdp = rel.shape[0]
    share = width // n_fsdp
    tiers = tier_bounds(n_fsdp)
    return pl.pallas_call(
        functools.partial(middle_back_kernel, n_fsdp, len(terms)),
        in_specs=[SM] * 2 + [VM] * (5 + len(terms)),
        out_specs=(VM,) * (len(tiers) + 3),
        out_shape=tuple(
            [jax.ShapeDtypeStruct(((hi - lo) * share, width), BF16) for lo, hi in tiers]
            + [
                jax.ShapeDtypeStruct((rows, width), F32),
                jax.ShapeDtypeStruct(merged.shape, BF16),
                jax.ShapeDtypeStruct((4, width), F32),
            ]
        ),
        scratch_shapes=[pltpu.VMEM((width, rows), BF16)] * 2,
        cost_estimate=takes(7),
        compiler_params=pltpu.CompilerParams(vmem_limit_bytes=36 << 20),
        name="middle_back",
    )(rel, count, merged, middle, dy, gain, wout, *terms)


def finish_kernel(count_ref, middle_ref, bproj_ref, *rest):
    term_refs, output_ref, stat_ref = rest[:-2], rest[-2], rest[-1]
    rows = middle_ref.shape[0]
    valid = lax.broadcasted_iota(jnp.int32, (rows, 1), 0) < count_ref[0]
    branch = functools.reduce(jnp.add, [ref[...].astype(F32) for ref in term_refs])
    branch = branch + bproj_ref[...]
    result = middle_ref[...] + branch
    output_ref[...] = jnp.where(valid, result, 0.0).astype(BF16)
    stat_ref[0:1, :] = jnp.sum(jnp.where(valid, result * result, 0.0), axis=0, keepdims=True)
    stat_ref[1:2, :] = jnp.sum(jnp.where(valid, branch * branch, 0.0), axis=0, keepdims=True)


def finish(count, middle, bproj, terms):
    rows, width = middle.shape
    return pl.pallas_call(
        finish_kernel,
        in_specs=[SM] + [VM] * (2 + len(terms)),
        out_specs=(VM,) * 2,
        out_shape=(
            jax.ShapeDtypeStruct((rows, width), BF16),
            jax.ShapeDtypeStruct((2, width), F32),
        ),
        cost_estimate=takes(0.1),
        compiler_params=pltpu.CompilerParams(vmem_limit_bytes=32 << 20),
        name="finish",
    )(count, middle, bproj, *terms)


def qkv_grad_kernel(x_ref, d_ref, w_ref, gain_ref, shift_ref, g_ref, vec_ref, sum_ref, acc):
    step = pl.program_id(0)
    n, _ = norm_parts(x_ref[...].astype(F32))
    low = (n * gain_ref[...] + shift_ref[...]).astype(BF16)
    d = d_ref[...]
    part = lax.dot_general(d, w_ref[...], NT, preferred_element_type=F32)
    gain_part = jnp.sum(part * n, axis=0, keepdims=True)
    shift_part = jnp.sum(part, axis=0, keepdims=True)
    sum_part = jnp.sum(d.astype(F32), axis=0, keepdims=True)
    g = jnp.dot(low.T, d, preferred_element_type=F32)

    @pl.when(step == 0)
    def _():
        acc[...] = g
        vec_ref[0:1, :] = gain_part
        vec_ref[1:2, :] = shift_part
        sum_ref[...] = sum_part

    @pl.when(step > 0)
    def _():
        acc[...] += g
        vec_ref[0:1, :] += gain_part
        vec_ref[1:2, :] += shift_part
        sum_ref[...] += sum_part

    @pl.when(step == pl.num_programs(0) - 1)
    def _():
        g_ref[...] = acc[...].astype(BF16)


def qkv_grads(x_all, d_own, w_own, gain, shift, block):
    total, width = x_all.shape
    wide = w_own.shape[1]

    def whole(*shape):
        return pl.BlockSpec(shape, lambda g: (0,) * len(shape))

    return pl.pallas_call(
        qkv_grad_kernel,
        grid=(total // block,),
        in_specs=[
            pl.BlockSpec((block, width), lambda g: (g, 0)),
            pl.BlockSpec((block, wide), lambda g: (g, 0)),
            whole(width, wide),
            whole(1, width),
            whole(1, width),
        ],
        out_specs=[whole(width, wide), whole(2, width), whole(1, wide)],
        out_shape=(
            jax.ShapeDtypeStruct((width, wide), BF16),
            jax.ShapeDtypeStruct((2, width), F32),
            jax.ShapeDtypeStruct((1, wide), F32),
        ),
        scratch_shapes=[pltpu.VMEM((width, wide), F32)],
        cost_estimate=takes(13),
        compiler_params=pltpu.CompilerParams(vmem_limit_bytes=40 << 20),
        name="qkv_grads",
    )(x_all, d_own, w_own, gain, shift)


def input_grad_kernel(d_ref, x_ref, gain_ref, d_middle_ref, w_ref, out_ref, d_s, one_s):
    step = pl.program_id(0)
    steps, _, share = one_s.shape

    @pl.when(step == 0)
    def _():
        d_s[...] = jnp.concatenate([d_ref[k] for k in range(d_ref.shape[0])], axis=1)

    one_s[step] = lax.dot_general(d_s[...], w_ref[...], NT, preferred_element_type=F32)

    @pl.when(step == steps - 1)
    def _():
        n, scale = norm_parts(x_ref[...].astype(F32))
        d_one = jnp.concatenate([one_s[k] for k in range(steps)], axis=1)
        e = d_one * gain_ref[...]
        out_ref[...] = d_middle_ref[...] + scale * (
            e - jnp.mean(e, axis=-1, keepdims=True) - n * jnp.mean(e * n, axis=-1, keepdims=True)
        )


def input_gradient(d_packed, w_all, x, gain, d_middle):
    rows, width = x.shape
    n_seq, _, each = d_packed.shape
    wide = w_all.shape[1]
    steps = 4

    def whole(*shape):
        return pl.BlockSpec(shape, lambda g: (0,) * len(shape), pipeline_mode=pl.Buffered(1))

    return pl.pallas_call(
        input_grad_kernel,
        grid=(steps,),
        in_specs=[
            whole(n_seq, rows, each),
            whole(rows, width),
            whole(1, width),
            whole(rows, width),
            pl.BlockSpec((width // steps, wide), lambda g: (g, 0)),
        ],
        out_specs=whole(rows, width),
        out_shape=jax.ShapeDtypeStruct((rows, width), F32),
        scratch_shapes=[
            pltpu.VMEM((rows, wide), BF16),
            pltpu.VMEM((steps, rows, width // steps), F32),
        ],
        cost_estimate=takes(8),
        compiler_params=pltpu.CompilerParams(vmem_limit_bytes=32 << 20),
        name="input_gradient",
    )(d_packed, x, gain, d_middle, w_all)


def place_kernel(layout, groups, order_ref, rel_ref, *refs):
    outs = refs[len(refs) - len(layout) :]
    step = pl.program_id(0)
    for k, group in enumerate(groups):

        @pl.when(step == k)
        def _():
            thin = sum(refs[i].shape[0] for i in group)
            at = 0

            def columns(each):
                parts = [refs[i][:, at : at + each].astype(F32) for i in group]
                return parts[0] if len(parts) == 1 else jnp.concatenate(parts, axis=0)

            for (kind, wide, blocks), out in zip(layout, outs):
                each = wide // blocks
                for a in range(blocks):
                    part = columns(each)
                    at += each
                    if kind == "rel":
                        lanes = pl.ds(pl.multiple_of(rel_ref[a] * each, each), each)
                        out[0, :, lanes] = part
                    elif len(out.shape) == 3:
                        out[0, a * thin : (a + 1) * thin, :] = part
                    else:
                        out[a * thin : (a + 1) * thin, :] = part


def place(order, rel, pieces, layout, n, held=None):
    halves = held is not None
    groups = [range(len(pieces))] if halves else [[k] for k in range(len(pieces))]
    thin = sum(pieces[k].shape[0] for k in groups[0])
    shapes = []
    specs = []
    for kind, wide, blocks in layout:
        each = wide // blocks
        if kind == "cols" and each % 128 == 0:
            shapes.append((blocks * thin, n * each))
            specs.append(pl.BlockSpec((blocks * thin, each), lambda g, order, _: (0, order[g])))
            continue
        size = (thin, wide) if kind == "rel" else (blocks * thin, each)
        shapes.append((n,) + size)
        specs.append(pl.BlockSpec((1,) + size, lambda g, order, _: (order[g], 0, 0)))
    given = () if held is None else tuple(held)
    first = 2 + len(pieces)
    return pl.pallas_call(
        functools.partial(place_kernel, layout, groups),
        grid_spec=pltpu.PrefetchScalarGridSpec(
            num_scalar_prefetch=2,
            grid=(len(groups),),
            in_specs=[
                pl.BlockSpec(p.shape, lambda g, *_: (0, 0), pipeline_mode=pl.Buffered(1))
                for p in pieces
            ]
            + [pl.BlockSpec(memory_space=pl.ANY)] * len(given),
            out_specs=specs,
        ),
        out_shape=tuple(jax.ShapeDtypeStruct(shape, F32) for shape in shapes),
        input_output_aliases={first + k: k for k in range(len(given))},
        cost_estimate=takes(len(pieces)),
        compiler_params=pltpu.CompilerParams(vmem_limit_bytes=48 << 20),
        name="place",
    )(order, rel, *pieces, *given)


def flat_matrices(placed, layout):
    results = []
    for (kind, _, _), out in zip(layout, placed):
        if len(out.shape) == 3 and kind == "cols":
            out = out.transpose(1, 0, 2).reshape(out.shape[1], -1)
        elif len(out.shape) == 3:
            out = out.reshape(-1, out.shape[2])
        results.append(out)
    return results


class Ring:
    def __init__(self, axis):
        self.axis = axis
        self.n = n = lax.axis_size(axis)
        me = lax.axis_index(axis)
        self.pos = jnp.where(me % 2 == 0, me // 2, n - 1 - me // 2)
        order = list(range(0, n, 2)) + list(range(1, n, 2))[::-1]
        self.up = [(order[i], order[(i + 1) % n]) for i in range(n)]
        self.down = [(b, a) for a, b in self.up]
        self.walk = [0]
        for step in range(1, n // 2):
            self.walk += [-step, step]
        self.walk.append(n // 2)
        p = (self.pos + jnp.asarray(self.walk, jnp.int32) + n) % n
        self.order = jnp.where(p < n // 2, 2 * p, 2 * (n - 1 - p) + 1)

    def shard(self, distance):
        n = self.n
        p = (self.pos + distance + n) % n
        return jnp.where(p < n // 2, 2 * p, 2 * (n - 1 - p) + 1)

    def send_up(self, value):
        return lax.ppermute(value, self.axis, self.up)

    def send_down(self, value):
        return lax.ppermute(value, self.axis, self.down)

    def gather(self, value):
        half = value.shape[0] // 2
        above = below = value
        out = [value]
        for _ in range(1, self.n // 2):
            below, above = yield self.send_up(below), self.send_down(above)
            out += [below, above]
        return out + list((yield self.send_up(below[:half]), self.send_down(above[half:])))

    def reduce(self, *values):
        rows = values[0].shape[0] // self.n
        half = rows // 2
        mid = self.n // 2

        def term(distance, first=0, count=rows):
            at = self.shard(distance) * rows + first
            parts = [lax.dynamic_slice_in_dim(v, at, count, 0).astype(F32) for v in values]
            return parts[0] if len(parts) == 1 else jnp.concatenate(parts, axis=1)

        up = self.send_up(term(mid, 0, half).astype(BF16))
        down = self.send_down(term(mid, half, rows - half).astype(BF16))
        for step in range(mid - 1, 0, -1):
            up, down = yield up, down
            mine = term(step)
            other = term(-step)
            if step == mid - 1:
                mine = jnp.concatenate([mine[:half] + up.astype(F32), mine[half:]], axis=0)
                other = jnp.concatenate([other[:half], other[half:] + down.astype(F32)], axis=0)
            else:
                mine = mine + up.astype(F32)
                other = other + down.astype(F32)
            up = self.send_up(mine.astype(BF16))
            down = self.send_down(other.astype(BF16))
        up, down = yield up, down
        return (term(0) + up.astype(F32) + down.astype(F32)).astype(BF16)


class Walk:
    def __init__(self, steps):
        self.steps = steps
        self.result = None
        self.moving = next(steps)

    def go(self, arrived):
        try:
            self.moving = self.steps.send(arrived)
        except StopIteration as end:
            self.moving = None
            self.result = end.value


def milestone(*values):
    return lax.optimization_barrier(values)


def bits(n):
    return [1 << b for b in range(n.bit_length() - 1)]


def swap(value, axis, bit):
    n = lax.axis_size(axis)
    return lax.ppermute(value, axis, [(i, i ^ bit) for i in range(n)])


def reach(n):
    masks = [0]
    for bit in reversed(bits(n)):
        masks = masks + [m | bit for m in masks]
    return masks


def cube_gather(value, axis, n=None):
    held = [value]
    for bit in reversed(bits(n or lax.axis_size(axis))):
        held = held + [swap(block, axis, bit) for block in held]
    return held


class Scatter:
    def __init__(self, tiers, axis):
        self.axis = axis
        tiers = list(tiers)
        self.left = self.top = len(tiers) - 1
        self.size = tiers[0].shape[0]
        self.terms = [[t] for t in tiers]
        self.moving = None

    def send(self):
        parts = self.terms[self.left]
        away = parts[0] if len(parts) == 1 else add_up(parts).astype(BF16)
        self.moving = swap(away, self.axis, 1 << (self.top - self.left))

    def take(self):
        for j, (lo, hi) in enumerate(tier_bounds(1 << (self.left - 1))):
            self.terms[j].append(self.moving[lo * self.size : hi * self.size])
        self.left -= 1


def add_up(terms):
    return functools.reduce(jnp.add, [t.astype(F32) for t in terms])


def cube_exchange(value, axis, dim):
    me = lax.axis_index(axis)
    n = lax.axis_size(axis)
    size = value.shape[dim] // n
    out = []
    for mask in reach(n):
        block = lax.dynamic_slice_in_dim(value, (me ^ mask) * size, size, dim)
        if mask:
            block = lax.ppermute(block, axis, [(i, i ^ mask) for i in range(n)])
        out.append(block)
    return out


def shards(
    tokens,
    cotangent,
    lengths,
    deal,
    ln1_gain,
    ln1_shift,
    w_qkv,
    bias_qv,
    w_out,
    bias_out,
    ln2_gain,
    ln2_shift,
    w_fc,
    bias_fc,
    w_proj,
    bias_proj,
):
    x = tokens[0]
    dy = cotangent[0]
    rows, width = x.shape
    ring = Ring("seq")
    n_seq = ring.n
    n_fsdp = lax.axis_size("fsdp")
    me_seq = lax.axis_index("seq")
    me_fsdp = lax.axis_index("fsdp")
    total_rows = rows * n_seq
    heads = H // n_seq
    hd = heads * HEAD
    wide = w_fc.shape[1]
    share = w_qkv.shape[0]
    groups = jnp.arange(n_fsdp, dtype=jnp.int32)
    picked = (deal[:, None] == groups[None, :]).astype(jnp.int32)
    home_rows = jnp.sum(picked[:, :, None] * lengths[None], axis=1)
    row = jnp.sum(jnp.where((groups == me_fsdp)[:, None], home_rows, 0), axis=0)
    last = lengths.shape[1] - 1
    masks = reach(n_fsdp)
    rel = me_fsdp ^ jnp.asarray(masks, jnp.int32)

    own_cols = lax.dynamic_slice_in_dim(w_qkv, me_seq * 3 * hd, 3 * hd, 1)
    small = (ln1_gain, ln1_shift, bias_qv, bias_out, ln2_gain, ln2_shift, bias_proj)
    small = jnp.concatenate(small)
    extra = -(-small.shape[0] // (3 * hd * 16)) * 16
    tail = jnp.pad(small, (0, extra * 3 * hd - small.shape[0])).reshape(extra, 3 * hd)

    walk = Walk(ring.gather(x))
    wfc = lax.all_gather(w_fc, "fsdp", axis=0, tiled=True)
    dy_all = lax.all_gather(dy, "fsdp", axis=0, tiled=True)
    moved, mine = milestone(walk.moving, (own_cols, tail))
    walk.go(moved)
    packs = [jnp.concatenate(mine, axis=0)]
    held = None
    for bit in reversed(bits(n_fsdp)):
        packs = packs + [swap(p, "fsdp", bit) for p in packs]

    def projected(blocks):
        nonlocal held
        for k in blocks:
            if k < n_seq - 1:
                at = ring.shard(ring.walk[k])
            else:
                at = ring.shard(n_seq // 2) * 2 + (k - n_seq + 1)
            held = project(
                at, pieces[k], gain_one, shift_one, w_roles, b_own, total_rows, held
            )

    moved_first = moved
    moved, packs, w_out = milestone(walk.moving, packs, w_out)
    walk.go(moved)
    top = n_fsdp // 2
    wout_far = swap(w_out, "fsdp", top)

    w_own = jnp.zeros((width, 3 * hd), BF16)
    vectors = jnp.zeros((n_fsdp, tail.size), BF16)
    for k, p in enumerate(packs):
        index = me_fsdp ^ masks[k]
        w_own = lax.dynamic_update_slice_in_dim(w_own, p[:share], index * share, 0)
        vectors = lax.dynamic_update_slice_in_dim(vectors, p[share:].reshape(1, -1), index, 0)
    w_roles = w_own.reshape(width, heads, 3, HEAD).transpose(0, 2, 1, 3).reshape(width, 3 * hd)
    cut = []
    at = 0
    for count in (share, share, 2 * share, share, share, share, share):
        cut.append(vectors[:, at : at + count].reshape(1, -1).astype(F32))
        at += count
    gain_one, shift_one, bqv, bout, gain_two, shift_two, bproj = cut
    b_own = lax.dynamic_index_in_dim(bqv.reshape(n_seq, heads, 2, HEAD), me_seq, 0, keepdims=False)
    b_own = jnp.concatenate(
        [b_own[:, 0].reshape(1, hd), jnp.zeros((1, hd), F32), b_own[:, 1].reshape(1, hd)], axis=1
    )

    pieces = [x] + list(moved_first) + list(moved)
    done = 0
    while walk.result is None:
        ready = len(pieces)
        projected(range(done, ready))
        done = ready
        moved, held = milestone(walk.moving, held)
        walk.go(moved)
        pieces += list(moved)
    projected(range(done, len(pieces)))
    held, wout_far = milestone(held, wout_far)
    x_all, qkv = held

    attended, lse = attention_forward(row, qkv, rows)
    wout = jnp.zeros((width, width), BF16)
    wout_pieces = cube_gather(w_out, "fsdp", top) + cube_gather(wout_far, "fsdp", top)
    for k, mask in enumerate(reach(top) + [m | top for m in reach(top)]):
        wout = lax.dynamic_update_slice_in_dim(wout, wout_pieces[k], (me_fsdp ^ mask) * share, 0)
    merged = lax.all_to_all(
        attended.reshape(n_seq, rows, hd), "seq", split_axis=0, concat_axis=0, tiled=True
    )

    merged, wout = milestone(merged, wout)

    ends = jnp.sum(home_rows[:, :last], axis=1)

    def valid_counts(index):
        of = jnp.sum(jnp.where(index[:, None] == groups[None, :], ends[None, :], 0), axis=1)
        return jnp.clip(of - me_seq * rows, 0, rows)

    near = me_fsdp ^ jnp.asarray(reach(top), jnp.int32)
    far = near ^ top
    near_far = jnp.concatenate([near, far])
    counts = valid_counts(near)
    low, middle, square_attn = attend_out(
        counts, merged, x, wout, bout, gain_two, shift_two
    )

    bfc = bias_fc.astype(F32)[None]
    low_far = swap(low, "fsdp", top)
    low_near = cube_gather(low, "fsdp", top)
    halves = len(tier_bounds(top))
    results = feed(rel, near, counts, low_near, dy_all, wfc, w_proj, bfc, True)
    two_near, feed_near = Scatter(results[:halves], "fsdp"), results[halves:]
    low_far, feed_near = milestone(low_far, feed_near)
    while two_near.left:
        two_near.send()
        two_near.take()
    low_far = cube_gather(low_far, "fsdp", top)
    results = feed(rel, far, valid_counts(far), low_far, dy_all, wfc, w_proj, bfc, False)
    two_far, feed_far = Scatter(results[:halves], "fsdp"), results[halves:]
    while two_far.left:
        two_far.send()
        two_far.moving, feed_far, two_near.terms = milestone(
            two_far.moving, feed_far, two_near.terms
        )
        two_far.take()

    far_two = swap(add_up(two_far.terms[0]).astype(BF16), "fsdp", top)
    gproj, gfc, gbfc = feed_grads(feed_near, feed_far, low_near + low_far, n_seq)
    far_two, gproj, gfc = milestone(far_two, gproj, gfc)

    thin = share // n_seq
    blocks = wide // width
    gfc = gfc.reshape(n_seq * n_fsdp * thin, wide // n_fsdp)
    together = gfc.shape[0] == gproj.shape[0]
    walk = Walk(ring.reduce(gproj, gfc) if together else ring.reduce(gfc))
    results = middle_back(
        rel, counts, merged, middle, dy, gain_two, wout, two_near.terms[0] + [far_two]
    )
    tiers = len(tier_bounds(n_fsdp))
    gout, (d_middle, d_merged, sums_two) = results[:tiers], results[tiers:]
    moved, d_merged, gout = milestone(walk.moving, d_merged, gout)

    d_heads = lax.all_to_all(d_merged, "seq", split_axis=0, concat_axis=0, tiled=True)
    walk.go(moved)
    gout = Scatter(gout, "fsdp")
    hidden = (feed_near[0], feed_far[0])
    while gout.left > 1:
        gout.send()
        gout.moving, hidden = milestone(gout.moving, hidden)
        gout.take()
    gout.send()
    mlp_near = Scatter(feed_out(hidden[0], w_proj, rows, True), "fsdp")
    mlp_far = Scatter(feed_out(hidden[1], w_proj, rows, False), "fsdp")
    while mlp_near.left:
        mlp_near.send()
        mlp_far.send()
        mlp_near.take()
        mlp_far.take()
    mlp_far = add_up(mlp_far.terms[0]).astype(BF16)
    gout.moving, mlp_far, mlp_near.terms = milestone(gout.moving, mlp_far, mlp_near.terms)
    gout.take()
    out_walk = Walk(ring.reduce(add_up(gout.terms[0])))
    moved, d_heads, out_moved = milestone(walk.moving, d_heads, out_walk.moving)

    walk.go(moved)
    out_walk.go(out_moved)
    mlp_far = swap(mlp_far, "fsdp", top)
    d_own = attention_backward(row, qkv, attended, lse, d_heads.reshape(total_rows, hd), rows)
    moved, out_moved, d_own, mlp_far = milestone(walk.moving, out_walk.moving, d_own, mlp_far)
    d_packed = lax.all_to_all(
        d_own.reshape(n_seq, rows, 3 * hd), "seq", split_axis=0, concat_axis=0, tiled=True
    )
    walk.go(moved)
    out_walk.go(out_moved)
    w_qkv = milestone(w_qkv, d_own)[0]
    w_all = lax.all_gather(w_qkv, "fsdp", axis=0, tiled=True)
    grad_qkv, sums_one, d_sums = qkv_grads(x_all, d_own, w_own, gain_one, shift_one, rows)
    while walk.result is None:
        moved, out_moved, grad_qkv, sums_one, d_sums, mlp_far = milestone(
            walk.moving, out_walk.moving, grad_qkv, sums_one, d_sums, mlp_far
        )
        walk.go(moved)
        out_walk.go(out_moved)
    mine = walk.result
    if together:
        mine_proj, mine_fc = mine[:, :width], mine[:, width:]
    else:
        mine_fc = mine
        walk = Walk(ring.reduce(gproj))
        while walk.result is None:
            walk.go(walk.moving)
        mine_proj = walk.result
    mine_proj = mine_proj.reshape(blocks, thin, width).transpose(1, 0, 2).reshape(thin, wide)
    mine_fc = cube_exchange(mine_fc, "fsdp", 0)
    parts = [
        lax.dynamic_slice_in_dim(grad_qkv, (me_fsdp ^ mask) * share, share, 0) for mask in masks
    ]
    parts = [jnp.concatenate(parts[lo:hi], axis=0) for lo, hi in tier_bounds(n_fsdp)]
    parts = Scatter(parts, "fsdp")
    while parts.left > 1:
        parts.send()
        parts.take()
    while out_walk.result is None:
        parts.terms, mine_fc, out_moved, mlp_far = milestone(
            parts.terms, mine_fc, out_walk.moving, mlp_far
        )
        out_walk.go(out_moved)
    parts.send()
    parts.take()
    share_qkv = add_up(parts.terms[0]).astype(BF16)
    beside_it = share_qkv.reshape(n_seq, thin, 3 * hd).transpose(1, 0, 2).reshape(thin, -1)
    mine = jnp.concatenate([mine_proj] + mine_fc + [out_walk.result, beside_it], axis=1)

    output, square_ends = finish(counts, middle, bproj, mlp_near.terms[0] + [mlp_far])
    mine, d_packed, square_ends, sums_one, d_sums = milestone(
        mine, d_packed, square_ends, sums_one, d_sums
    )
    walk = Walk(ring.gather(mine))
    squares = jnp.concatenate([square_ends[:1], square_attn, square_ends[1:]], axis=0)
    squares = jnp.concatenate([jnp.sum(squares, axis=1), counts[:1].astype(F32)])[None]
    squares = jnp.concatenate([squares, jnp.zeros((n_fsdp - 1, 4), F32)], axis=0)
    grad_bfc = lax.dynamic_update_slice_in_dim(
        jnp.zeros((n_fsdp, wide // n_fsdp), F32), gbfc, me_fsdp, 0
    )
    d_sums = d_sums.reshape(heads, 3, HEAD)
    d_sums = jnp.stack([d_sums[:, 0], d_sums[:, 2]], axis=1).reshape(1, 2 * hd)
    grad_bqv = lax.dynamic_update_slice_in_dim(
        jnp.zeros((n_seq, 2 * hd), F32), d_sums, me_seq, 0
    )
    vectors = [sums_one[0], sums_one[1], grad_bqv, *[sums_two[k] for k in range(4)], grad_bfc]
    vectors = [v.reshape(n_fsdp, -1) for v in vectors]
    sums = jnp.concatenate(vectors + [squares], axis=1)
    for bit in bits(n_fsdp):
        sums = sums + swap(sums, "fsdp", bit)
    hops = bits(n_seq)
    arrived = [mine]

    layout = (
        ("rows", wide, blocks),
        ("rel", wide, n_fsdp),
        ("rows", width, 1),
        ("cols", 3 * width, n_seq),
    )
    steps = n_seq // 2
    input_grad = placed = own = squares = None
    for step in range(steps):
        ahead = steps - step
        count = len(hops)
        for bit in hops[:count]:
            sums = sums + swap(sums, "seq", bit)
        hops = hops[count:]
        if ahead == min(3, steps):
            input_grad = input_gradient(d_packed, w_all, x, gain_one, d_middle)
        if ahead == min(2, steps):
            own = lax.dynamic_slice_in_dim(sums, me_fsdp, 1, 0)[0]
            squared = sums[0, -4:]
            squares = jnp.sqrt(squared[:3] / (squared[3] * width))
        if ahead == 1:
            placed = place(ring.order, rel, arrived, layout, n_seq)
        moved, sums, input_grad, placed, own, squares, output = milestone(
            walk.moving, sums, input_grad, placed, own, squares, output
        )
        if ahead > 1:
            arrived += list(moved)
        walk.go(moved)
    stats = squares
    farthest = ring.shard(n_seq // 2).reshape(1)
    placed = place(farthest, rel, walk.result[-2:], layout, n_seq, placed)
    grad_proj, grad_fc, grad_out, grad_wqkv = flat_matrices(placed, layout)

    shares = []
    at = 0
    for vector in vectors:
        shares.append(own[at : at + vector.shape[1]])
        at += vector.shape[1]
    g1, s1, bqv, bout, g2, s2, bproj, bfc = shares
    return (
        output[None],
        input_grad[None],
        g1,
        s1,
        grad_wqkv,
        bqv,
        grad_out,
        bout,
        g2,
        s2,
        grad_fc,
        bfc,
        grad_proj,
        bproj,
        stats,
    )


def solution(mesh):
    rows_split = P("fsdp", "seq", None)
    matrix = P("fsdp", None)
    vector = P("fsdp")
    params = (
        vector,
        vector,
        matrix,
        vector,
        matrix,
        vector,
        vector,
        vector,
        matrix,
        vector,
        matrix,
        vector,
    )
    return jax.shard_map(
        shards,
        mesh=mesh,
        in_specs=(rows_split, rows_split, P(), P()) + params,
        out_specs=(rows_split, rows_split) + params + (P(),),
        check_vma=False,
    )
```
